32 devices in a mesh: seq: 8 (over y, x, core), dp: 4 (over z).
Axes of the slice: x: 2, y: 2, z: 4, core: 2. Of those that a mesh axis runs over, the one named last changes fastest.
Arguments:
- tokens: bfloat16 [4, 2, 1024, 2048], P('dp', None, 'seq'), may hold values from -6 to 6
- lengths: int32 [4, 2], P('dp'), may hold values from 1024 to 1024, as said below
- attn_gain: bfloat16 [2048], P(('seq', 'dp')), may hold values from 0.25 to 1.75
- w_qdown: bfloat16 [2048, 1024], P(('seq', 'dp')), may hold values from -0.125 to 0.125
- q_gain: bfloat16 [1024], P(('seq', 'dp')), may hold values from 0.25 to 1.75
- w_qup: bfloat16 [1024, 4096], P(('seq', 'dp')), may hold values from -0.1875 to 0.1875
- w_key: bfloat16 [2048, 256], P(('seq', 'dp')), may hold values from -0.125 to 0.125
- w_value: bfloat16 [2048, 256], P(('seq', 'dp')), may hold values from -0.125 to 0.125
- w_out: bfloat16 [4096, 2048], P(('seq', 'dp')), may hold values from -1.5 to 1.5
- ffn_gain: bfloat16 [2048], P(('seq', 'dp')), may hold values from 0.25 to 1.75
- w_gate: bfloat16 [2048, 5632], P(('seq', 'dp')), may hold values from -0.125 to 0.125
- w_up: bfloat16 [2048, 5632], P(('seq', 'dp')), may hold values from -0.125 to 0.125
- w_down: bfloat16 [5632, 2048], P(('seq', 'dp')), may hold values from -0.078125 to 0.078125
- cotangent: bfloat16 [4, 2, 1024, 2048], P('dp', None, 'seq'), may hold values from -6 to 6
Outputs:
- out_tokens: bfloat16 [4, 2, 1024, 2048], P('dp', None, 'seq')
- grad_tokens: float32 [4, 2, 1024, 2048], P('dp', None, 'seq')
- grad_attn_gain: float32 [2048], P(('seq', 'dp'))
- grad_w_qdown: float32 [2048, 1024], P(('seq', 'dp'))
- grad_q_gain: float32 [1024], P(('seq', 'dp'))
- grad_w_qup: float32 [1024, 4096], P(('seq', 'dp'))
- grad_w_key: float32 [2048, 256], P(('seq', 'dp'))
- grad_w_value: float32 [2048, 256], P(('seq', 'dp'))
- grad_w_out: float32 [4096, 2048], P(('seq', 'dp'))
- grad_ffn_gain: float32 [2048], P(('seq', 'dp'))
- grad_w_gate: float32 [2048, 5632], P(('seq', 'dp'))
- grad_w_up: float32 [2048, 5632], P(('seq', 'dp'))
- grad_w_down: float32 [5632, 2048], P(('seq', 'dp'))
The draws below stay inside these ranges and needn't reach their ends.
Inputs may be any that keep to these rules, and one draw needn't show every extreme that they name: `lengths`: in every group, one sequence, chosen by the draw, has the full length 1024; positions at or past a sequence's length are padding.
All inputs are finite; a program needn't handle non-finite values.
Results may differ from the reference program's by a relative error of at most 0.015.
Values may be sent and summed in bfloat16 or wider, within the bound.
A program may use at most 512 MiB of HBM per device.

```python
import math
from functools import partial
import jax
import jax.numpy as jnp
from jax import lax

D = 2048
QL = 1024
HEADS = 16
HD = 256
FF = 5632
SEQS = 2
MINLEN = 1024
CAP = 128
GROUPS = 4
MAXLEN = 1024
TOKENS = 8192
N_SEQ = 8


def draw_lengths(key, part):
    key = jax.random.fold_in(key, 7)
    pick_key, length_key = jax.random.split(key)
    longest = jax.random.randint(pick_key, (GROUPS,), 0, SEQS)
    drawn_lengths = jax.random.randint(length_key, (GROUPS, SEQS), MINLEN, CAP * N_SEQ + 1)
    slot_ids = jnp.arange(SEQS, dtype=jnp.int32)[None, :]
    return jnp.where(slot_ids == longest[:, None], CAP * N_SEQ, drawn_lengths).astype(jnp.int32)


def with_spikes(result, own_key, source, target, parts, factor):
    def block_of(position):
        return (jnp.arange(result.shape[position]) // (result.shape[position] // parts)).reshape((-1,) + (1,) * (result.ndim - 1 - position))

    near = jax.random.permutation(own_key, parts)[block_of(target)]
    far = (block_of(target) + parts // 2) % parts
    return jnp.where((block_of(source) == near) | (block_of(source) == far), factor * result, result)


def steps_of(key, shape, cuts, smallest, largest):
    def one(position, parts):
        draws = jax.random.uniform(jax.random.fold_in(jax.random.fold_in(key, 6), position), (parts,), jnp.float32, smallest / len(cuts), largest / len(cuts))
        return jnp.repeat(jnp.exp(draws), shape[position] // parts).reshape((-1,) + (1,) * (len(shape) - position - 1))

    gain = one(*cuts[0])
    for cut in cuts[1:]:
        gain = gain * one(*cut)
    return gain


def centred(stream_key, shape, scale, limit, shards=(), kind=jnp.bfloat16):
    result = jax.random.normal(stream_key, shape, jnp.float32) * scale
    if len(shards) > 0:
        result = steps_of(stream_key, shape, shards, -0.22, 0.18) * result
    return jnp.clip(result, min=-limit, max=limit).astype(kind)


def noise_with(own_key, extent, scale, reach, pieces, heavy, kind=jnp.bfloat16):
    entries = scale * jax.random.normal(own_key, extent, jnp.float32)
    if pieces:
        entries = entries * steps_of(own_key, extent, pieces, -0.22, 0.18)
    return jnp.clip(with_spikes(entries, jax.random.fold_in(own_key, 3), *heavy), -reach, reach).astype(kind)


def setup_inputs(seed: int = 0) -> dict:
    keys = jax.random.split(jax.random.key(seed), 15)
    tokens = noise_with(keys[0], (GROUPS, SEQS, MAXLEN, D), 1.0, 6.0, ((0, 4), (2, 8)), (2, 3, 8, 2.0))
    lengths = draw_lengths(jax.random.fold_in(keys[14], 71), 0)
    attn_gain = jnp.clip(1.0 + 0.15 * jax.random.normal(keys[2], (D,), jnp.float32), 0.25, 1.75).astype(jnp.bfloat16)
    w_qdown = centred(keys[3], (D, QL), D ** -0.5, 0.125, ((0, 32),))
    q_gain = jnp.clip(1.0 + 0.15 * jax.random.normal(keys[4], (QL,), jnp.float32), 0.25, 1.75).astype(jnp.bfloat16)
    w_qup = centred(keys[5], (QL, HEADS * HD), QL ** -0.5, 0.1875, ((0, 32),))
    w_key = centred(keys[6], (D, HD), D ** -0.5, 0.125, ((0, 32),))
    w_value = centred(keys[7], (D, HD), D ** -0.5, 0.125, ((0, 32),))
    w_out = centred(keys[8], (HEADS * HD, D), (max(4, HEADS * HD // 256)) ** -0.5, 1.5, ((0, 32),))
    ffn_gain = jnp.clip(1.0 + 0.15 * jax.random.normal(keys[9], (D,), jnp.float32), 0.25, 1.75).astype(jnp.bfloat16)
    w_gate = centred(keys[10], (D, FF), D ** -0.5, 0.125, ((0, 32),))
    w_up = centred(keys[11], (D, FF), D ** -0.5, 0.125, ((0, 32),))
    w_down = centred(keys[12], (FF, D), FF ** -0.5, 0.078125, ((0, 32),))
    cotangent = centred(keys[13], (GROUPS, SEQS, MAXLEN, D), 1.0, 6.0, ((0, 4), (2, 8)))
    return {"tokens": tokens, "lengths": lengths, "attn_gain": attn_gain, "w_qdown": w_qdown, "q_gain": q_gain, "w_qup": w_qup, "w_key": w_key, "w_value": w_value, "w_out": w_out, "ffn_gain": ffn_gain, "w_gate": w_gate, "w_up": w_up, "w_down": w_down, "cotangent": cotangent}


epsilon = 1e-06

@jax.custom_vjp
def low(v):
    return lax.optimization_barrier(v.astype(jnp.bfloat16)).astype(jnp.float32)

@jax.custom_vjp
def low_back(v):
    return v

def low_keep(v):
    return (low(v), None)

def low_pass(kept, grad):
    return (grad,)

def back_keep(v):
    return (v, None)

def back_low(kept, grad):
    return (low(grad),)
low.defvjp(low_keep, low_pass)
low_back.defvjp(back_keep, back_low)

def matmul(left, right):
    return jnp.dot(left, right, precision=lax.Precision.HIGHEST, preferred_element_type=jnp.float32)

def rms_scale(values):
    return lax.rsqrt(lax.optimization_barrier(jnp.mean(values * values, axis=-1, keepdims=True)) + epsilon)

def rotate_half(values):
    half_width = values.shape[-1] // 2
    return jnp.concatenate([-values[..., half_width:], values[..., :half_width]], axis=-1)

def rotary(positions, head_width):
    half_width = head_width // 2
    frequency = jnp.exp(jnp.arange(half_width, dtype=jnp.float32) * (-2.0 * math.log(10000.0) / head_width))
    angles = positions.astype(jnp.float32)[:, None] * frequency[None, :]
    cos_table = jnp.cos(angles)
    sin_table = jnp.sin(angles)
    return (jnp.concatenate([cos_table, cos_table], -1), jnp.concatenate([sin_table, sin_table], -1))

def attend(query_rows, key_rows, value_rows, length):
    seq_span = key_rows.shape[0]
    flat_queries = query_rows.reshape(seq_span * HEADS, HD)
    scores = low_back(matmul(flat_queries, key_rows.T) * (1.0 / math.sqrt(HD)))
    query_pos = jnp.repeat(jnp.arange(seq_span, dtype=jnp.int32), HEADS)
    key_pos = jnp.arange(seq_span, dtype=jnp.int32)
    visible = (key_pos[None, :] <= query_pos[:, None]) & (key_pos[None, :] < length)
    scores = jnp.where(visible, scores, -1e+30)
    row_top = lax.optimization_barrier(jnp.max(scores, axis=-1, keepdims=True))
    log_total = row_top + jnp.log(lax.optimization_barrier(jnp.sum(jnp.exp(scores - row_top), axis=-1, keepdims=True)))
    attn_probs = low(jnp.exp(scores - log_total))
    return matmul(attn_probs, value_rows).reshape(seq_span, HEADS * HD)

def layer_group(params, group_rows, group_lengths):
    attn_gain, w_qdown, q_gain, w_qup, w_key, w_value, w_out, ffn_gain, w_gate, w_up, w_down = params
    slot_count, seq_span, model_width = group_rows.shape
    flat_rows = group_rows.reshape(slot_count * seq_span, model_width)
    normed = low(flat_rows * rms_scale(flat_rows) * attn_gain)
    q_down = low_back(matmul(normed, w_qdown))
    q_normed = low(q_down * rms_scale(q_down) * q_gain)
    q_raw = low_back(matmul(q_normed, w_qup)).reshape(slot_count, seq_span, HEADS, HD)
    cos_table, sin_table = rotary(jnp.arange(seq_span, dtype=jnp.int32), HD)
    queries = low(q_raw * cos_table[None, :, None, :] + rotate_half(q_raw) * sin_table[None, :, None, :])
    k_raw = low_back(matmul(normed, w_key)).reshape(slot_count, seq_span, HD)
    key_rows = low(k_raw * cos_table + rotate_half(k_raw) * sin_table)
    value_rows = low(low_back(matmul(normed, w_value))).reshape(slot_count, seq_span, HD)
    attend_block = jax.checkpoint(attend)
    mixed = lax.map(lambda member: attend_block(member[0], member[1], member[2], member[3]), (queries, key_rows, value_rows, group_lengths))
    mixed = low(low_back(mixed.reshape(slot_count * seq_span, HEADS * HD)))
    middle = flat_rows + low_back(matmul(mixed, w_out))
    normed2 = low(middle * rms_scale(middle) * ffn_gain)
    gate_proj = low_back(matmul(normed2, w_gate))
    up_proj = low_back(matmul(normed2, w_up))
    activated = low(jax.nn.silu(gate_proj) * up_proj)
    output = middle + low_back(matmul(activated, w_down))
    return output.reshape(slot_count, seq_span, model_width)

def reference(tokens, lengths, attn_gain, w_qdown, q_gain, w_qup, w_key, w_value, w_out, ffn_gain, w_gate, w_up, w_down, cotangent):
    params = (attn_gain.astype(jnp.float32), w_qdown.astype(jnp.float32), q_gain.astype(jnp.float32), w_qup.astype(jnp.float32), w_key.astype(jnp.float32), w_value.astype(jnp.float32), w_out.astype(jnp.float32), ffn_gain.astype(jnp.float32), w_gate.astype(jnp.float32), w_up.astype(jnp.float32), w_down.astype(jnp.float32))
    inputs = tokens.astype(jnp.float32)
    valid_mask = (jnp.arange(MAXLEN, dtype=jnp.int32)[None, None, :] < lengths[:, :, None]).astype(jnp.float32)

    def forward(weights, rows):
        group_step = jax.checkpoint(partial(layer_group, weights))
        return lax.map(lambda member: group_step(member[0], member[1]), (rows, lengths))
    output, pullback = jax.vjp(forward, params, inputs)
    grad_params, grad_inputs = pullback(cotangent.astype(jnp.float32) * valid_mask[..., None])
    factor = 1.0 / math.sqrt(TOKENS)
    return (output.astype(jnp.bfloat16), grad_inputs, grad_params[0] * factor, grad_params[1] * factor, grad_params[2] * factor, grad_params[3] * factor, grad_params[4] * factor, grad_params[5] * factor, grad_params[6] * factor, grad_params[7] * factor, grad_params[8] * factor, grad_params[9] * factor, grad_params[10] * factor)
```

```python
import math

import jax
import jax.numpy as jnp
import numpy as np
from jax import lax
from jax.sharding import Mesh
from jax.sharding import PartitionSpec as P

epsilon = 1e-06
CORES = 2
f32, bf16 = jnp.float32, jnp.bfloat16


def rms_scale(values):
    return lax.rsqrt(jnp.mean(values * values, axis=-1, keepdims=True) + epsilon)


def rotate_half(values):
    half_width = values.shape[-1] // 2
    return jnp.concatenate([-values[..., half_width:], values[..., :half_width]], axis=-1)


def rotary(positions, head_width):
    half_width = head_width // 2
    frequency = jnp.exp(
        jnp.arange(half_width, dtype=f32) * (-2.0 * math.log(10000.0) / head_width)
    )
    angles = positions.astype(f32)[:, None] * frequency[None, :]
    cos_table = jnp.cos(angles)
    sin_table = jnp.sin(angles)
    return (
        jnp.concatenate([cos_table, cos_table], -1),
        jnp.concatenate([sin_table, sin_table], -1),
    )


def matmul(left, right):
    return jnp.dot(left, right, preferred_element_type=f32)


def inner_rows(left, right):
    return lax.dot_general(left, right, (((0,), (0,)), ((), ())), preferred_element_type=f32)


def outer_cols(left, right):
    return lax.dot_general(left, right, (((1,), (1,)), ((), ())), preferred_element_type=f32)


def norm_back(grad_in, inputs, scale_rows, gain):
    weighted = grad_in * gain
    return scale_rows * weighted - inputs * scale_rows**3 * jnp.mean(
        weighted * inputs, axis=-1, keepdims=True
    )


def take(blocks, index):
    return lax.dynamic_index_in_dim(blocks, index, 0, keepdims=False)


def swap_cores(block):
    return lax.ppermute(block, "core", [(0, 1), (1, 0)])


def to_chip(block, bits):
    count = lax.axis_size("chip")
    return lax.ppermute(block, "chip", [(i, i ^ bits) for i in range(count)])


def placed_blocks(pairs, count):
    result = jnp.zeros((count,) + pairs[0][1].shape, pairs[0][1].dtype)
    for index, block in pairs:
        result = lax.dynamic_update_index_in_dim(result, block, index, 0)
    return result


def gather_chips(block):
    count, me = lax.axis_size("chip"), lax.axis_index("chip")
    rows = block.shape[0]
    if count != 4:
        return lax.all_gather(block, "chip", axis=0, tiled=True)
    top, low = block[: rows // 2], block[rows // 2 :]
    top_x, low_y = to_chip(top, 1), to_chip(low, 2)
    top_y, low_x = to_chip(top, 2), to_chip(low, 1)
    top_d, low_d = to_chip(top_x, 2), to_chip(low_y, 1)
    pairs = [
        (2 * me, top),
        (2 * me + 1, low),
        (2 * (me ^ 1), top_x),
        (2 * (me ^ 1) + 1, low_x),
        (2 * (me ^ 2), top_y),
        (2 * (me ^ 2) + 1, low_y),
        (2 * (me ^ 3), top_d),
        (2 * (me ^ 3) + 1, low_d),
    ]
    return placed_blocks(pairs, 2 * count).reshape(count * rows, block.shape[1])


def add(left, right):
    return left.astype(f32) + right.astype(f32)


def scatter_chips(terms):
    count, me = lax.axis_size("chip"), lax.axis_index("chip")
    if count != 4:
        return lax.psum_scatter(terms, "chip", scatter_dimension=0, tiled=True).astype(f32)
    rows = terms.shape[0] // count
    blocks = terms.reshape(2 * count, rows // 2, terms.shape[1])
    top = [take(blocks, 2 * (me ^ k)) for k in range(4)]
    low = [take(blocks, 2 * (me ^ k) + 1) for k in range(4)]
    top_far = add(top[2], to_chip(top[3], 1)).astype(bf16)
    low_far = add(low[1], to_chip(low[3], 2)).astype(bf16)
    top_near = add(top[0], to_chip(top[1], 1))
    low_near = add(low[0], to_chip(low[2], 2))
    top_sum = top_near + to_chip(top_far, 2).astype(f32)
    low_sum = low_near + to_chip(low_far, 1).astype(f32)
    return jnp.concatenate([top_sum, low_sum], 0)


def exchange_chips(blocks):
    count, me = lax.axis_size("chip"), lax.axis_index("chip")
    pairs = [(me, take(blocks, me))]
    for bits in range(1, count):
        pairs.append((me ^ bits, to_chip(take(blocks, me ^ bits), bits)))
    return placed_blocks(pairs, count)


def by_columns(weight):
    count = lax.axis_size("chip")
    rows, width = weight.shape
    return weight.reshape(rows, count, width // count).transpose(1, 0, 2)


def gather_columns(weight):
    mine = exchange_chips(by_columns(weight))
    whole = lax.all_gather(mine, ("core", "dp"), axis=1, tiled=False)
    return whole.reshape(-1, mine.shape[-1])


def gather_rows(weight):
    return lax.all_gather(weight, ("core", "dp"), axis=0, tiled=True)


def sum_cores(terms):
    me = lax.axis_index("core")
    return add(take(terms, me), swap_cores(take(terms, 1 - me))).astype(bf16)


def scatter_rows(terms):
    rows, width = terms.shape
    half = sum_cores(terms.reshape(CORES, rows // CORES, width))
    return lax.psum_scatter(half, "dp", scatter_dimension=0, tiled=True)


def scatter_columns(terms):
    chips, dp = lax.axis_size("chip"), lax.axis_size("dp")
    width = terms.shape[1]
    split = terms.reshape(chips, CORES, dp, -1, width).transpose(1, 2, 0, 3, 4)
    half = sum_cores(split.reshape(CORES, dp, -1, width))
    mine = lax.psum_scatter(half, "dp", scatter_dimension=0, tiled=True)
    mine = exchange_chips(mine.reshape(chips, -1, width))
    return mine.transpose(1, 0, 2).reshape(-1, chips * width)


def pair_in(block):
    me = lax.axis_index("core")
    kept, got = take(block, me), swap_cores(take(block, 1 - me))
    return jnp.where(
        me == 0, jnp.concatenate([kept, got], 0), jnp.concatenate([got, kept], 0)
    )


def pair_out(rows):
    me = lax.axis_index("core")
    blocks = rows.reshape(CORES, -1, rows.shape[1])
    kept, got = take(blocks, me), swap_cores(take(blocks, 1 - me))
    return jnp.where(me == 0, jnp.stack([kept, got]), jnp.stack([got, kept]))


def attention_scores(queries, keys, length, score_scale):
    span = keys.shape[0]
    pos = jnp.arange(span, dtype=jnp.int32)
    visible = (pos[None, :] <= pos[:, None]) & (pos[None, :] < length)
    scores = jnp.einsum("hqd,kd->hqk", queries, keys, preferred_element_type=f32)
    return jnp.where(visible[None], scores * score_scale, -1e30)


def per_device(
    tokens,
    lengths,
    attn_gain,
    w_qdown,
    q_gain,
    w_qup,
    w_key,
    w_value,
    w_out,
    ffn_gain,
    w_gate,
    w_up,
    w_down,
    cotangent,
):
    slot_count, seq_span, width = tokens.shape[1:]
    assert slot_count == CORES
    chips, dp = lax.axis_size("chip"), lax.axis_size("dp")
    chip, core = lax.axis_index("chip"), lax.axis_index("core")
    devices = chips * CORES * dp
    row_count = CORES * seq_span
    span = chips * row_count
    head_width = w_key.shape[1]
    q_width = w_qdown.shape[1]
    heads = w_qup.shape[1] // head_width // chips
    score_scale = 1.0 / math.sqrt(head_width)
    grad_scale = 1.0 / math.sqrt(slot_count * seq_span * devices)

    own_rows, own_q = attn_gain.shape[0], q_gain.shape[0]
    gains = jnp.stack([attn_gain, ffn_gain, jnp.pad(q_gain, (0, own_rows - own_q))], 1)
    small = jnp.concatenate([w_qdown, w_key, w_value, jnp.pad(gains, ((0, 0), (0, 125)))], 1)
    small = lax.all_gather(small, ("chip", "core", "dp"), axis=0, tiled=True)
    down_q = small[:, :q_width]
    key_value = small[:, q_width : q_width + 2 * head_width]
    gains = small[:, q_width + 2 * head_width :][:, :3].astype(f32)
    gain_one, gain_two = gains[:, 0], gains[:, 1]
    gain_q = gains[:, 2].reshape(devices, own_rows)[:, :own_q].reshape(-1)
    up_q = gather_columns(w_qup)
    out_proj = gather_rows(w_out)
    gate_proj = gather_columns(w_gate)
    up_proj = gather_columns(w_up)
    down_proj = gather_rows(w_down)

    length = lengths[0, core]
    positions = chip * row_count + jnp.arange(row_count, dtype=jnp.int32)
    cos_own, sin_own = rotary(positions, head_width)
    cos_all, sin_all = rotary(jnp.arange(span, dtype=jnp.int32), head_width)
    valid_mask = (positions < length).astype(f32)[:, None]

    inputs = pair_in(tokens[0]).astype(f32)
    seed_grad = (pair_in(cotangent[0]).astype(f32) * valid_mask).astype(bf16)
    seed_all = gather_chips(seed_grad)

    scale_one = rms_scale(inputs)
    normed = (inputs * scale_one * gain_one).astype(bf16)
    normed_cols = exchange_chips(by_columns(normed)).reshape(span, -1)
    q_down = matmul(normed, down_q)
    scale_q = rms_scale(q_down)
    q_normed = (q_down * scale_q * gain_q).astype(bf16)
    kv_raw = matmul(normed, key_value)
    k_raw, v_raw = kv_raw[:, :head_width], kv_raw[:, head_width:]
    key_rows = (k_raw * cos_own + rotate_half(k_raw) * sin_own).astype(bf16)
    shared = gather_chips(jnp.concatenate([q_normed, key_rows, v_raw.astype(bf16)], 1))
    q_normed_all = shared[:, :q_width]
    keys = shared[:, q_width : q_width + head_width]
    values = shared[:, q_width + head_width :]

    q_raw = matmul(q_normed_all, up_q).reshape(span, heads, head_width)
    queries = (q_raw * cos_all[:, None] + rotate_half(q_raw) * sin_all[:, None]).astype(bf16)
    queries = queries.transpose(1, 0, 2)
    scores = attention_scores(queries, keys, length, score_scale)
    row_top = jnp.max(scores, axis=-1, keepdims=True)
    log_total = row_top + jnp.log(jnp.sum(jnp.exp(scores - row_top), axis=-1, keepdims=True))
    probs = jnp.exp(scores - log_total).astype(bf16)
    mixed = jnp.einsum("hqk,kd->hqd", probs, values, preferred_element_type=f32)
    mixed = mixed.astype(bf16).transpose(1, 0, 2).reshape(span, heads * head_width)
    middle = inputs + scatter_chips(matmul(mixed, out_proj).astype(bf16))
    scale_two = rms_scale(middle)
    normed2 = gather_chips((middle * scale_two * gain_two).astype(bf16))

    gate_val = matmul(normed2, gate_proj)
    up_val = matmul(normed2, up_proj)
    sigma = jax.nn.sigmoid(gate_val)
    activated = (gate_val * sigma * up_val).astype(bf16)
    output = middle + scatter_chips(matmul(activated, down_proj).astype(bf16))
    out_tokens = pair_out(output.astype(bf16))[None]

    grad_act = outer_cols(seed_all, down_proj)
    gate_grad = (grad_act * up_val * sigma * (1.0 + gate_val * (1.0 - sigma))).astype(bf16)
    up_grad = (grad_act * gate_val * sigma).astype(bf16)
    grad_normed2 = scatter_chips(
        (outer_cols(gate_grad, gate_proj) + outer_cols(up_grad, up_proj)).astype(bf16)
    )
    grad_w_down = scatter_rows((inner_rows(activated, seed_all) * grad_scale).astype(bf16))
    grad_w_gate = scatter_columns((inner_rows(normed2, gate_grad) * grad_scale).astype(bf16))
    grad_w_up = scatter_columns((inner_rows(normed2, up_grad) * grad_scale).astype(bf16))
    gain_two_terms = jnp.sum(grad_normed2 * middle * scale_two, axis=0) * grad_scale
    grad_middle = seed_grad.astype(f32) + norm_back(grad_normed2, middle, scale_two, gain_two)
    grad_branch = gather_chips(grad_middle.astype(bf16))
    grad_mixed = outer_cols(grad_branch, out_proj).astype(bf16)
    grad_w_out = scatter_rows((inner_rows(mixed, grad_branch) * grad_scale).astype(bf16))

    grad_mixed = grad_mixed.reshape(span, heads, head_width).transpose(1, 0, 2)
    scores = attention_scores(queries, keys, length, score_scale)
    exact = jnp.exp(scores - log_total)
    grad_probs = jnp.einsum("hqd,kd->hqk", grad_mixed, values, preferred_element_type=f32)
    grad_scores = (
        exact * (grad_probs - jnp.sum(exact * grad_probs, axis=-1, keepdims=True))
    ).astype(bf16)
    grad_q = jnp.einsum("hqk,kd->qhd", grad_scores, keys, preferred_element_type=f32)
    grad_q = grad_q * score_scale
    grad_k = jnp.einsum("hqk,hqd->kd", grad_scores, queries, preferred_element_type=f32)
    grad_v = jnp.einsum(
        "hqk,hqd->kd", exact.astype(bf16), grad_mixed, preferred_element_type=f32
    )
    grad_q = grad_q * cos_all[:, None] - rotate_half(grad_q * sin_all[:, None])
    grad_q = grad_q.astype(bf16).reshape(span, heads * head_width)
    grad_w_qup = scatter_columns((inner_rows(q_normed_all, grad_q) * grad_scale).astype(bf16))
    back = jnp.concatenate([outer_cols(grad_q, up_q), grad_k * score_scale, grad_v], 1)
    back = scatter_chips(back.astype(bf16))
    grad_q_normed = back[:, :q_width]
    key_sum = back[:, q_width : q_width + head_width]
    value_sum = back[:, q_width + head_width :]
    grad_k = key_sum * cos_own - rotate_half(key_sum * sin_own)
    grad_q_down = norm_back(grad_q_normed, q_down, scale_q, gain_q)
    gain_q_terms = jnp.sum(grad_q_normed * q_down * scale_q, axis=0) * grad_scale
    back = jnp.concatenate([grad_q_down, grad_k, value_sum], 1).astype(bf16)
    grad_normed = outer_cols(back, small[:, : q_width + 2 * head_width])
    grad_inputs = grad_middle + norm_back(grad_normed, inputs, scale_one, gain_one)
    grad_tokens = pair_out(grad_inputs)[None]
    gain_one_terms = jnp.sum(grad_normed * inputs * scale_one, axis=0) * grad_scale

    grad_small = (inner_rows(normed_cols, gather_chips(back)) * grad_scale).astype(bf16)
    grad_small = scatter_rows(grad_small).astype(f32)
    grad_gains = jnp.concatenate(
        [
            gain_one_terms.reshape(devices, own_rows),
            gain_two_terms.reshape(devices, own_rows),
            gain_q_terms.reshape(devices, own_q),
        ],
        1,
    )
    grad_gains = lax.psum_scatter(
        grad_gains, ("chip", "core", "dp"), scatter_dimension=0, tiled=True
    )[0]
    return (
        out_tokens,
        grad_tokens,
        grad_gains[:own_rows],
        grad_small[:, :q_width],
        grad_gains[2 * own_rows :],
        grad_w_qup.astype(f32),
        grad_small[:, q_width : q_width + head_width],
        grad_small[:, q_width + head_width :],
        grad_w_out.astype(f32),
        grad_gains[own_rows : 2 * own_rows],
        grad_w_gate.astype(f32),
        grad_w_up.astype(f32),
        grad_w_down.astype(f32),
    )


def solution(mesh):
    seq, dp = mesh.shape["seq"], mesh.shape["dp"]
    chips = Mesh(
        np.asarray(mesh.devices).reshape(seq // CORES, CORES, dp), ("chip", "core", "dp")
    )
    every = ("chip", "core", "dp")
    rows, vector = P(every, None), P(every)
    block = P("dp", None, ("chip", "core"), None)
    weights = (vector, rows, vector, rows, rows, rows, rows, vector, rows, rows, rows)
    return jax.shard_map(
        per_device,
        mesh=chips,
        in_specs=(block, P("dp", None)) + weights + (block,),
        out_specs=(block, block) + weights,
        check_vma=False,
    )
```

```python
import functools
import math

import jax
import jax.numpy as jnp
import numpy as np
from jax import lax
from jax.experimental import pallas as pl
from jax.experimental.pallas import tpu as pltpu
from jax.sharding import Mesh
from jax.sharding import PartitionSpec as P

epsilon = 1e-06
CORES = 2
TILE = 256
f32, bf16 = jnp.float32, jnp.bfloat16
BESIDE = pl.CostEstimate(flops=1, bytes_accessed=1, transcendentals=0)


def rms_scale(values):
    return lax.rsqrt(jnp.mean(values * values, axis=-1, keepdims=True) + epsilon)


def rotate_half(values):
    half_width = values.shape[-1] // 2
    return jnp.concatenate([-values[..., half_width:], values[..., :half_width]], axis=-1)


def rotary(positions, head_width):
    half_width = head_width // 2
    frequency = jnp.exp(
        jnp.arange(half_width, dtype=f32) * (-2.0 * math.log(10000.0) / head_width)
    )
    angles = positions.astype(f32)[:, None] * frequency[None, :]
    cos_table = jnp.cos(angles)
    sin_table = jnp.sin(angles)
    return (
        jnp.concatenate([cos_table, cos_table], -1),
        jnp.concatenate([sin_table, sin_table], -1),
    )


def matmul(left, right):
    return jnp.dot(left, right, preferred_element_type=f32)


def inner_rows(left, right):
    return lax.dot_general(left, right, (((0,), (0,)), ((), ())), preferred_element_type=f32)


def outer_cols(left, right):
    return lax.dot_general(left, right, (((1,), (1,)), ((), ())), preferred_element_type=f32)


def norm_back(grad_in, inputs, scale_rows, gain):
    weighted = grad_in * gain
    return scale_rows * weighted - inputs * scale_rows**3 * jnp.mean(
        weighted * inputs, axis=-1, keepdims=True
    )


def take(blocks, index):
    return lax.dynamic_index_in_dim(blocks, index, 0, keepdims=False)


def swap_cores(block):
    return lax.ppermute(block, "core", [(0, 1), (1, 0)])


def to_chip(block, bits):
    count = lax.axis_size("chip")
    return lax.ppermute(block, "chip", [(i, i ^ bits) for i in range(count)])


def gather_near(block):
    rows = block.shape[0]
    if lax.axis_size("chip") != 4:
        return (block,)
    top, low = block[: rows // 2], block[rows // 2 :]
    return top, low, to_chip(top, 1), to_chip(low, 1), to_chip(top, 2), to_chip(low, 2)


def join_kernel(*refs):
    *piece_refs, out_ref = refs
    for k, ref in enumerate(piece_refs):

        @pl.when(pl.program_id(0) == k)
        def _():
            out_ref[...] = ref[...]


def join_rows(pieces):
    rows, width = pieces[0].shape
    count = len(pieces)
    return pl.pallas_call(
        join_kernel,
        grid=(count,),
        in_specs=[pl.BlockSpec((rows, width), lambda k: (0, 0))] * count,
        out_specs=pl.BlockSpec((rows, width), lambda k: (k, 0)),
        out_shape=jax.ShapeDtypeStruct((count * rows, width), pieces[0].dtype),
        compiler_params=pltpu.CompilerParams(vmem_limit_bytes=24 << 20),
        cost_estimate=BESIDE,
    )(*pieces)


def gather_far(near):
    if lax.axis_size("chip") != 4:
        return lax.all_gather(near[0], "chip", axis=0, tiled=True)
    return join_rows(list(near) + list(far_halves(near)))


def far_halves(near):
    return to_chip(near[2], 2), to_chip(near[5], 1)


def chip_flip():
    return lax.axis_index("chip") if lax.axis_size("chip") == 4 else jnp.int32(0)


def reordered(blocks, flip):
    bits = 1
    while bits < len(blocks):
        swapped = [blocks[k ^ bits] for k in range(len(blocks))]
        blocks = [jnp.where(flip & bits > 0, b, a) for a, b in zip(blocks, swapped)]
        bits *= 2
    return blocks


def gather_chips(block):
    return gather_far(gather_near(block))


def add(left, right):
    return left.astype(f32) + right.astype(f32)


def scatter_near(pieces):
    if lax.axis_size("chip") != 4:
        return tuple(pieces)
    top, low = pieces[::2], pieces[1::2]
    top_far = add(top[2], to_chip(top[3], 1)).astype(bf16)
    low_far = add(low[1], to_chip(low[3], 2)).astype(bf16)
    return top_far, low_far, top[0], to_chip(top[1], 1), low[0], to_chip(low[2], 2)


def scatter_far(near):
    if lax.axis_size("chip") != 4:
        return lax.psum_scatter(near[0], "chip", scatter_dimension=0, tiled=True).astype(f32)
    top_far, low_far, top, top_x, low, low_y = near
    top = add(top, top_x) + to_chip(top_far, 2).astype(f32)
    low = add(low, low_y) + to_chip(low_far, 1).astype(f32)
    return jnp.concatenate([top, low], 0)


def scatter_chips(pieces, beside=()):
    near, beside = tie(scatter_near(pieces), tuple(beside))
    total = scatter_far(near)
    return (total,) + beside if beside else total


def exchange(parts):
    count = lax.axis_size("chip")
    if count != 4:
        blocks = lax.all_to_all(jnp.stack(parts), "chip", 0, 0, tiled=True)
        return [blocks[k] for k in range(count)]
    return [parts[0]] + [to_chip(parts[k], k) for k in range(1, count)]


def tie(*values):
    return lax.optimization_barrier(values)


def by_columns(weight):
    count = lax.axis_size("chip")
    rows, width = weight.shape
    return weight.reshape(rows, count, width // count).transpose(1, 0, 2)


def gather_columns(parts):
    mine = jnp.stack(exchange(parts))[:, None]
    whole = lax.all_gather(mine, ("core", "dp"), axis=1, tiled=True)
    return whole


def gather_rows(weight):
    return lax.all_gather(weight, ("core", "dp"), axis=0, tiled=True)


def sum_cores(terms):
    me = lax.axis_index("core")
    return add(take(terms, me), swap_cores(take(terms, 1 - me))).astype(bf16)


def halve_rows(terms):
    rows, width = terms.shape
    return sum_cores(terms.reshape(CORES, rows // CORES, width))


def scatter_dp(half):
    return lax.psum_scatter(half, "dp", scatter_dimension=0, tiled=True)


def halve_columns(terms):
    cores, dp, chips, own, width = terms.shape
    return sum_cores(terms.reshape(cores, dp, chips * own, width))


def join_blocks(mine):
    blocks = exchange(jnp.split(mine.reshape(-1, mine.shape[-1]), lax.axis_size("chip"), 0))
    return reordered(blocks, chip_flip())


def join_columns(mine):
    return jnp.concatenate(join_blocks(mine), 1).astype(f32)


def sum_chips(values):
    count, bits = lax.axis_size("chip"), 1
    while bits < count:
        values = values + to_chip(values, bits)
        bits *= 2
    return values


def row_sums(values):
    sums = jnp.sum(values, axis=-1).reshape(-1, 128)
    return sum_chips(sums).reshape(-1, 1)


def pair_in(block):
    me = lax.axis_index("core")
    kept, got = take(block, me), swap_cores(take(block, 1 - me))
    return jnp.where(
        me == 0, jnp.concatenate([kept, got], 0), jnp.concatenate([got, kept], 0)
    )


def pair_out(rows):
    me = lax.axis_index("core")
    blocks = rows.reshape(CORES, -1, rows.shape[1])
    kept, got = take(blocks, me), swap_cores(take(blocks, 1 - me))
    return jnp.where(me == 0, jnp.stack([kept, got]), jnp.stack([got, kept]))


def visible_scores(keys, queries, first, length, score_scale):
    scores = outer_cols(keys, queries) * score_scale
    key_pos = lax.broadcasted_iota(jnp.int32, scores.shape, 0)
    query_pos = lax.broadcasted_iota(jnp.int32, scores.shape, 1) + first
    return jnp.where((key_pos <= query_pos) & (key_pos < length), scores, -1e30)


def flipped(start, flip):
    return pl.ds(pl.multiple_of(((start // TILE) ^ flip) * TILE, TILE), TILE)


def attend_kernel(
    score_scale,
    length_ref,
    flip_ref,
    rows_ref,
    up_ref,
    keys_ref,
    values_t_ref,
    cos_ref,
    sin_ref,
    queries_ref,
    mixed_ref,
    total_ref,
):
    length, flip = length_ref[0], flip_ref[0]
    chips = lax.axis_size("chip")
    depth = up_ref.shape[1]
    for start in range(0, keys_ref.shape[0], TILE):
        stop = start + TILE
        raw = 0.0
        for part in range(chips):
            raw = raw + matmul(rows_ref[part, start:stop, :depth], up_ref[part])
        raw = raw * cos_ref[start:stop, :] + rotate_half(raw) * sin_ref[start:stop, :]
        queries = raw.astype(bf16)
        queries_ref[start:stop, :] = queries
        scores = visible_scores(keys_ref[:stop, :], queries, start, length, score_scale)
        top = jnp.max(scores, axis=0, keepdims=True)
        powers = jnp.exp(scores - top)
        total = jnp.sum(powers, axis=0, keepdims=True)
        total_ref[0, :, start:stop] = top + jnp.log(total)
        probs = (powers * (1.0 / total)).astype(bf16)
        mixed = matmul(values_t_ref[:, :stop], probs)
        mixed_ref[flipped(start, flip), :] = mixed.T.astype(bf16)


def attend(length, flip, rows, up, keys, values, cos_table, sin_table, score_scale):
    span, head_width = keys.shape
    heads = up.shape[2] // head_width
    whole = lambda array: pl.BlockSpec(array.shape, lambda h: (0, 0))
    head = lambda height: pl.BlockSpec((height, head_width), lambda h: (0, h))
    values_t = values.T
    return pl.pallas_call(
        functools.partial(attend_kernel, score_scale),
        grid=(heads,),
        in_specs=[
            pl.BlockSpec(memory_space=pltpu.SMEM),
            pl.BlockSpec(memory_space=pltpu.SMEM),
            pl.BlockSpec(rows.shape, lambda h: (0, 0, 0)),
            pl.BlockSpec(up.shape[:2] + (head_width,), lambda h: (0, 0, h)),
            whole(keys),
            whole(values_t),
            whole(cos_table),
            whole(sin_table),
        ],
        out_specs=[
            head(span),
            head(span),
            pl.BlockSpec((1, 1, span), lambda h: (h, 0, 0)),
        ],
        out_shape=[
            jax.ShapeDtypeStruct((span, heads * head_width), bf16),
            jax.ShapeDtypeStruct((span, heads * head_width), bf16),
            jax.ShapeDtypeStruct((heads, 1, span), f32),
        ],
        compiler_params=pltpu.CompilerParams(vmem_limit_bytes=48 << 20),
        cost_estimate=BESIDE,
    )(length, flip, rows, up, keys, values_t, cos_table, sin_table)


def attend_back_kernel(
    score_scale,
    length_ref,
    flip_ref,
    queries_ref,
    grad_ref,
    total_ref,
    keys_ref,
    keys_t_ref,
    values_ref,
    cos_ref,
    sin_ref,
    grad_q_ref,
    grad_k_ref,
    grad_v_ref,
):
    length, flip = length_ref[0], flip_ref[0]

    @pl.when(pl.program_id(0) == 0)
    def _():
        grad_k_ref[...] = jnp.zeros_like(grad_k_ref)
        grad_v_ref[...] = jnp.zeros_like(grad_v_ref)

    for start in range(0, queries_ref.shape[0], TILE):
        stop = start + TILE
        queries, grads = queries_ref[start:stop, :], grad_ref[flipped(start, flip), :]
        scores = visible_scores(keys_ref[:stop, :], queries, start, length, score_scale)
        probs = jnp.exp(scores - total_ref[0, :, start:stop])
        grad_probs = outer_cols(values_ref[:stop, :], grads)
        mean = jnp.sum(probs * grad_probs, axis=0, keepdims=True)
        grad_scores = (probs * (grad_probs - mean)).astype(bf16)
        grad_v_ref[:stop, :] += matmul(probs.astype(bf16), grads)
        grad_k_ref[:stop, :] += matmul(grad_scores, queries) * score_scale
        grad_q = matmul(keys_t_ref[:, :stop], grad_scores).T * score_scale
        grad_q = grad_q * cos_ref[start:stop, :] - rotate_half(
            grad_q * sin_ref[start:stop, :]
        )
        grad_q_ref[start:stop, :] = grad_q.astype(bf16)


def attend_back(
    length, flip, queries, grads, total, keys, values, cos_table, sin_table, score_scale
):
    span, head_width = keys.shape
    heads = queries.shape[1] // head_width
    whole = lambda array: pl.BlockSpec(array.shape, lambda h: (0, 0))
    head = pl.BlockSpec((span, head_width), lambda h: (0, h))
    keys_t = keys.T
    summed = jax.ShapeDtypeStruct((span, head_width), f32)
    return pl.pallas_call(
        functools.partial(attend_back_kernel, score_scale),
        grid=(heads,),
        in_specs=[
            pl.BlockSpec(memory_space=pltpu.SMEM),
            pl.BlockSpec(memory_space=pltpu.SMEM),
            head,
            head,
            pl.BlockSpec((1, 1, span), lambda h: (h, 0, 0)),
            whole(keys),
            whole(keys_t),
            whole(values),
            whole(cos_table),
            whole(sin_table),
        ],
        out_specs=[head, whole(keys), whole(keys)],
        out_shape=[jax.ShapeDtypeStruct(queries.shape, bf16), summed, summed],
        compiler_params=pltpu.CompilerParams(vmem_limit_bytes=48 << 20),
        cost_estimate=BESIDE,
    )(length, flip, queries, grads, total, keys, keys_t, values, cos_table, sin_table)


CONTRACT = {"nn": ((1,), (0,)), "nt": ((1,), (1,)), "tn": ((0,), (0,))}


def write_halves(out_refs, block, value):
    rows = value.shape[0] // 2
    for k in range(len(out_refs) // 2):

        @pl.when(block == k)
        def _():
            out_refs[2 * k][...] = value[:rows]
            out_refs[2 * k + 1][...] = value[rows:]


def product_kernel(kind, scale, layout, count, _, *refs):
    inputs, out_refs = refs[: 2 * count], refs[2 * count :]
    total = 0.0
    for left, right in zip(inputs[::2], inputs[1::2]):
        total = total + lax.dot_general(
            left[...], right[...], (CONTRACT[kind], ((), ())), preferred_element_type=f32
        )
    out_ref = out_refs[0]
    total = (total * scale).astype(bf16)
    if layout == "split":
        out_ref[0, :, 0] = total.reshape(out_ref.shape[1], out_ref.shape[3], out_ref.shape[4])
    elif layout == "pieces":
        write_halves(out_refs, pl.program_id(0), total)
    else:
        out_ref[...] = total


def product(kind, *pairs, scale=1.0, layout=None, plain=False):
    left, right = pairs[0]
    rows = left.shape[1] if kind == "tn" else left.shape[0]
    width = right.shape[0] if kind == "nt" else right.shape[1]
    chips, dp = lax.axis_size("chip"), lax.axis_size("dp")
    own = rows // (chips * CORES * dp)
    tiles = [t for t in (256, 128) if rows % t == 0]
    if layout == "split":
        tiles = [dp * own]
    elif layout == "pieces":
        tiles = [rows // chips] if chips == 4 else []
    if not tiles or tiles[0] % 128 or width % 128:
        total = sum(
            lax.dot_general(a, b, (CONTRACT[kind], ((), ())), preferred_element_type=f32)
            for a, b in pairs
        )
        total = (total * scale).astype(bf16)
        if layout == "split":
            total = total.reshape(chips, CORES, dp, own, width).transpose(1, 2, 0, 3, 4)
        return as_pieces(total) if layout == "pieces" else total
    tile = tiles[0]
    inputs, specs = [], []
    for left, right in pairs:
        inputs += [left, right]
        if kind == "tn":
            specs.append(pl.BlockSpec((left.shape[0], tile), lambda i, f: (0, i)))
        else:
            specs.append(pl.BlockSpec((tile, left.shape[1]), lambda i, f: (i, 0)))
        specs.append(pl.BlockSpec(right.shape, lambda i, f: (0, 0)))
    if layout == "split":
        shapes = [(CORES, dp, chips, own, width)]
        outs = [
            pl.BlockSpec(
                (1, dp, 1, own, width), lambda i, f: (i % CORES, 0, (i // CORES) ^ f[0], 0, 0)
            )
        ]
    elif layout == "pieces":
        shapes = [(tile // 2, width)] * (2 * chips)
        outs = [pl.BlockSpec(shape, lambda i, f: (0, 0)) for shape in shapes]
    else:
        shapes = [(rows, width)]
        outs = [pl.BlockSpec((tile, width), lambda i, f: (i, 0))]
    results = pl.pallas_call(
        functools.partial(product_kernel, kind, scale, layout, len(pairs)),
        grid_spec=pltpu.PrefetchScalarGridSpec(
            num_scalar_prefetch=1, grid=(rows // tile,), in_specs=specs, out_specs=outs
        ),
        out_shape=[jax.ShapeDtypeStruct(shape, bf16) for shape in shapes],
        compiler_params=pltpu.CompilerParams(vmem_limit_bytes=56 << 20),
        cost_estimate=BESIDE,
    )(jnp.zeros(1, jnp.int32) if plain else chip_flip()[None], *inputs)
    return results if layout == "pieces" else results[0]


def as_pieces(terms):
    return jnp.split(terms, 8, 0) if lax.axis_size("chip") == 4 else [terms]


def back_kernel(grad_ref, up_ref, grad_k_ref, grad_v_ref, place_ref, *out_refs):
    grads = outer_cols(grad_ref[...], up_ref[0]).astype(bf16)
    parts = jnp.concatenate([grad_k_ref[...], grad_v_ref[...]], 1).astype(bf16)
    parts = outer_cols(parts, place_ref[0]).astype(bf16)
    write_halves(out_refs, pl.program_id(0), jnp.concatenate([grads, parts], 1))


def back_terms(grad_q, up_q, grad_k, grad_v, place):
    chips, depth, width = up_q.shape
    span = grad_q.shape[0]
    if chips != 4:
        grads = jnp.einsum("tn,kin->kti", grad_q, up_q, preferred_element_type=f32)
        parts = jnp.concatenate([grad_k, grad_v], 1).astype(bf16)
        parts = jnp.einsum("sn,kcn->ksc", parts, place, preferred_element_type=f32)
        terms = jnp.concatenate([grads, parts], 2).astype(bf16)
        return [terms.reshape(chips * span, -1)]
    whole = lambda array: pl.BlockSpec(array.shape, lambda k: (0, 0))
    block = lambda array: pl.BlockSpec((1,) + array.shape[1:], lambda k: (k, 0, 0))
    shape = (span // 2, depth + place.shape[1])
    return pl.pallas_call(
        back_kernel,
        grid=(chips,),
        in_specs=[whole(grad_q), block(up_q), whole(grad_k), whole(grad_v), block(place)],
        out_specs=[pl.BlockSpec(shape, lambda k: (0, 0))] * (2 * chips),
        out_shape=[jax.ShapeDtypeStruct(shape, bf16)] * (2 * chips),
        compiler_params=pltpu.CompilerParams(vmem_limit_bytes=48 << 20),
        cost_estimate=BESIDE,
    )(grad_q, up_q, grad_k, grad_v, place)


def spread_kernel(flip_rows, count, flip_ref, *refs):
    left_refs, weight_ref, out_refs = refs[:count], refs[count], refs[count + 1 :]
    chips, groups, _, own, _ = weight_ref.shape
    depth = groups * own
    columns = []
    for place in range(chips):
        total = 0.0
        for j, left_ref in enumerate(left_refs):
            block = weight_ref[place ^ flip_ref[0], :, j].reshape(depth, weight_ref.shape[4])
            total = total + outer_cols(left_ref[...], block[:, : left_ref.shape[1]])
        columns.append(total.astype(bf16))
    block = pl.program_id(0) ^ flip_ref[0] if flip_rows else pl.program_id(0)
    write_halves(out_refs, block, jnp.concatenate(columns, 1))


def spread(lefts, weight, flip_rows=False):
    chips, groups, _, own, width = weight.shape
    rows, depth = lefts[0].shape[0], chips * groups * own
    if chips != 4 or lefts[0].shape[1] % 128:
        total = sum(
            outer_cols(left, weight[:, :, j].reshape(depth, width)[:, : left.shape[1]])
            for j, left in enumerate(lefts)
        )
        return as_pieces(total.astype(bf16))
    tile = rows // chips
    shape = (tile // 2, depth)
    return pl.pallas_call(
        functools.partial(spread_kernel, flip_rows, len(lefts)),
        grid_spec=pltpu.PrefetchScalarGridSpec(
            num_scalar_prefetch=1,
            grid=(chips,),
            in_specs=[pl.BlockSpec((tile, left.shape[1]), lambda i, f: (i, 0)) for left in lefts]
            + [pl.BlockSpec(weight.shape, lambda i, f: (0, 0, 0, 0, 0))],
            out_specs=[pl.BlockSpec(shape, lambda i, f: (0, 0))] * (2 * chips),
        ),
        out_shape=[jax.ShapeDtypeStruct(shape, bf16)] * (2 * chips),
        compiler_params=pltpu.CompilerParams(vmem_limit_bytes=56 << 20),
        cost_estimate=BESIDE,
    )(chip_flip()[None], *lefts, weight)


def split_kernel(_, small_ref, qup_ref, gate_ref, up_ref, *out_refs):
    chips = len(out_refs) // 3
    own = gate_ref.shape[0]
    for k in range(chips):

        @pl.when(pl.program_id(0) == k)
        def _():
            out_refs[k][...] = small_ref[0]
            out_refs[chips + k][...] = qup_ref[...]
            out_refs[2 * chips + k][:own, :] = gate_ref[...]
            out_refs[2 * chips + k][own:, :] = up_ref[...]


def split_columns(small, w_qup, w_gate, w_up):
    chips = lax.axis_size("chip")
    own, width = w_gate.shape
    width = width // chips
    if chips != 4 or width % 128:
        gate_up = jnp.concatenate([by_columns(w_gate), by_columns(w_up)], 1)
        return list(small), list(by_columns(w_qup)), list(gate_up)
    own_q, q_width = w_qup.shape[0], w_qup.shape[1] // chips
    shapes = [small.shape[1:], (own_q, q_width), (2 * own, width)]
    columns = lambda rows, size: pl.BlockSpec((rows, size), lambda k, f: (0, k ^ f[0]))
    outs = pl.pallas_call(
        split_kernel,
        grid_spec=pltpu.PrefetchScalarGridSpec(
            num_scalar_prefetch=1,
            grid=(chips,),
            in_specs=[
                pl.BlockSpec((1,) + small.shape[1:], lambda k, f: (k ^ f[0], 0, 0)),
                columns(own_q, q_width),
                columns(own, width),
                columns(own, width),
            ],
            out_specs=[
                pl.BlockSpec(shape, lambda k, f: (0, 0)) for shape in shapes for _ in range(chips)
            ],
        ),
        out_shape=[jax.ShapeDtypeStruct(shape, bf16) for shape in shapes for _ in range(chips)],
        cost_estimate=BESIDE,
    )(chip_flip()[None], small, w_qup, w_gate, w_up)
    return outs[:chips], outs[chips : 2 * chips], outs[2 * chips :]


def normed_kernel(flip_ref, *refs):
    *piece_refs, gain_ref, small_ref, normed_ref, raw_ref = refs
    per_step = len(piece_refs) // pl.num_programs(0)
    for k in range(pl.num_programs(0)):

        @pl.when(pl.program_id(0) == k)
        def _():
            pieces = [ref[...] for ref in piece_refs[k * per_step : (k + 1) * per_step]]
            rows = jnp.concatenate(pieces, 0).astype(f32)
            normed = (rows * rms_scale(rows) * gain_ref[...]).astype(bf16)
            normed_ref[...] = normed
            depth = small_ref.shape[1]
            raw = 0.0
            for place in range(small_ref.shape[0]):
                weight = small_ref[place ^ flip_ref[0]][:, : raw_ref.shape[1]]
                columns = normed[:, place * depth : (place + 1) * depth]
                raw = raw + matmul(columns, weight)
            raw_ref[...] = raw


def normed_rows(near, gain, small, width_out):
    chips = lax.axis_size("chip")
    if chips != 4:
        rows = lax.all_gather(near[0], "chip", axis=0, tiled=True).astype(f32)
        normed = (rows * rms_scale(rows) * gain).astype(bf16)
        small = small.reshape(normed.shape[1], -1)[:, :width_out]
        return normed, matmul(normed, small)
    pieces = list(near) + list(far_halves(near))
    half, width = pieces[0].shape
    whole = lambda array: pl.BlockSpec(array.shape, lambda k, f: (0,) * array.ndim)
    block = lambda size: pl.BlockSpec((2 * half, size), lambda k, f: (k ^ f[0], 0))
    gain = gain[None, :]
    rows = chips * 2 * half
    return pl.pallas_call(
        normed_kernel,
        grid_spec=pltpu.PrefetchScalarGridSpec(
            num_scalar_prefetch=1,
            grid=(chips,),
            in_specs=[whole(piece) for piece in pieces] + [whole(gain), whole(small)],
            out_specs=[block(width), block(width_out)],
        ),
        out_shape=[
            jax.ShapeDtypeStruct((rows, width), bf16),
            jax.ShapeDtypeStruct((rows, width_out), f32),
        ],
        compiler_params=pltpu.CompilerParams(vmem_limit_bytes=48 << 20),
        cost_estimate=BESIDE,
    )(chip_flip()[None], *pieces, gain, small)


def gate_terms(gate, up):
    sigma = jax.nn.sigmoid(gate)
    silu = gate * sigma
    return (
        (silu * up).astype(bf16),
        silu.astype(bf16),
        (up * sigma * (1.0 + gate * (1.0 - sigma))).astype(bf16),
    )


def gate_kernel(flip_ref, rows_ref, weight_ref, active_ref, silu_ref, slope_ref):
    chips, groups, _, own, width = weight_ref.shape
    depth = groups * own
    both = 0.0
    for place in range(chips):
        block = weight_ref[place ^ flip_ref[0]]
        block = jnp.concatenate([block[:, j].reshape(depth, width) for j in range(2)], 1)
        both = both + matmul(rows_ref[:, place * depth : (place + 1) * depth], block)
    active_ref[...], silu_ref[...], slope_ref[...] = gate_terms(both[:, :width], both[:, width:])


def gated(rows, gate_up):
    chips, groups, _, own, width = gate_up.shape
    if width % 128:
        gate, up = [gate_up[:, :, j].reshape(rows.shape[1], width) for j in range(2)]
        return gate_terms(matmul(rows, gate), matmul(rows, up))
    out = pl.BlockSpec((rows.shape[0], 128), lambda i, f: (0, i))
    return pl.pallas_call(
        gate_kernel,
        grid_spec=pltpu.PrefetchScalarGridSpec(
            num_scalar_prefetch=1,
            grid=(width // 128,),
            in_specs=[
                pl.BlockSpec(rows.shape, lambda i, f: (0, 0)),
                pl.BlockSpec((chips, groups, 2, own, 128), lambda i, f: (0, 0, 0, 0, i)),
            ],
            out_specs=[out] * 3,
        ),
        out_shape=[jax.ShapeDtypeStruct((rows.shape[0], width), bf16)] * 3,
        compiler_params=pltpu.CompilerParams(vmem_limit_bytes=48 << 20),
        cost_estimate=BESIDE,
    )(chip_flip()[None], rows, gate_up)


def gate_back_kernel(seed_ref, down_ref, silu_ref, slope_ref, gate_ref, up_ref):
    grads = outer_cols(seed_ref[...], down_ref[...])
    gate_ref[...] = (grads * slope_ref[...].astype(f32)).astype(bf16)
    up_ref[...] = (grads * silu_ref[...].astype(f32)).astype(bf16)


def gated_back(seed, down_proj, silu, slope):
    width, depth = down_proj.shape
    if width % 128:
        grads = outer_cols(seed, down_proj)
        return (grads * slope.astype(f32)).astype(bf16), (grads * silu.astype(f32)).astype(bf16)
    rows = lambda size: pl.BlockSpec((TILE, size), lambda i: (i, 0))
    return pl.pallas_call(
        gate_back_kernel,
        grid=(seed.shape[0] // TILE,),
        in_specs=[
            rows(depth),
            pl.BlockSpec(down_proj.shape, lambda i: (0, 0)),
            rows(width),
            rows(width),
        ],
        out_specs=[rows(width)] * 2,
        out_shape=[jax.ShapeDtypeStruct(silu.shape, bf16)] * 2,
        compiler_params=pltpu.CompilerParams(vmem_limit_bytes=48 << 20),
        cost_estimate=BESIDE,
    )(seed, down_proj, silu, slope)


def per_device(
    tokens,
    lengths,
    attn_gain,
    w_qdown,
    q_gain,
    w_qup,
    w_key,
    w_value,
    w_out,
    ffn_gain,
    w_gate,
    w_up,
    w_down,
    cotangent,
):
    slot_count, seq_span, width = tokens.shape[1:]
    assert slot_count == CORES
    chips, dp = lax.axis_size("chip"), lax.axis_size("dp")
    chip, core = lax.axis_index("chip"), lax.axis_index("core")
    devices = chips * CORES * dp
    row_count = CORES * seq_span
    span = chips * row_count
    head_width = w_key.shape[1]
    q_width = w_qdown.shape[1]
    score_scale = 1.0 / math.sqrt(head_width)
    grad_scale = 1.0 / math.sqrt(slot_count * seq_span * devices)

    half = head_width // 2
    own_rows, own_q = attn_gain.shape[0], q_gain.shape[0]
    q_cols, v_cols, k_cols = q_width // chips, head_width // chips, half // chips
    small_cols = q_cols + 2 * v_cols
    length = lengths[0, core]
    positions = chip * row_count + jnp.arange(row_count, dtype=jnp.int32)
    valid_mask = (positions < length).astype(f32)[:, None]
    tokens_own = pair_in(tokens[0])
    inputs = tokens_own.astype(f32)
    flip = chip_flip()[None]

    gains = jnp.stack([attn_gain, ffn_gain, jnp.pad(q_gain, (0, own_rows - own_q))], 1)
    gains = jnp.pad(gains, ((0, 0), (0, 125)))
    key_pairs = w_key.reshape(own_rows, 2, chips, k_cols).transpose(2, 0, 1, 3)
    small = jnp.concatenate(
        [
            by_columns(w_qdown),
            key_pairs.reshape(chips, own_rows, 2 * k_cols),
            by_columns(w_value),
            jnp.broadcast_to(gains, (chips,) + gains.shape),
        ],
        2,
    )
    small, up_q, gate_up = split_columns(small, w_qup, w_gate, w_up)
    tokens_own, small = tie(tokens_own, small)
    tokens_near = gather_near(tokens_own)
    small = gather_columns(small)
    small, w_out, cotangent, tokens_near, gate_up = tie(
        small, w_out, cotangent, tokens_near, gate_up
    )
    up_q, gate_up = gather_columns(up_q), gather_columns(gate_up)
    seed_grad = (pair_in(cotangent[0]).astype(f32) * valid_mask).astype(bf16)
    gains = small.reshape(chips, -1, small.shape[-1])[:, :, small_cols : small_cols + 3]
    gains = jnp.concatenate(reordered(list(gains.astype(f32)), flip[0]), 0)
    gain_one, gain_two = gains[:, 0], gains[:, 1]
    gain_q = gains[:, 2].reshape(devices, own_rows)[:, :own_q].reshape(-1)
    gain_q = lax.dynamic_slice_in_dim(gain_q, chip * q_cols, q_cols, 0)
    out_proj = gather_rows(w_out)
    up_q = up_q.reshape(chips, q_cols, -1)
    gate_up = gate_up.reshape(chips, CORES * dp, 2, own_rows, -1)
    down_proj = gather_rows(w_down)

    cos_all, sin_all = rotary(jnp.arange(span, dtype=jnp.int32), head_width)
    cos_own = lax.dynamic_slice_in_dim(cos_all, chip * k_cols, k_cols, 1)
    sin_own = lax.dynamic_slice_in_dim(sin_all, chip * k_cols, k_cols, 1)
    normed_all, raw = normed_rows(
        tokens_near, gain_one, small.reshape(chips, -1, small.shape[-1]), small_cols
    )
    q_down = raw[:, :q_cols]
    scale_q = lax.rsqrt(row_sums(q_down * q_down) / q_width + epsilon)
    q_normed = (q_down * scale_q * gain_q).astype(bf16)
    k_one, k_two = raw[:, q_cols : q_cols + k_cols], raw[:, q_cols + k_cols : q_cols + 2 * k_cols]
    key_cols = [k_one * cos_own - k_two * sin_own, k_two * cos_own + k_one * sin_own]
    shared = jnp.concatenate(key_cols + [raw[:, q_cols + v_cols :]], 1).astype(bf16)
    shared = gather_chips(jnp.concatenate([q_normed, shared], 1))
    shared, seed_tied = tie(shared, seed_grad)
    seed_near = gather_near(seed_tied)
    shared = shared.reshape(chips, span, small_cols)
    local, sender = jnp.arange(2 * v_cols), (jnp.arange(chips) ^ flip[0])[:, None]
    target = jnp.where(
        local < v_cols,
        local // k_cols * half + sender * k_cols + local % k_cols,
        head_width + sender * v_cols + local - v_cols,
    )
    place = (target[:, :, None] == jnp.arange(2 * head_width)).astype(bf16)
    key_values = jnp.einsum(
        "ksc,kcn->sn", shared[:, :, q_cols:], place, preferred_element_type=f32
    ).astype(bf16)
    keys, values = key_values[:, :head_width], key_values[:, head_width:]

    queries, mixed, log_total = attend(
        length[None], flip, shared, up_q, keys, values, cos_all, sin_all, score_scale
    )
    part, *seed_near = tie(product("nn", (mixed, out_proj), layout="pieces"), *seed_near)
    middle = inputs + scatter_chips(part)
    scale_two = rms_scale(middle)
    normed2 = gather_chips((middle * scale_two * gain_two).astype(bf16))

    normed2, *seed_near = tie(normed2, *seed_near)
    seed_all = gather_far(seed_near)
    activated, silu, slope = gated(normed2, gate_up)
    down_terms = product("tn", (activated, seed_all), scale=grad_scale)
    down_terms, down_proj = tie(down_terms, down_proj)
    down_half = halve_rows(down_terms)
    gate_grad, up_grad = gated_back(seed_all, down_proj, silu, slope)
    gate_tied, up_tied, down_half = tie(gate_grad, up_grad, down_half)
    grad_w_down = scatter_dp(down_half)
    part = spread([gate_tied, up_tied], gate_up)
    part, gate_grad, up_grad = tie(part, gate_grad, up_grad)
    gate_part, up_part = [
        product("tn", (normed2, grad), scale=grad_scale, layout="split")
        for grad in (gate_grad, up_grad)
    ]
    grad_normed2, gate_sum, up_sum = scatter_chips(part, (gate_part, up_part))
    gate_half, up_half = halve_columns(gate_sum), halve_columns(up_sum)
    grad_w_gate = scatter_dp(gate_half)
    grad_normed2, grad_w_down, up_half = tie(grad_normed2, grad_w_down, up_half)
    grad_w_up = scatter_dp(up_half)
    grad_middle = seed_grad.astype(f32) + norm_back(grad_normed2, middle, scale_two, gain_two)
    grad_branch, activated = tie(grad_middle.astype(bf16), activated)
    grad_branch, grad_w_gate, out_part = tie(
        gather_chips(grad_branch), grad_w_gate, product("nn", (activated, down_proj), layout="pieces")
    )
    out_near = scatter_near(out_part)
    grad_mixed = product("nt", (grad_branch, out_proj))
    grad_q, grad_k, grad_v = attend_back(
        length[None], flip, queries, grad_mixed, log_total, keys, values, cos_all, sin_all, score_scale
    )
    grad_q, out_near = tie(grad_q, out_near)
    back = back_terms(grad_q, up_q, grad_k, grad_v, place)
    back, mixed, grad_q = tie(back, mixed, grad_q)
    out_half = halve_rows(product("tn", (mixed, grad_branch), scale=grad_scale))
    back, grad_q, out_half, grad_w_up = scatter_chips(back, (grad_q, out_half, grad_w_up))
    grad_w_out = scatter_dp(out_half)
    q_rows = shared[:, :, :q_cols].transpose(1, 0, 2).reshape(span, q_width)
    qup_half = halve_columns(
        product("tn", (q_rows, grad_q), scale=grad_scale, layout="split", plain=True)
    )
    back, qup_half, out_near = tie(back, qup_half, out_near)
    grad_w_qup = scatter_dp(qup_half)
    weighted = back[:, :q_cols] * gain_q
    mean = row_sums(weighted * q_down) / q_width
    grad_q_down = scale_q * weighted - q_down * scale_q**3 * mean
    k_one, k_two = back[:, q_cols : q_cols + k_cols], back[:, q_cols + k_cols : q_cols + 2 * k_cols]
    back = jnp.concatenate(
        [
            grad_q_down,
            k_one * cos_own + k_two * sin_own,
            k_two * cos_own - k_one * sin_own,
            back[:, q_cols + v_cols :],
        ],
        1,
    ).astype(bf16)
    output = middle + scatter_far(out_near)
    terms, back, grad_w_out, output = tie(
        spread([back], small[:, :, None], flip_rows=True), back, grad_w_out, output
    )
    small_sum = product("tn", (normed_all, back), scale=grad_scale, layout="split")
    grad_normed, small_sum, grad_w_gate, grad_w_up = scatter_chips(
        terms, (small_sum, grad_w_gate, grad_w_up)
    )
    small_half, grad_w_qup = tie(halve_columns(small_sum), grad_w_qup)
    grad_small = scatter_dp(small_half)
    out_tokens = pair_out(output.astype(bf16))[None]
    grad_inputs = grad_middle + norm_back(grad_normed, inputs, rms_scale(inputs), gain_one)
    grad_tokens = pair_out(grad_inputs)[None]
    grad_w_qup = join_columns(grad_w_qup)
    parts = jnp.stack(join_blocks(grad_small), 1).astype(f32)
    grad_w_key = parts[:, :, q_cols : q_cols + v_cols].reshape(own_rows, chips, 2, k_cols)
    grad_w_key = grad_w_key.transpose(0, 2, 1, 3).reshape(own_rows, head_width)
    grad_w_gate, grad_w_up = join_columns(grad_w_gate), join_columns(grad_w_up)
    grad_w_qdown = parts[:, :, :q_cols].reshape(own_rows, q_width)
    grad_w_value = parts[:, :, q_cols + v_cols :].reshape(own_rows, head_width)
    overlap = lambda weight, grad: jnp.sum(weight.astype(f32) * grad, axis=1)
    attn_terms = overlap(w_qdown, grad_w_qdown) + overlap(w_key, grad_w_key)
    attn_terms = attn_terms + overlap(w_value, grad_w_value)
    ffn_terms = overlap(w_gate, grad_w_gate) + overlap(w_up, grad_w_up)
    return (
        out_tokens,
        grad_tokens,
        attn_terms / attn_gain.astype(f32),
        grad_w_qdown,
        overlap(w_qup, grad_w_qup) / q_gain.astype(f32),
        grad_w_qup,
        grad_w_key,
        grad_w_value,
        grad_w_out.astype(f32),
        ffn_terms / ffn_gain.astype(f32),
        grad_w_gate,
        grad_w_up,
        grad_w_down.astype(f32),
    )


def solution(mesh):
    seq, dp = mesh.shape["seq"], mesh.shape["dp"]
    chips = Mesh(
        np.asarray(mesh.devices).reshape(seq // CORES, CORES, dp), ("chip", "core", "dp")
    )
    every = ("chip", "core", "dp")
    rows, vector = P(every, None), P(every)
    block = P("dp", None, ("chip", "core"), None)
    weights = (vector, rows, vector, rows, rows, rows, rows, vector, rows, rows, rows)
    return jax.shard_map(
        per_device,
        mesh=chips,
        in_specs=(block, P("dp", None)) + weights + (block,),
        out_specs=(block, block) + weights,
        check_vma=False,
    )
```

```python
import functools
import math

import jax
import jax.numpy as jnp
import numpy as np
from jax import lax
from jax.experimental import pallas as pl
from jax.experimental.pallas import tpu as pltpu
from jax.sharding import Mesh
from jax.sharding import PartitionSpec as P

epsilon = 1e-06
CORES = 2
TILE = 256
f32, bf16 = jnp.float32, jnp.bfloat16
BESIDE = pl.CostEstimate(flops=1, bytes_accessed=1, transcendentals=0)


def rms_scale(values):
    return lax.rsqrt(jnp.mean(values * values, axis=-1, keepdims=True) + epsilon)


def rotate_half(values):
    half_width = values.shape[-1] // 2
    return jnp.concatenate([-values[..., half_width:], values[..., :half_width]], axis=-1)


def rotary(positions, head_width):
    half_width = head_width // 2
    frequency = jnp.exp(
        jnp.arange(half_width, dtype=f32) * (-2.0 * math.log(10000.0) / head_width)
    )
    angles = positions.astype(f32)[:, None] * frequency[None, :]
    cos_table = jnp.cos(angles)
    sin_table = jnp.sin(angles)
    return (
        jnp.concatenate([cos_table, cos_table], -1),
        jnp.concatenate([sin_table, sin_table], -1),
    )


def matmul(left, right):
    return jnp.dot(left, right, preferred_element_type=f32)


def inner_rows(left, right):
    return lax.dot_general(left, right, (((0,), (0,)), ((), ())), preferred_element_type=f32)


def outer_cols(left, right):
    return lax.dot_general(left, right, (((1,), (1,)), ((), ())), preferred_element_type=f32)


def norm_back(grad_in, inputs, scale_rows, gain):
    weighted = grad_in * gain
    return scale_rows * weighted - inputs * scale_rows**3 * jnp.mean(
        weighted * inputs, axis=-1, keepdims=True
    )


def take(blocks, index):
    return lax.dynamic_index_in_dim(blocks, index, 0, keepdims=False)


def swap_cores(block):
    return lax.ppermute(block, "core", [(0, 1), (1, 0)])


def to_chip(block, bits):
    count = lax.axis_size("chip")
    return lax.ppermute(block, "chip", [(i, i ^ bits) for i in range(count)])


def gather_near(block):
    rows = block.shape[0]
    if lax.axis_size("chip") != 4:
        return (block,)
    top, low = block[: rows // 2], block[rows // 2 :]
    return top, low, to_chip(top, 1), to_chip(low, 1), to_chip(top, 2), to_chip(low, 2)


def join_kernel(*refs):
    *piece_refs, out_ref = refs
    for k, ref in enumerate(piece_refs):

        @pl.when(pl.program_id(0) == k)
        def _():
            out_ref[...] = ref[...]


def join_rows(pieces):
    rows, width = pieces[0].shape
    count = len(pieces)
    if count == 1:
        return pieces[0]
    return pl.pallas_call(
        join_kernel,
        grid=(count,),
        in_specs=[pl.BlockSpec((rows, width), lambda k: (0, 0))] * count,
        out_specs=pl.BlockSpec((rows, width), lambda k: (k, 0)),
        out_shape=jax.ShapeDtypeStruct((count * rows, width), pieces[0].dtype),
        compiler_params=pltpu.CompilerParams(vmem_limit_bytes=24 << 20),
        cost_estimate=BESIDE,
    )(*pieces)


def gather_far(near):
    return join_rows(far_pieces(near))


def far_pieces(near):
    if lax.axis_size("chip") != 4:
        return [lax.all_gather(near[0], "chip", axis=0, tiled=True)]
    return list(near) + [to_chip(near[2], 2), to_chip(near[5], 1)]


def chip_flip():
    return lax.axis_index("chip") if lax.axis_size("chip") == 4 else jnp.int32(0)


def reordered(blocks, flip):
    bits = 1
    while bits < len(blocks):
        swapped = [blocks[k ^ bits] for k in range(len(blocks))]
        blocks = [jnp.where(flip & bits > 0, b, a) for a, b in zip(blocks, swapped)]
        bits *= 2
    return blocks


def gather_chips(block):
    return gather_far(gather_near(block))


def add(left, right):
    return left.astype(f32) + right.astype(f32)


def scatter_near(pieces):
    if lax.axis_size("chip") != 4:
        return tuple(pieces)
    top, low = pieces[::2], pieces[1::2]
    far = (top[2], to_chip(top[3], 1), low[1], to_chip(low[3], 2))
    return far + (top[0], to_chip(top[1], 1), low[0], to_chip(low[2], 2))


def scatter_far(near):
    if lax.axis_size("chip") != 4:
        return lax.psum_scatter(near[0], "chip", scatter_dimension=0, tiled=True).astype(f32)
    top_far, low_far = add(near[0], near[1]).astype(bf16), add(near[2], near[3]).astype(bf16)
    top = add(near[4], near[5]) + to_chip(top_far, 2).astype(f32)
    low = add(near[6], near[7]) + to_chip(low_far, 1).astype(f32)
    return jnp.concatenate([top, low], 0)


def scatter_chips(pieces, beside=()):
    near, beside = tie(scatter_near(pieces), tuple(beside))
    total = scatter_far(near)
    return (total,) + beside if beside else total


def exchange(parts):
    count = lax.axis_size("chip")
    if count != 4:
        blocks = lax.all_to_all(jnp.stack(parts), "chip", 0, 0, tiled=True)
        return [blocks[k] for k in range(count)]
    return [parts[0]] + [to_chip(parts[k], k) for k in range(1, count)]


def tie(*values):
    return lax.optimization_barrier(values)


def by_columns(weight):
    count = lax.axis_size("chip")
    rows, width = weight.shape
    return weight.reshape(rows, count, width // count).transpose(1, 0, 2)


def gather_blocks(blocks):
    mine = jnp.stack(blocks)[:, None]
    return lax.all_gather(mine, ("core", "dp"), axis=1, tiled=True)


def gather_columns(parts):
    return gather_blocks(exchange(parts))


def gather_rows(weight):
    return lax.all_gather(weight, ("core", "dp"), axis=0, tiled=True)


def sum_cores(own, other):
    return add(own, swap_cores(other)).astype(bf16)


def scatter_dp(half):
    half = half.reshape(lax.axis_size("dp"), -1, half.shape[-1])
    return lax.psum_scatter(half, "dp", scatter_dimension=0, tiled=True)


def trade_blocks(mine):
    return exchange(jnp.split(mine.reshape(-1, mine.shape[-1]), lax.axis_size("chip"), 0))


def join_columns(blocks):
    return jnp.concatenate(reordered(blocks, chip_flip()), 1).astype(f32)


def sum_chips(values):
    count, bits = lax.axis_size("chip"), 1
    while bits < count:
        values = values + to_chip(values, bits)
        bits *= 2
    return values


def row_sums(values):
    sums = jnp.sum(values, axis=-1).reshape(-1, 128)
    return sum_chips(sums).reshape(-1, 1)


def pair_in(block):
    me = lax.axis_index("core")
    kept, got = take(block, me), swap_cores(take(block, 1 - me))
    return jnp.where(
        me == 0, jnp.concatenate([kept, got], 0), jnp.concatenate([got, kept], 0)
    )


def pair_out(rows):
    me = lax.axis_index("core")
    blocks = rows.reshape(CORES, -1, rows.shape[1])
    kept, got = take(blocks, me), swap_cores(take(blocks, 1 - me))
    return jnp.where(me == 0, jnp.stack([kept, got]), jnp.stack([got, kept]))


def visible_scores(keys, queries, first, length, score_scale):
    scores = outer_cols(keys, queries) * score_scale
    key_pos = lax.broadcasted_iota(jnp.int32, scores.shape, 0)
    query_pos = lax.broadcasted_iota(jnp.int32, scores.shape, 1) + first
    return jnp.where((key_pos <= query_pos) & (key_pos < length), scores, -1e30)


def flipped(start, flip):
    return pl.ds(pl.multiple_of(((start // TILE) ^ flip) * TILE, TILE), TILE)


def attend_kernel(
    score_scale,
    length_ref,
    flip_ref,
    rows_ref,
    up_ref,
    keys_ref,
    values_t_ref,
    cos_ref,
    sin_ref,
    queries_ref,
    mixed_ref,
    total_ref,
):
    length, flip = length_ref[0], flip_ref[0]
    chips = lax.axis_size("chip")
    depth = up_ref.shape[1]
    for start in range(0, keys_ref.shape[0], TILE):
        stop = start + TILE
        raw = 0.0
        for part in range(chips):
            raw = raw + matmul(rows_ref[part, start:stop, :depth], up_ref[part])
        raw = raw * cos_ref[start:stop, :] + rotate_half(raw) * sin_ref[start:stop, :]
        queries = raw.astype(bf16)
        queries_ref[start:stop, :] = queries
        scores = visible_scores(keys_ref[:stop, :], queries, start, length, score_scale)
        top = jnp.max(scores, axis=0, keepdims=True)
        powers = jnp.exp(scores - top)
        total = jnp.sum(powers, axis=0, keepdims=True)
        total_ref[0, :, start:stop] = top + jnp.log(total)
        probs = (powers * (1.0 / total)).astype(bf16)
        mixed = matmul(values_t_ref[:, :stop], probs)
        mixed_ref[flipped(start, flip), :] = mixed.T.astype(bf16)


def attend(length, flip, rows, up, keys, values, cos_table, sin_table, score_scale):
    span, head_width = keys.shape
    heads = up.shape[2] // head_width
    whole = lambda array: pl.BlockSpec(array.shape, lambda h: (0, 0))
    head = lambda height: pl.BlockSpec((height, head_width), lambda h: (0, h))
    values_t = values.T
    return pl.pallas_call(
        functools.partial(attend_kernel, score_scale),
        grid=(heads,),
        in_specs=[
            pl.BlockSpec(memory_space=pltpu.SMEM),
            pl.BlockSpec(memory_space=pltpu.SMEM),
            pl.BlockSpec(rows.shape, lambda h: (0, 0, 0)),
            pl.BlockSpec(up.shape[:2] + (head_width,), lambda h: (0, 0, h)),
            whole(keys),
            whole(values_t),
            whole(cos_table),
            whole(sin_table),
        ],
        out_specs=[
            head(span),
            head(span),
            pl.BlockSpec((1, 1, span), lambda h: (h, 0, 0)),
        ],
        out_shape=[
            jax.ShapeDtypeStruct((span, heads * head_width), bf16),
            jax.ShapeDtypeStruct((span, heads * head_width), bf16),
            jax.ShapeDtypeStruct((heads, 1, span), f32),
        ],
        compiler_params=pltpu.CompilerParams(vmem_limit_bytes=48 << 20),
        cost_estimate=BESIDE,
    )(length, flip, rows, up, keys, values_t, cos_table, sin_table)


def attend_back_kernel(
    score_scale,
    length_ref,
    flip_ref,
    queries_ref,
    grad_ref,
    total_ref,
    keys_ref,
    keys_t_ref,
    values_ref,
    cos_ref,
    sin_ref,
    grad_q_ref,
    grad_k_ref,
    grad_v_ref,
):
    length, flip = length_ref[0], flip_ref[0]

    @pl.when(pl.program_id(0) == 0)
    def _():
        grad_k_ref[...] = jnp.zeros_like(grad_k_ref)
        grad_v_ref[...] = jnp.zeros_like(grad_v_ref)

    for start in range(0, queries_ref.shape[0], TILE):
        stop = start + TILE
        queries, grads = queries_ref[start:stop, :], grad_ref[flipped(start, flip), :]
        scores = visible_scores(keys_ref[:stop, :], queries, start, length, score_scale)
        probs = jnp.exp(scores - total_ref[0, :, start:stop])
        grad_probs = outer_cols(values_ref[:stop, :], grads)
        mean = jnp.sum(probs * grad_probs, axis=0, keepdims=True)
        grad_scores = (probs * (grad_probs - mean)).astype(bf16)
        grad_v_ref[:stop, :] += matmul(probs.astype(bf16), grads)
        grad_k_ref[:stop, :] += matmul(grad_scores, queries) * score_scale
        grad_q = matmul(keys_t_ref[:, :stop], grad_scores).T * score_scale
        grad_q = grad_q * cos_ref[start:stop, :] - rotate_half(
            grad_q * sin_ref[start:stop, :]
        )
        grad_q_ref[start:stop, :] = grad_q.astype(bf16)


def attend_back(
    length, flip, queries, grads, total, keys, values, cos_table, sin_table, score_scale
):
    span, head_width = keys.shape
    heads = queries.shape[1] // head_width
    whole = lambda array: pl.BlockSpec(array.shape, lambda h: (0, 0))
    head = pl.BlockSpec((span, head_width), lambda h: (0, h))
    keys_t = keys.T
    summed = jax.ShapeDtypeStruct((span, head_width), f32)
    return pl.pallas_call(
        functools.partial(attend_back_kernel, score_scale),
        grid=(heads,),
        in_specs=[
            pl.BlockSpec(memory_space=pltpu.SMEM),
            pl.BlockSpec(memory_space=pltpu.SMEM),
            head,
            head,
            pl.BlockSpec((1, 1, span), lambda h: (h, 0, 0)),
            whole(keys),
            whole(keys_t),
            whole(values),
            whole(cos_table),
            whole(sin_table),
        ],
        out_specs=[head, whole(keys), whole(keys)],
        out_shape=[jax.ShapeDtypeStruct(queries.shape, bf16), summed, summed],
        compiler_params=pltpu.CompilerParams(vmem_limit_bytes=48 << 20),
        cost_estimate=BESIDE,
    )(length, flip, queries, grads, total, keys, keys_t, values, cos_table, sin_table)


CONTRACT = {"nn": ((1,), (0,)), "nt": ((1,), (1,)), "tn": ((0,), (0,))}


def write_halves(out_refs, block, value):
    rows = value.shape[0] // 2
    for k in range(len(out_refs) // 2):

        @pl.when(block == k)
        def _():
            out_refs[2 * k][...] = value[:rows]
            out_refs[2 * k + 1][...] = value[rows:]


def product_kernel(kind, pieces, left_ref, right_ref, *out_refs):
    total = lax.dot_general(
        left_ref[...], right_ref[...], (CONTRACT[kind], ((), ())), preferred_element_type=f32
    ).astype(bf16)
    if pieces:
        write_halves(out_refs, pl.program_id(0), total)
    else:
        out_refs[0][...] = total


def product(kind, left, right, pieces=False):
    rows, width = left.shape[0], right.shape[0] if kind == "nt" else right.shape[1]
    chips = lax.axis_size("chip")
    tile = rows // chips if pieces else TILE
    if (pieces and chips != 4) or rows % tile or tile % 128 or width % 128 or right.shape[0] % 128:
        total = lax.dot_general(
            left, right, (CONTRACT[kind], ((), ())), preferred_element_type=f32
        ).astype(bf16)
        return as_pieces(total) if pieces else total
    if pieces:
        shapes = [(tile // 2, width)] * (2 * chips)
        outs = [pl.BlockSpec(shape, lambda i: (0, 0)) for shape in shapes]
    else:
        shapes = [(rows, width)]
        outs = [pl.BlockSpec((tile, width), lambda i: (i, 0))]
    results = pl.pallas_call(
        functools.partial(product_kernel, kind, pieces),
        grid=(rows // tile,),
        in_specs=[
            pl.BlockSpec((tile, left.shape[1]), lambda i: (i, 0)),
            pl.BlockSpec(right.shape, lambda i: (0, 0)),
        ],
        out_specs=outs,
        out_shape=[jax.ShapeDtypeStruct(shape, bf16) for shape in shapes],
        compiler_params=pltpu.CompilerParams(vmem_limit_bytes=56 << 20),
        cost_estimate=BESIDE,
    )(left, right)
    return results if pieces else results[0]


def terms_kernel(scale, place_ref, left_ref, right_ref, own_ref, other_ref):
    total = lax.dot_general(
        left_ref[...], right_ref[...], (CONTRACT["tn"], ((), ())), preferred_element_type=f32
    )
    total = (total * scale).astype(bf16).reshape(own_ref.shape)

    @pl.when(pl.program_id(0) == 0)
    def _():
        other_ref[...] = total

    @pl.when(pl.program_id(0) == 1)
    def _():
        own_ref[...] = total


def uneven_kernel(scale, place_ref, left_ref, right_ref, own_ref, other_ref, total_ref):
    total = lax.dot_general(
        left_ref[...], right_ref[...], (CONTRACT["tn"], ((), ())), preferred_element_type=f32
    )
    total_ref[...] = (total * scale).astype(bf16)
    half, core = own_ref.shape[0], place_ref[1]
    own_ref[...] = total_ref[pl.ds(pl.multiple_of(core * half, half), half), :]
    other_ref[...] = total_ref[pl.ds(pl.multiple_of((1 - core) * half, half), half), :]


def weight_terms(left, right, scale, flip=None):
    depth, rows = left.shape
    width = right.shape[1]
    chips, dp = lax.axis_size("chip"), lax.axis_size("dp")
    core = lax.axis_index("core")
    own = rows // (CORES * dp) if flip is None else rows // (chips * CORES * dp)
    half = (dp, chips, own, width) if flip is not None else (dp * own, width)
    tile = dp * own if flip is not None else TILE
    steps = rows // CORES // tile
    whole = lambda array: pl.BlockSpec(array.shape, lambda *_: (0, 0))
    place = jnp.stack([jnp.int32(0) if flip is None else flip, core])
    params = dict(
        out_shape=[jax.ShapeDtypeStruct(half, bf16)] * 2,
        compiler_params=pltpu.CompilerParams(vmem_limit_bytes=56 << 20),
        cost_estimate=BESIDE,
    )
    if tile % 128 == 0 and width % 128 == 0 and rows % (CORES * tile) == 0:
        if flip is not None:
            source = lambda j, k, p: (0, k * CORES + (p[1] ^ 1 ^ j))
            block = (dp, 1, own, width)
            target = lambda k, p: (0, k ^ p[0], 0, 0)
        else:
            source = lambda j, k, p: (0, (p[1] ^ 1 ^ j) * steps + k)
            block = (tile, width)
            target = lambda k, p: (k, 0)
        return pl.pallas_call(
            functools.partial(terms_kernel, scale),
            grid_spec=pltpu.PrefetchScalarGridSpec(
                num_scalar_prefetch=1,
                grid=(CORES, steps),
                in_specs=[pl.BlockSpec((depth, tile), source), whole(right)],
                out_specs=[
                    pl.BlockSpec(block, lambda j, k, p: target(jnp.where(j == 1, k, 0), p)),
                    pl.BlockSpec(
                        block, lambda j, k, p: target(jnp.where(j == 0, k, steps - 1), p)
                    ),
                ],
            ),
            **params,
        )(place, left, right)
    if flip is None and rows % 128 == 0 and width % 512 == 0:
        columns = lambda size: pl.BlockSpec((size, 512), lambda i, p: (0, i))
        return pl.pallas_call(
            functools.partial(uneven_kernel, scale),
            grid_spec=pltpu.PrefetchScalarGridSpec(
                num_scalar_prefetch=1,
                grid=(width // 512,),
                in_specs=[whole(left), columns(depth)],
                out_specs=[columns(rows // CORES)] * 2,
                scratch_shapes=[pltpu.VMEM((rows, 512), bf16)],
            ),
            **params,
        )(place, left, right)
    total = (inner_rows(left, right) * scale).astype(bf16)
    if flip is not None:
        total = total.reshape(chips, CORES, dp, own, width).transpose(1, 2, 0, 3, 4)
    else:
        total = total.reshape((CORES,) + half)
    return take(total, core), take(total, 1 - core)


def as_pieces(terms):
    return jnp.split(terms, 8, 0) if lax.axis_size("chip") == 4 else [terms]


def back_kernel(grad_ref, up_ref, grad_k_ref, grad_v_ref, place_ref, *out_refs):
    grads = outer_cols(grad_ref[...], up_ref[0]).astype(bf16)
    parts = jnp.concatenate([grad_k_ref[...], grad_v_ref[...]], 1).astype(bf16)
    parts = outer_cols(parts, place_ref[0]).astype(bf16)
    write_halves(out_refs, pl.program_id(0), jnp.concatenate([grads, parts], 1))


def back_terms(grad_q, up_q, grad_k, grad_v, place):
    chips, depth, width = up_q.shape
    span = grad_q.shape[0]
    if chips != 4:
        grads = jnp.einsum("tn,kin->kti", grad_q, up_q, preferred_element_type=f32)
        parts = jnp.concatenate([grad_k, grad_v], 1).astype(bf16)
        parts = jnp.einsum("sn,kcn->ksc", parts, place, preferred_element_type=f32)
        terms = jnp.concatenate([grads, parts], 2).astype(bf16)
        return [terms.reshape(chips * span, -1)]
    whole = lambda array: pl.BlockSpec(array.shape, lambda k: (0, 0))
    block = lambda array: pl.BlockSpec((1,) + array.shape[1:], lambda k: (k, 0, 0))
    shape = (span // 2, depth + place.shape[1])
    return pl.pallas_call(
        back_kernel,
        grid=(chips,),
        in_specs=[whole(grad_q), block(up_q), whole(grad_k), whole(grad_v), block(place)],
        out_specs=[pl.BlockSpec(shape, lambda k: (0, 0))] * (2 * chips),
        out_shape=[jax.ShapeDtypeStruct(shape, bf16)] * (2 * chips),
        compiler_params=pltpu.CompilerParams(vmem_limit_bytes=48 << 20),
        cost_estimate=BESIDE,
    )(grad_q, up_q, grad_k, grad_v, place)


def spread_kernel(flip_rows, count, own, flip_ref, *refs):
    left_refs, weight_ref, out_refs = refs[:count], refs[count], refs[count + 1 :]
    chips, groups, _, _, width = weight_ref.shape
    depth = groups * own
    columns = []
    for place in range(chips):
        total = 0.0
        for j, left_ref in enumerate(left_refs):
            block = weight_ref[place ^ flip_ref[0], :, j, :own].reshape(depth, width)
            total = total + outer_cols(left_ref[...], block)
        columns.append(total.astype(bf16))
    block = pl.program_id(0) ^ flip_ref[0] if flip_rows else pl.program_id(0)
    write_halves(out_refs, block, jnp.concatenate(columns, 1))


def spread(lefts, weight, own, flip_rows=False):
    chips, groups, _, _, width = weight.shape
    rows, depth = lefts[0].shape[0], chips * groups * own
    if chips != 4 or lefts[0].shape[1] % 128:
        total = sum(
            outer_cols(left, weight[:, :, j, :own].reshape(depth, width))
            for j, left in enumerate(lefts)
        )
        return as_pieces(total.astype(bf16))
    tile = rows // chips
    shape = (tile // 2, depth)
    return pl.pallas_call(
        functools.partial(spread_kernel, flip_rows, len(lefts), own),
        grid_spec=pltpu.PrefetchScalarGridSpec(
            num_scalar_prefetch=1,
            grid=(chips,),
            in_specs=[pl.BlockSpec((tile, left.shape[1]), lambda i, f: (i, 0)) for left in lefts]
            + [pl.BlockSpec(weight.shape, lambda i, f: (0, 0, 0, 0, 0))],
            out_specs=[pl.BlockSpec(shape, lambda i, f: (0, 0))] * (2 * chips),
        ),
        out_shape=[jax.ShapeDtypeStruct(shape, bf16)] * (2 * chips),
        compiler_params=pltpu.CompilerParams(vmem_limit_bytes=56 << 20),
        cost_estimate=BESIDE,
    )(chip_flip()[None], *lefts, weight)


def split_kernel(_, small_ref, qup_ref, gate_ref, up_ref, *out_refs):
    chips = len(out_refs) // 3
    own = gate_ref.shape[0]
    for k in range(chips):

        @pl.when(pl.program_id(0) == k)
        def _():
            out_refs[k][...] = small_ref[0]
            out_refs[chips + k][...] = qup_ref[...]
            out_refs[2 * chips + k][:own, :] = gate_ref[...]
            out_refs[2 * chips + k][own:, :] = up_ref[...]


def split_columns(small, w_qup, w_gate, w_up):
    chips = lax.axis_size("chip")
    own, width = w_gate.shape
    width = width // chips
    if chips != 4 or width % 128:
        gate_up = jnp.concatenate([by_columns(w_gate), by_columns(w_up)], 1)
        return list(small), list(by_columns(w_qup)), list(gate_up)
    own_q, q_width = w_qup.shape[0], w_qup.shape[1] // chips
    shapes = [small.shape[1:], (own_q, q_width), (2 * own, width)]
    columns = lambda rows, size: pl.BlockSpec((rows, size), lambda k, f: (0, k ^ f[0]))
    outs = pl.pallas_call(
        split_kernel,
        grid_spec=pltpu.PrefetchScalarGridSpec(
            num_scalar_prefetch=1,
            grid=(chips,),
            in_specs=[
                pl.BlockSpec((1,) + small.shape[1:], lambda k, f: (k ^ f[0], 0, 0)),
                columns(own_q, q_width),
                columns(own, width),
                columns(own, width),
            ],
            out_specs=[
                pl.BlockSpec(shape, lambda k, f: (0, 0)) for shape in shapes for _ in range(chips)
            ],
        ),
        out_shape=[jax.ShapeDtypeStruct(shape, bf16) for shape in shapes for _ in range(chips)],
        cost_estimate=BESIDE,
    )(chip_flip()[None], small, w_qup, w_gate, w_up)
    return outs[:chips], outs[chips : 2 * chips], outs[2 * chips :]


def normed_kernel(flip_ref, *refs):
    *piece_refs, gain_ref, small_ref, normed_ref, raw_ref = refs
    per_step = len(piece_refs) // pl.num_programs(0)
    for k in range(pl.num_programs(0)):

        @pl.when(pl.program_id(0) == k)
        def _():
            pieces = [ref[...] for ref in piece_refs[k * per_step : (k + 1) * per_step]]
            rows = jnp.concatenate(pieces, 0).astype(f32)
            normed = (rows * rms_scale(rows) * gain_ref[...]).astype(bf16)
            normed_ref[...] = normed
            chips, groups, _, width = small_ref.shape
            depth = normed.shape[1] // chips
            own = depth // groups
            raw = 0.0
            for place in range(chips):
                weight = small_ref[place ^ flip_ref[0], :, :own].reshape(depth, width)
                columns = normed[:, place * depth : (place + 1) * depth]
                raw = raw + matmul(columns, weight)
            raw_ref[...] = raw


def normed_rows(pieces, gain, small, own):
    chips = lax.axis_size("chip")
    if chips != 4:
        rows = pieces[0].astype(f32)
        normed = (rows * rms_scale(rows) * gain).astype(bf16)
        small = small[:, :, :own].reshape(normed.shape[1], -1)
        return normed, matmul(normed, small)
    half, width = pieces[0].shape
    whole = lambda array: pl.BlockSpec(array.shape, lambda k, f: (0,) * array.ndim)
    block = lambda size: pl.BlockSpec((2 * half, size), lambda k, f: (k ^ f[0], 0))
    gain = gain[None, :]
    rows = chips * 2 * half
    return pl.pallas_call(
        normed_kernel,
        grid_spec=pltpu.PrefetchScalarGridSpec(
            num_scalar_prefetch=1,
            grid=(chips,),
            in_specs=[whole(piece) for piece in pieces] + [whole(gain), whole(small)],
            out_specs=[block(width), block(small.shape[-1])],
        ),
        out_shape=[
            jax.ShapeDtypeStruct((rows, width), bf16),
            jax.ShapeDtypeStruct((rows, small.shape[-1]), f32),
        ],
        compiler_params=pltpu.CompilerParams(vmem_limit_bytes=48 << 20),
        cost_estimate=BESIDE,
    )(chip_flip()[None], *pieces, gain, small)


def gate_terms(gate, up):
    sigma = jax.nn.sigmoid(gate)
    silu = gate * sigma
    return (
        (silu * up).astype(bf16),
        silu.astype(bf16),
        (up * sigma * (1.0 + gate * (1.0 - sigma))).astype(bf16),
    )


def gate_kernel(flip_ref, rows_ref, weight_ref, active_ref, silu_ref, slope_ref):
    chips, groups, _, own, width = weight_ref.shape
    depth = groups * own
    both = 0.0
    for place in range(chips):
        block = weight_ref[place ^ flip_ref[0]]
        block = jnp.concatenate([block[:, j].reshape(depth, width) for j in range(2)], 1)
        both = both + matmul(rows_ref[:, place * depth : (place + 1) * depth], block)
    active_ref[...], silu_ref[...], slope_ref[...] = gate_terms(both[:, :width], both[:, width:])


def gated(rows, gate_up):
    chips, groups, _, own, width = gate_up.shape
    if width % 128:
        gate, up = [gate_up[:, :, j].reshape(rows.shape[1], width) for j in range(2)]
        return gate_terms(matmul(rows, gate), matmul(rows, up))
    out = pl.BlockSpec((rows.shape[0], 128), lambda i, f: (0, i))
    return pl.pallas_call(
        gate_kernel,
        grid_spec=pltpu.PrefetchScalarGridSpec(
            num_scalar_prefetch=1,
            grid=(width // 128,),
            in_specs=[
                pl.BlockSpec(rows.shape, lambda i, f: (0, 0)),
                pl.BlockSpec((chips, groups, 2, own, 128), lambda i, f: (0, 0, 0, 0, i)),
            ],
            out_specs=[out] * 3,
        ),
        out_shape=[jax.ShapeDtypeStruct((rows.shape[0], width), bf16)] * 3,
        compiler_params=pltpu.CompilerParams(vmem_limit_bytes=48 << 20),
        cost_estimate=BESIDE,
    )(chip_flip()[None], rows, gate_up)


def gate_back_kernel(seed_ref, down_ref, silu_ref, slope_ref, gate_ref, up_ref):
    grads = outer_cols(seed_ref[...], down_ref[...])
    gate_ref[...] = (grads * slope_ref[...].astype(f32)).astype(bf16)
    up_ref[...] = (grads * silu_ref[...].astype(f32)).astype(bf16)


def gated_back(seed, down_proj, silu, slope):
    width, depth = down_proj.shape
    if width % 128:
        grads = outer_cols(seed, down_proj)
        return (grads * slope.astype(f32)).astype(bf16), (grads * silu.astype(f32)).astype(bf16)
    rows = lambda size: pl.BlockSpec((TILE, size), lambda i: (i, 0))
    return pl.pallas_call(
        gate_back_kernel,
        grid=(seed.shape[0] // TILE,),
        in_specs=[
            rows(depth),
            pl.BlockSpec(down_proj.shape, lambda i: (0, 0)),
            rows(width),
            rows(width),
        ],
        out_specs=[rows(width)] * 2,
        out_shape=[jax.ShapeDtypeStruct(silu.shape, bf16)] * 2,
        compiler_params=pltpu.CompilerParams(vmem_limit_bytes=48 << 20),
        cost_estimate=BESIDE,
    )(seed, down_proj, silu, slope)


def per_device(
    tokens,
    lengths,
    attn_gain,
    w_qdown,
    q_gain,
    w_qup,
    w_key,
    w_value,
    w_out,
    ffn_gain,
    w_gate,
    w_up,
    w_down,
    cotangent,
):
    slot_count, seq_span, width = tokens.shape[1:]
    assert slot_count == CORES
    chips, dp = lax.axis_size("chip"), lax.axis_size("dp")
    chip, core = lax.axis_index("chip"), lax.axis_index("core")
    devices = chips * CORES * dp
    row_count = CORES * seq_span
    span = chips * row_count
    head_width = w_key.shape[1]
    q_width = w_qdown.shape[1]
    down_shape = w_down.shape
    score_scale = 1.0 / math.sqrt(head_width)
    grad_scale = 1.0 / math.sqrt(slot_count * seq_span * devices)

    half = head_width // 2
    own_rows, own_q = attn_gain.shape[0], q_gain.shape[0]
    q_cols, v_cols, k_cols = q_width // chips, head_width // chips, half // chips
    small_cols = q_cols + 2 * v_cols
    length = lengths[0, core]
    positions = chip * row_count + jnp.arange(row_count, dtype=jnp.int32)
    valid_mask = (positions < length).astype(f32)[:, None]
    tokens_own = pair_in(tokens[0])
    inputs = tokens_own.astype(f32)
    flip = chip_flip()[None]

    key_pairs = w_key.reshape(own_rows, 2, chips, k_cols).transpose(2, 0, 1, 3)
    small = jnp.concatenate(
        [
            by_columns(w_qdown),
            key_pairs.reshape(chips, own_rows, 2 * k_cols),
            by_columns(w_value),
        ],
        2,
    )
    gains = [jnp.pad(gain, (0, small_cols - gain.shape[0])) for gain in (attn_gain, ffn_gain, q_gain)]
    gains = jnp.pad(jnp.stack(gains), ((0, 13), (0, 0)))
    small = jnp.concatenate([small, jnp.broadcast_to(gains, (chips,) + gains.shape)], 1)
    small, up_q, gate_up = split_columns(small, w_qup, w_gate, w_up)
    tokens_own, small = tie(tokens_own, small)
    tokens_near = gather_near(tokens_own)
    cos_all, sin_all = rotary(jnp.arange(span, dtype=jnp.int32), head_width)
    cos_own = lax.dynamic_slice_in_dim(cos_all, chip * k_cols, k_cols, 1)
    sin_own = lax.dynamic_slice_in_dim(sin_all, chip * k_cols, k_cols, 1)
    out_proj, small, tokens_near, tables = tie(
        gather_rows(w_out), exchange(small), tokens_near, (cos_all, sin_all, cos_own, sin_own)
    )
    cos_all, sin_all, cos_own, sin_own = tables
    small = gather_blocks(small)
    tokens_pieces, up_q, gate_up = tie(far_pieces(tokens_near), up_q, gate_up)
    up_q = gather_columns(up_q)
    small, cotangent, gate_up = tie(small, cotangent, gate_up)
    seed_grad = (pair_in(cotangent[0]).astype(f32) * valid_mask).astype(bf16)
    gains = small[:, :, own_rows : own_rows + 3].astype(f32)
    gains = jnp.stack(reordered(list(gains), flip[0]))
    gain_one = gains[:, :, 0, :own_rows].reshape(-1)
    gain_two = gains[:, :, 1, :own_rows].reshape(-1)
    gain_q = gains[:, :, 2, :own_q].reshape(chips, -1)[chip]
    up_q = up_q.reshape(chips, q_cols, -1)

    normed_all, raw = normed_rows(
        tokens_pieces, gain_one, small, own_rows
    )
    raw, gate_up = tie(raw, exchange(gate_up))
    gate_up = gather_blocks(gate_up)
    down_proj = gather_rows(w_down)
    gate_up = gate_up.reshape(chips, CORES * dp, 2, own_rows, -1)
    q_down = raw[:, :q_cols]
    scale_q = lax.rsqrt(row_sums(q_down * q_down) / q_width + epsilon)
    q_normed = (q_down * scale_q * gain_q).astype(bf16)
    k_one, k_two = raw[:, q_cols : q_cols + k_cols], raw[:, q_cols + k_cols : q_cols + 2 * k_cols]
    key_cols = [k_one * cos_own - k_two * sin_own, k_two * cos_own + k_one * sin_own]
    shared = jnp.concatenate(key_cols + [raw[:, q_cols + v_cols :]], 1).astype(bf16)
    shared = gather_chips(jnp.concatenate([q_normed, shared], 1))
    shared, seed_tied = tie(shared, seed_grad)
    seed_near = gather_near(seed_tied)
    shared = shared.reshape(chips, span, small_cols)
    local, sender = jnp.arange(2 * v_cols), (jnp.arange(chips) ^ flip[0])[:, None]
    target = jnp.where(
        local < v_cols,
        local // k_cols * half + sender * k_cols + local % k_cols,
        head_width + sender * v_cols + local - v_cols,
    )
    place = (target[:, :, None] == jnp.arange(2 * head_width)).astype(bf16)
    key_values = jnp.einsum(
        "ksc,kcn->sn", shared[:, :, q_cols:], place, preferred_element_type=f32
    ).astype(bf16)
    keys, values = key_values[:, :head_width], key_values[:, head_width:]

    queries, mixed, log_total = attend(
        length[None], flip, shared, up_q, keys, values, cos_all, sin_all, score_scale
    )
    part, *seed_near = tie(product("nn", mixed, out_proj, pieces=True), *seed_near)
    middle = inputs + scatter_chips(part)
    scale_two = rms_scale(middle)
    normed2 = gather_chips((middle * scale_two * gain_two).astype(bf16))

    normed2, *seed_near = tie(normed2, *seed_near)
    activated, silu, slope = gated(normed2, gate_up)
    activated, seed_pieces = tie(activated, far_pieces(seed_near))
    seed_all = join_rows(seed_pieces)
    down_terms = weight_terms(activated, seed_all, grad_scale)
    down_terms, down_proj = tie(down_terms, down_proj)
    down_half = sum_cores(*down_terms)
    gate_grad, up_grad = gated_back(seed_all, down_proj, silu, slope)
    gate_grad, up_grad, down_half = tie(gate_grad, up_grad, down_half)
    grad_w_down = scatter_dp(down_half)
    gate_part = weight_terms(normed2, gate_grad, grad_scale, flip[0])
    gate_tied, up_tied, gate_part = tie(gate_grad, up_grad, gate_part)
    part = spread([gate_tied, up_tied], gate_up, own_rows)
    part, up_grad, gate_half = tie(part, up_grad, sum_cores(*gate_part))
    grad_w_gate = scatter_dp(gate_half)
    up_part = weight_terms(normed2, up_grad, grad_scale, flip[0])
    grad_normed2, up_part = scatter_chips(part, (up_part,))
    up_half = sum_cores(*up_part)
    grad_normed2, grad_w_down, up_half = tie(grad_normed2, grad_w_down, up_half)
    grad_w_up = scatter_dp(up_half)
    grad_middle = seed_grad.astype(f32) + norm_back(grad_normed2, middle, scale_two, gain_two)
    grad_branch, activated = tie(grad_middle.astype(bf16), activated)
    q_rows = shared[:, :, :q_cols].transpose(1, 0, 2).reshape(span, q_width)
    grad_branch, out_part, q_rows = tie(
        gather_chips(grad_branch), product("nn", activated, down_proj, pieces=True), q_rows
    )
    out_near = scatter_near(out_part)
    out_terms = weight_terms(mixed, grad_branch, grad_scale)
    out_terms, grad_branch, grad_w_gate = tie(out_terms, grad_branch, grad_w_gate)
    grad_mixed, out_half = tie(product("nt", grad_branch, out_proj), sum_cores(*out_terms))
    grad_w_out = scatter_dp(out_half)
    grad_q, grad_k, grad_v = attend_back(
        length[None], flip, queries, grad_mixed, log_total, keys, values, cos_all, sin_all, score_scale
    )
    grad_q, out_near = tie(grad_q, out_near)
    output = middle + scatter_far(out_near)
    back, grad_q = tie(back_terms(grad_q, up_q, grad_k, grad_v, place), grad_q)
    qup_part = weight_terms(q_rows, grad_q, grad_scale, jnp.int32(0))
    back, qup_part, grad_w_up, output = scatter_chips(back, (qup_part, grad_w_up, output))
    back, qup_half = tie(back, sum_cores(*qup_part))
    grad_w_qup = scatter_dp(qup_half)
    weighted = back[:, :q_cols] * gain_q
    mean = row_sums(weighted * q_down) / q_width
    pair = jnp.concatenate([grad_w_gate, grad_w_up], 2)
    mean, pair = tie(mean, pair)
    pair = trade_blocks(pair)
    grad_q_down = scale_q * weighted - q_down * scale_q**3 * mean
    k_one, k_two = back[:, q_cols : q_cols + k_cols], back[:, q_cols + k_cols : q_cols + 2 * k_cols]
    back = jnp.concatenate(
        [
            grad_q_down,
            k_one * cos_own + k_two * sin_own,
            k_two * cos_own - k_one * sin_own,
            back[:, q_cols + v_cols :],
        ],
        1,
    ).astype(bf16)
    small_half = sum_cores(*weight_terms(normed_all, back, grad_scale, flip[0]))
    back, small_half, grad_w_out = tie(back, small_half, grad_w_out)
    grad_small = scatter_dp(small_half)
    terms = spread([back], small[:, :, None], own_rows, flip_rows=True)
    grad_normed, pair, grad_w_qup = scatter_chips(terms, (pair, grad_w_qup))
    grad_w_qup = trade_blocks(grad_w_qup)
    grad_normed, grad_small = tie(grad_normed, grad_small)
    out_tokens = pair_out(output.astype(bf16))[None]
    grad_inputs = grad_middle + norm_back(grad_normed, inputs, rms_scale(inputs), gain_one)
    grad_tokens = pair_out(grad_inputs)[None]
    grad_w_qup = join_columns(grad_w_qup)
    parts = jnp.stack(reordered(trade_blocks(grad_small), flip[0]), 1).astype(f32)
    grad_w_key = parts[:, :, q_cols : q_cols + v_cols].reshape(own_rows, chips, 2, k_cols)
    grad_w_key = grad_w_key.transpose(0, 2, 1, 3).reshape(own_rows, head_width)
    pairs = [jnp.split(block, 2, 1) for block in pair]
    grad_w_gate, grad_w_up = [join_columns([pair[j] for pair in pairs]) for j in range(2)]
    grad_w_qdown = parts[:, :, :q_cols].reshape(own_rows, q_width)
    grad_w_value = parts[:, :, q_cols + v_cols :].reshape(own_rows, head_width)
    overlap = lambda weight, grad: jnp.sum(weight.astype(f32) * grad, axis=1)
    attn_terms = overlap(w_qdown, grad_w_qdown) + overlap(w_key, grad_w_key)
    attn_terms = attn_terms + overlap(w_value, grad_w_value)
    ffn_terms = overlap(w_gate, grad_w_gate) + overlap(w_up, grad_w_up)
    return (
        out_tokens,
        grad_tokens,
        attn_terms / attn_gain.astype(f32),
        grad_w_qdown,
        overlap(w_qup, grad_w_qup) / q_gain.astype(f32),
        grad_w_qup,
        grad_w_key,
        grad_w_value,
        grad_w_out.astype(f32).reshape(w_out.shape),
        ffn_terms / ffn_gain.astype(f32),
        grad_w_gate,
        grad_w_up,
        grad_w_down.astype(f32).reshape(down_shape),
    )


def solution(mesh):
    seq, dp = mesh.shape["seq"], mesh.shape["dp"]
    chips = Mesh(
        np.asarray(mesh.devices).reshape(seq // CORES, CORES, dp), ("chip", "core", "dp")
    )
    every = ("chip", "core", "dp")
    rows, vector = P(every, None), P(every)
    block = P("dp", None, ("chip", "core"), None)
    weights = (vector, rows, vector, rows, rows, rows, rows, vector, rows, rows, rows)
    return jax.shard_map(
        per_device,
        mesh=chips,
        in_specs=(block, P("dp", None)) + weights + (block,),
        out_specs=(block, block) + weights,
        check_vma=False,
    )
```

```python
import functools
import math

import jax
import jax.numpy as jnp
import numpy as np
from jax import lax
from jax.experimental import pallas as pl
from jax.experimental.pallas import tpu as pltpu
from jax.sharding import Mesh
from jax.sharding import PartitionSpec as P

epsilon = 1e-06
CORES = 2
TILE = 256
f32, bf16 = jnp.float32, jnp.bfloat16
BESIDE = pl.CostEstimate(flops=1, bytes_accessed=1, transcendentals=0)


def rms_scale(values):
    return lax.rsqrt(jnp.mean(values * values, axis=-1, keepdims=True) + epsilon)


def rotate_half(values):
    half_width = values.shape[-1] // 2
    return jnp.concatenate([-values[..., half_width:], values[..., :half_width]], axis=-1)


def rotary(positions, head_width):
    half_width = head_width // 2
    frequency = jnp.exp(
        jnp.arange(half_width, dtype=f32) * (-2.0 * math.log(10000.0) / head_width)
    )
    angles = positions.astype(f32)[:, None] * frequency[None, :]
    cos_table = jnp.cos(angles)
    sin_table = jnp.sin(angles)
    return (
        jnp.concatenate([cos_table, cos_table], -1),
        jnp.concatenate([sin_table, sin_table], -1),
    )


def matmul(left, right):
    return jnp.dot(left, right, preferred_element_type=f32)


def inner_rows(left, right):
    return lax.dot_general(left, right, (((0,), (0,)), ((), ())), preferred_element_type=f32)


def outer_cols(left, right):
    return lax.dot_general(left, right, (((1,), (1,)), ((), ())), preferred_element_type=f32)


def norm_back(grad_in, inputs, scale_rows, gain):
    weighted = grad_in * gain
    return scale_rows * weighted - inputs * scale_rows**3 * jnp.mean(
        weighted * inputs, axis=-1, keepdims=True
    )


def take(blocks, index):
    return lax.dynamic_index_in_dim(blocks, index, 0, keepdims=False)


def swap_cores(block):
    return lax.ppermute(block, "core", [(0, 1), (1, 0)])


def to_chip(block, bits):
    count = lax.axis_size("chip")
    return lax.ppermute(block, "chip", [(i, i ^ bits) for i in range(count)])


def gather_near(block):
    rows = block.shape[0]
    if lax.axis_size("chip") != 4:
        return (block,)
    top, low = block[: rows // 2], block[rows // 2 :]
    return top, low, to_chip(top, 1), to_chip(low, 1), to_chip(top, 2), to_chip(low, 2)


def join_kernel(*refs):
    *piece_refs, out_ref = refs
    for k, ref in enumerate(piece_refs):

        @pl.when(pl.program_id(0) == k)
        def _():
            out_ref[...] = ref[...]


def join_rows(pieces):
    rows, width = pieces[0].shape
    count = len(pieces)
    if count == 1:
        return pieces[0]
    return pl.pallas_call(
        join_kernel,
        grid=(count,),
        in_specs=[pl.BlockSpec((rows, width), lambda k: (0, 0))] * count,
        out_specs=pl.BlockSpec((rows, width), lambda k: (k, 0)),
        out_shape=jax.ShapeDtypeStruct((count * rows, width), pieces[0].dtype),
        compiler_params=pltpu.CompilerParams(vmem_limit_bytes=24 << 20),
        cost_estimate=BESIDE,
    )(*pieces)


def gather_far(near):
    return join_rows(far_pieces(near))


def far_pieces(near):
    if lax.axis_size("chip") != 4:
        return [lax.all_gather(near[0], "chip", axis=0, tiled=True)]
    return list(near) + [to_chip(near[2], 2), to_chip(near[5], 1)]


def chip_flip():
    return lax.axis_index("chip") if lax.axis_size("chip") == 4 else jnp.int32(0)


def reordered(blocks, flip):
    bits = 1
    while bits < len(blocks):
        swapped = [blocks[k ^ bits] for k in range(len(blocks))]
        blocks = [jnp.where(flip & bits > 0, b, a) for a, b in zip(blocks, swapped)]
        bits *= 2
    return blocks


def gather_chips(block):
    return gather_far(gather_near(block))


def add(left, right):
    return left.astype(f32) + right.astype(f32)


def scatter_near(pieces):
    if lax.axis_size("chip") != 4:
        return tuple(pieces)
    top, low = pieces[::2], pieces[1::2]
    far = (top[2], to_chip(top[3], 1), low[1], to_chip(low[3], 2))
    return far + (top[0], to_chip(top[1], 1), low[0], to_chip(low[2], 2))


def scatter_far(near):
    if lax.axis_size("chip") != 4:
        return lax.psum_scatter(near[0], "chip", scatter_dimension=0, tiled=True).astype(f32)
    top_far, low_far = add(near[0], near[1]).astype(bf16), add(near[2], near[3]).astype(bf16)
    top = add(near[4], near[5]) + to_chip(top_far, 2).astype(f32)
    low = add(near[6], near[7]) + to_chip(low_far, 1).astype(f32)
    return jnp.concatenate([top, low], 0)


def scatter_chips(pieces, beside=()):
    near, beside = tie(scatter_near(pieces), tuple(beside))
    total = scatter_far(near)
    return (total,) + beside if beside else total


def exchange(parts):
    count = lax.axis_size("chip")
    if count != 4:
        blocks = lax.all_to_all(jnp.stack(parts), "chip", 0, 0, tiled=True)
        return [blocks[k] for k in range(count)]
    return [parts[0]] + [to_chip(parts[k], k) for k in range(1, count)]


def tie(*values):
    return lax.optimization_barrier(values)


def by_columns(weight):
    count = lax.axis_size("chip")
    rows, width = weight.shape
    return weight.reshape(rows, count, width // count).transpose(1, 0, 2)


def gather_blocks(blocks):
    mine = jnp.stack(blocks)[:, None]
    return lax.all_gather(mine, ("core", "dp"), axis=1, tiled=True)


def gather_columns(parts):
    return gather_blocks(exchange(parts))


def gather_rows(weight):
    return lax.all_gather(weight, ("core", "dp"), axis=0, tiled=True)


def sum_cores(own, other):
    return add(own, swap_cores(other)).astype(bf16)


def scatter_dp(half):
    half = half.reshape(lax.axis_size("dp"), -1, half.shape[-1])
    return lax.psum_scatter(half, "dp", scatter_dimension=0, tiled=True)


def trade_blocks(mine):
    return exchange(jnp.split(mine.reshape(-1, mine.shape[-1]), lax.axis_size("chip"), 0))


def join_columns(blocks):
    return jnp.concatenate(reordered(blocks, chip_flip()), 1).astype(f32)


def sum_chips(values):
    count, bits = lax.axis_size("chip"), 1
    while bits < count:
        values = values + to_chip(values, bits)
        bits *= 2
    return values


def row_sums(values):
    sums = jnp.sum(values, axis=-1).reshape(-1, 128)
    return sum_chips(sums).reshape(-1, 1)


def pair_in(block):
    me = lax.axis_index("core")
    kept, got = take(block, me), swap_cores(take(block, 1 - me))
    return jnp.where(
        me == 0, jnp.concatenate([kept, got], 0), jnp.concatenate([got, kept], 0)
    )


def pair_out(rows):
    me = lax.axis_index("core")
    blocks = rows.reshape(CORES, -1, rows.shape[1])
    kept, got = take(blocks, me), swap_cores(take(blocks, 1 - me))
    return jnp.where(me == 0, jnp.stack([kept, got]), jnp.stack([got, kept]))


def visible_scores(keys, queries, first, length, score_scale):
    scores = outer_cols(keys, queries) * score_scale
    key_pos = lax.broadcasted_iota(jnp.int32, scores.shape, 0)
    query_pos = lax.broadcasted_iota(jnp.int32, scores.shape, 1) + first
    return jnp.where((key_pos <= query_pos) & (key_pos < length), scores, -1e30)


def flipped(start, flip):
    return pl.ds(pl.multiple_of(((start // TILE) ^ flip) * TILE, TILE), TILE)


def attend_kernel(
    score_scale,
    length_ref,
    flip_ref,
    rows_ref,
    up_ref,
    keys_ref,
    values_t_ref,
    cos_ref,
    sin_ref,
    queries_ref,
    mixed_ref,
    total_ref,
):
    length, flip = length_ref[0], flip_ref[0]
    chips = lax.axis_size("chip")
    depth = up_ref.shape[1]
    for start in range(0, keys_ref.shape[0], TILE):
        stop = start + TILE
        raw = 0.0
        for part in range(chips):
            raw = raw + matmul(rows_ref[part, start:stop, :depth], up_ref[part])
        raw = raw * cos_ref[start:stop, :] + rotate_half(raw) * sin_ref[start:stop, :]
        queries = raw.astype(bf16)
        queries_ref[start:stop, :] = queries
        scores = visible_scores(keys_ref[:stop, :], queries, start, length, score_scale)
        top = jnp.max(scores, axis=0, keepdims=True)
        powers = jnp.exp(scores - top)
        total = jnp.sum(powers, axis=0, keepdims=True)
        total_ref[0, :, start:stop] = top + jnp.log(total)
        probs = (powers * (1.0 / total)).astype(bf16)
        mixed = matmul(values_t_ref[:, :stop], probs)
        mixed_ref[flipped(start, flip), :] = mixed.T.astype(bf16)


def attend(length, flip, rows, up, keys, values, cos_table, sin_table, score_scale):
    span, head_width = keys.shape
    heads = up.shape[2] // head_width
    whole = lambda array: pl.BlockSpec(array.shape, lambda h: (0, 0))
    head = lambda height: pl.BlockSpec((height, head_width), lambda h: (0, h))
    values_t = values.T
    return pl.pallas_call(
        functools.partial(attend_kernel, score_scale),
        grid=(heads,),
        in_specs=[
            pl.BlockSpec(memory_space=pltpu.SMEM),
            pl.BlockSpec(memory_space=pltpu.SMEM),
            pl.BlockSpec(rows.shape, lambda h: (0, 0, 0)),
            pl.BlockSpec(up.shape[:2] + (head_width,), lambda h: (0, 0, h)),
            whole(keys),
            whole(values_t),
            whole(cos_table),
            whole(sin_table),
        ],
        out_specs=[
            head(span),
            head(span),
            pl.BlockSpec((1, 1, span), lambda h: (h, 0, 0)),
        ],
        out_shape=[
            jax.ShapeDtypeStruct((span, heads * head_width), bf16),
            jax.ShapeDtypeStruct((span, heads * head_width), bf16),
            jax.ShapeDtypeStruct((heads, 1, span), f32),
        ],
        compiler_params=pltpu.CompilerParams(vmem_limit_bytes=62 << 20),
        cost_estimate=BESIDE,
    )(length, flip, rows, up, keys, values_t, cos_table, sin_table)


def attend_back_kernel(
    score_scale,
    length_ref,
    flip_ref,
    queries_ref,
    grad_ref,
    total_ref,
    keys_ref,
    keys_t_ref,
    values_ref,
    cos_ref,
    sin_ref,
    grad_q_ref,
    grad_k_ref,
    grad_v_ref,
):
    length, flip = length_ref[0], flip_ref[0]

    @pl.when(pl.program_id(0) == 0)
    def _():
        grad_k_ref[...] = jnp.zeros_like(grad_k_ref)
        grad_v_ref[...] = jnp.zeros_like(grad_v_ref)

    for start in range(0, queries_ref.shape[0], TILE):
        stop = start + TILE
        queries, grads = queries_ref[start:stop, :], grad_ref[flipped(start, flip), :]
        scores = visible_scores(keys_ref[:stop, :], queries, start, length, score_scale)
        probs = jnp.exp(scores - total_ref[0, :, start:stop])
        grad_probs = outer_cols(values_ref[:stop, :], grads)
        mean = jnp.sum(probs * grad_probs, axis=0, keepdims=True)
        grad_scores = (probs * (grad_probs - mean)).astype(bf16)
        grad_v_ref[:stop, :] += matmul(probs.astype(bf16), grads)
        grad_k_ref[:stop, :] += matmul(grad_scores, queries) * score_scale
        grad_q = matmul(keys_t_ref[:, :stop], grad_scores).T * score_scale
        grad_q = grad_q * cos_ref[start:stop, :] - rotate_half(
            grad_q * sin_ref[start:stop, :]
        )
        grad_q_ref[start:stop, :] = grad_q.astype(bf16)


def attend_back(
    length, flip, queries, grads, total, keys, values, cos_table, sin_table, score_scale
):
    span, head_width = keys.shape
    heads = queries.shape[1] // head_width
    whole = lambda array: pl.BlockSpec(array.shape, lambda h: (0, 0))
    head = pl.BlockSpec((span, head_width), lambda h: (0, h))
    keys_t = keys.T
    summed = jax.ShapeDtypeStruct((span, head_width), f32)
    return pl.pallas_call(
        functools.partial(attend_back_kernel, score_scale),
        grid=(heads,),
        in_specs=[
            pl.BlockSpec(memory_space=pltpu.SMEM),
            pl.BlockSpec(memory_space=pltpu.SMEM),
            head,
            head,
            pl.BlockSpec((1, 1, span), lambda h: (h, 0, 0)),
            whole(keys),
            whole(keys_t),
            whole(values),
            whole(cos_table),
            whole(sin_table),
        ],
        out_specs=[head, whole(keys), whole(keys)],
        out_shape=[jax.ShapeDtypeStruct(queries.shape, bf16), summed, summed],
        compiler_params=pltpu.CompilerParams(vmem_limit_bytes=62 << 20),
        cost_estimate=BESIDE,
    )(length, flip, queries, grads, total, keys, keys_t, values, cos_table, sin_table)


CONTRACT = {"nn": ((1,), (0,)), "nt": ((1,), (1,)), "tn": ((0,), (0,))}


def write_halves(out_refs, block, value):
    rows = value.shape[0] // 2
    for k in range(len(out_refs) // 2):

        @pl.when(block == k)
        def _():
            out_refs[2 * k][...] = value[:rows]
            out_refs[2 * k + 1][...] = value[rows:]


def product_kernel(kind, pieces, left_ref, right_ref, *out_refs):
    total = lax.dot_general(
        left_ref[...], right_ref[...], (CONTRACT[kind], ((), ())), preferred_element_type=f32
    ).astype(bf16)
    if pieces:
        write_halves(out_refs, pl.program_id(0), total)
    else:
        out_refs[0][...] = total


def product(kind, left, right, pieces=False):
    rows, width = left.shape[0], right.shape[0] if kind == "nt" else right.shape[1]
    chips = lax.axis_size("chip")
    tile = rows // chips if pieces else TILE
    if (pieces and chips != 4) or rows % tile or tile % 128 or width % 128 or right.shape[0] % 128:
        total = lax.dot_general(
            left, right, (CONTRACT[kind], ((), ())), preferred_element_type=f32
        ).astype(bf16)
        return as_pieces(total) if pieces else total
    if pieces:
        shapes = [(tile // 2, width)] * (2 * chips)
        outs = [pl.BlockSpec(shape, lambda i: (0, 0)) for shape in shapes]
    else:
        shapes = [(rows, width)]
        outs = [pl.BlockSpec((tile, width), lambda i: (i, 0))]
    results = pl.pallas_call(
        functools.partial(product_kernel, kind, pieces),
        grid=(rows // tile,),
        in_specs=[
            pl.BlockSpec((tile, left.shape[1]), lambda i: (i, 0)),
            pl.BlockSpec(right.shape, lambda i: (0, 0)),
        ],
        out_specs=outs,
        out_shape=[jax.ShapeDtypeStruct(shape, bf16) for shape in shapes],
        compiler_params=pltpu.CompilerParams(vmem_limit_bytes=56 << 20),
        cost_estimate=BESIDE,
    )(left, right)
    return results if pieces else results[0]


def terms_kernel(scale, place_ref, left_ref, right_ref, own_ref, other_ref):
    total = lax.dot_general(
        left_ref[...], right_ref[...], (CONTRACT["tn"], ((), ())), preferred_element_type=f32
    )
    total = (total * scale).astype(bf16).reshape(own_ref.shape)

    @pl.when(pl.program_id(0) == 0)
    def _():
        other_ref[...] = total

    @pl.when(pl.program_id(0) == 1)
    def _():
        own_ref[...] = total


def uneven_kernel(scale, place_ref, left_ref, right_ref, own_ref, other_ref, total_ref):
    total = lax.dot_general(
        left_ref[...], right_ref[...], (CONTRACT["tn"], ((), ())), preferred_element_type=f32
    )
    total_ref[...] = (total * scale).astype(bf16)
    half, core = own_ref.shape[0], place_ref[1]
    own_ref[...] = total_ref[pl.ds(pl.multiple_of(core * half, half), half), :]
    other_ref[...] = total_ref[pl.ds(pl.multiple_of((1 - core) * half, half), half), :]


def weight_terms(left, right, scale, flip=None):
    depth, rows = left.shape
    width = right.shape[1]
    chips, dp = lax.axis_size("chip"), lax.axis_size("dp")
    core = lax.axis_index("core")
    own = rows // (CORES * dp) if flip is None else rows // (chips * CORES * dp)
    half = (dp, chips, own, width) if flip is not None else (dp * own, width)
    tile = dp * own if flip is not None else TILE
    steps = rows // CORES // tile
    whole = lambda array: pl.BlockSpec(array.shape, lambda *_: (0, 0))
    place = jnp.stack([jnp.int32(0) if flip is None else flip, core])
    params = dict(
        out_shape=[jax.ShapeDtypeStruct(half, bf16)] * 2,
        compiler_params=pltpu.CompilerParams(vmem_limit_bytes=56 << 20),
        cost_estimate=BESIDE,
    )
    if tile % 128 == 0 and width % 128 == 0 and rows % (CORES * tile) == 0:
        if flip is not None:
            source = lambda j, k, p: (0, k * CORES + (p[1] ^ 1 ^ j))
            block = (dp, 1, own, width)
            target = lambda k, p: (0, k ^ p[0], 0, 0)
        else:
            source = lambda j, k, p: (0, (p[1] ^ 1 ^ j) * steps + k)
            block = (tile, width)
            target = lambda k, p: (k, 0)
        return pl.pallas_call(
            functools.partial(terms_kernel, scale),
            grid_spec=pltpu.PrefetchScalarGridSpec(
                num_scalar_prefetch=1,
                grid=(CORES, steps),
                in_specs=[pl.BlockSpec((depth, tile), source), whole(right)],
                out_specs=[
                    pl.BlockSpec(block, lambda j, k, p: target(jnp.where(j == 1, k, 0), p)),
                    pl.BlockSpec(
                        block, lambda j, k, p: target(jnp.where(j == 0, k, steps - 1), p)
                    ),
                ],
            ),
            **params,
        )(place, left, right)
    if flip is None and rows % 128 == 0 and width % 512 == 0:
        columns = lambda size: pl.BlockSpec((size, 512), lambda i, p: (0, i))
        return pl.pallas_call(
            functools.partial(uneven_kernel, scale),
            grid_spec=pltpu.PrefetchScalarGridSpec(
                num_scalar_prefetch=1,
                grid=(width // 512,),
                in_specs=[whole(left), columns(depth)],
                out_specs=[columns(rows // CORES)] * 2,
                scratch_shapes=[pltpu.VMEM((rows, 512), bf16)],
            ),
            **params,
        )(place, left, right)
    total = (inner_rows(left, right) * scale).astype(bf16)
    if flip is not None:
        total = total.reshape(chips, CORES, dp, own, width).transpose(1, 2, 0, 3, 4)
    else:
        total = total.reshape((CORES,) + half)
    return take(total, core), take(total, 1 - core)


def as_pieces(terms):
    return jnp.split(terms, 8, 0) if lax.axis_size("chip") == 4 else [terms]


def back_kernel(grad_ref, up_ref, grad_k_ref, grad_v_ref, place_ref, *out_refs):
    grads = outer_cols(grad_ref[...], up_ref[0]).astype(bf16)
    parts = jnp.concatenate([grad_k_ref[...], grad_v_ref[...]], 1).astype(bf16)
    parts = outer_cols(parts, place_ref[0]).astype(bf16)
    write_halves(out_refs, pl.program_id(0), jnp.concatenate([grads, parts], 1))


def back_terms(grad_q, up_q, grad_k, grad_v, place):
    chips, depth, width = up_q.shape
    span = grad_q.shape[0]
    if chips != 4:
        grads = jnp.einsum("tn,kin->kti", grad_q, up_q, preferred_element_type=f32)
        parts = jnp.concatenate([grad_k, grad_v], 1).astype(bf16)
        parts = jnp.einsum("sn,kcn->ksc", parts, place, preferred_element_type=f32)
        terms = jnp.concatenate([grads, parts], 2).astype(bf16)
        return [terms.reshape(chips * span, -1)]
    whole = lambda array: pl.BlockSpec(array.shape, lambda k: (0, 0))
    block = lambda array: pl.BlockSpec((1,) + array.shape[1:], lambda k: (k, 0, 0))
    shape = (span // 2, depth + place.shape[1])
    return pl.pallas_call(
        back_kernel,
        grid=(chips,),
        in_specs=[whole(grad_q), block(up_q), whole(grad_k), whole(grad_v), block(place)],
        out_specs=[pl.BlockSpec(shape, lambda k: (0, 0))] * (2 * chips),
        out_shape=[jax.ShapeDtypeStruct(shape, bf16)] * (2 * chips),
        compiler_params=pltpu.CompilerParams(vmem_limit_bytes=48 << 20),
        cost_estimate=BESIDE,
    )(grad_q, up_q, grad_k, grad_v, place)


def spread_kernel(flip_rows, count, own, flip_ref, *refs):
    left_refs, weight_ref, out_refs = refs[:count], refs[count], refs[count + 1 :]
    chips, groups, _, _, width = weight_ref.shape
    depth = groups * own
    columns = []
    for place in range(chips):
        total = 0.0
        for j, left_ref in enumerate(left_refs):
            block = weight_ref[place ^ flip_ref[0], :, j, :own].reshape(depth, width)
            total = total + outer_cols(left_ref[...], block)
        columns.append(total.astype(bf16))
    block = pl.program_id(0) ^ flip_ref[0] if flip_rows else pl.program_id(0)
    write_halves(out_refs, block, jnp.concatenate(columns, 1))


def spread(lefts, weight, own, flip_rows=False):
    chips, groups, _, _, width = weight.shape
    rows, depth = lefts[0].shape[0], chips * groups * own
    if chips != 4 or lefts[0].shape[1] % 128:
        total = sum(
            outer_cols(left, weight[:, :, j, :own].reshape(depth, width))
            for j, left in enumerate(lefts)
        )
        return as_pieces(total.astype(bf16))
    tile = rows // chips
    shape = (tile // 2, depth)
    return pl.pallas_call(
        functools.partial(spread_kernel, flip_rows, len(lefts), own),
        grid_spec=pltpu.PrefetchScalarGridSpec(
            num_scalar_prefetch=1,
            grid=(chips,),
            in_specs=[pl.BlockSpec((tile, left.shape[1]), lambda i, f: (i, 0)) for left in lefts]
            + [pl.BlockSpec(weight.shape, lambda i, f: (0, 0, 0, 0, 0))],
            out_specs=[pl.BlockSpec(shape, lambda i, f: (0, 0))] * (2 * chips),
        ),
        out_shape=[jax.ShapeDtypeStruct(shape, bf16)] * (2 * chips),
        compiler_params=pltpu.CompilerParams(vmem_limit_bytes=56 << 20),
        cost_estimate=BESIDE,
    )(chip_flip()[None], *lefts, weight)


def whole_kernel(own, place_ref, *refs):
    *left_refs, mine_ref, other_ref, out_ref = refs
    chips = len(left_refs)
    groups, width = mine_ref.shape[2], mine_ref.shape[4]
    half = chips // CORES
    total = 0.0
    for k in range(chips):
        block = pl.program_id(0) ^ k ^ place_ref[0]
        mine = mine_ref[k, block % half, :, :own].reshape(groups * own, width)
        other = other_ref[k, block % half, :, :own].reshape(groups * own, width)
        weight = jnp.where(block // half == place_ref[1], mine, other)
        total = total + outer_cols(left_refs[k][...], weight)
    out_ref[...] = total


def whole_products(lefts, mine, other, weights, own):
    chips = len(lefts)
    rows = lefts[0].shape[0]
    if chips != 4:
        every = lax.all_gather(weights[:, :, :own], "chip", axis=0)
        return sum(
            outer_cols(lefts[k], every[k].reshape(-1, every.shape[-1])) for k in range(chips)
        )
    depth = mine.shape[2] * own
    whole = lambda array: pl.BlockSpec(array.shape, lambda i, p: (0,) * array.ndim)
    return pl.pallas_call(
        functools.partial(whole_kernel, own),
        grid_spec=pltpu.PrefetchScalarGridSpec(
            num_scalar_prefetch=1,
            grid=(chips,),
            in_specs=[whole(left) for left in lefts] + [whole(mine), whole(other)],
            out_specs=pl.BlockSpec((rows, depth), lambda i, p: (0, i)),
        ),
        out_shape=jax.ShapeDtypeStruct((rows, chips * depth), f32),
        compiler_params=pltpu.CompilerParams(vmem_limit_bytes=48 << 20),
        cost_estimate=BESIDE,
    )(jnp.stack([chip_flip(), lax.axis_index("core")]), *lefts, mine, other)


def split_kernel(_, small_ref, qup_ref, gate_ref, up_ref, *out_refs):
    chips = len(out_refs) // 3
    own = gate_ref.shape[0]
    for k in range(chips):

        @pl.when(pl.program_id(0) == k)
        def _():
            out_refs[k][...] = small_ref[0]
            out_refs[chips + k][...] = qup_ref[...]
            out_refs[2 * chips + k][:own, :] = gate_ref[...]
            out_refs[2 * chips + k][own:, :] = up_ref[...]


def split_columns(small, w_qup, w_gate, w_up):
    chips = lax.axis_size("chip")
    own, width = w_gate.shape
    width = width // chips
    if chips != 4 or width % 128:
        gate_up = jnp.concatenate([by_columns(w_gate), by_columns(w_up)], 1)
        return list(small), list(by_columns(w_qup)), list(gate_up)
    own_q, q_width = w_qup.shape[0], w_qup.shape[1] // chips
    shapes = [small.shape[1:], (own_q, q_width), (2 * own, width)]
    columns = lambda rows, size: pl.BlockSpec((rows, size), lambda k, f: (0, k ^ f[0]))
    outs = pl.pallas_call(
        split_kernel,
        grid_spec=pltpu.PrefetchScalarGridSpec(
            num_scalar_prefetch=1,
            grid=(chips,),
            in_specs=[
                pl.BlockSpec((1,) + small.shape[1:], lambda k, f: (k ^ f[0], 0, 0)),
                columns(own_q, q_width),
                columns(own, width),
                columns(own, width),
            ],
            out_specs=[
                pl.BlockSpec(shape, lambda k, f: (0, 0)) for shape in shapes for _ in range(chips)
            ],
        ),
        out_shape=[jax.ShapeDtypeStruct(shape, bf16) for shape in shapes for _ in range(chips)],
        cost_estimate=BESIDE,
    )(chip_flip()[None], small, w_qup, w_gate, w_up)
    return outs[:chips], outs[chips : 2 * chips], outs[2 * chips :]


def normed_kernel(flip_ref, *refs):
    *piece_refs, gain_ref, small_ref, normed_ref, query_ref, pair_ref = refs
    per_step = len(piece_refs) // pl.num_programs(0)
    for k in range(pl.num_programs(0)):

        @pl.when(pl.program_id(0) == k)
        def _():
            pieces = [ref[...] for ref in piece_refs[k * per_step : (k + 1) * per_step]]
            rows = jnp.concatenate(pieces, 0).astype(f32)
            normed = (rows * rms_scale(rows) * gain_ref[...]).astype(bf16)
            normed_ref[...] = normed
            chips, groups, _, width = small_ref.shape
            depth = normed.shape[1] // chips
            own = depth // groups
            raw = 0.0
            for place in range(chips):
                weight = small_ref[place ^ flip_ref[0], :, :own].reshape(depth, width)
                columns = normed[:, place * depth : (place + 1) * depth]
                raw = raw + matmul(columns, weight)
            split = query_ref.shape[1]
            query_ref[...], pair_ref[...] = raw[:, :split], raw[:, split:]


def normed_rows(pieces, gain, small, own, split):
    chips = lax.axis_size("chip")
    if chips != 4:
        rows = pieces[0].astype(f32)
        normed = (rows * rms_scale(rows) * gain).astype(bf16)
        small = small[:, :, :own].reshape(normed.shape[1], -1)
        raw = matmul(normed, small)
        return normed, raw[:, :split], raw[:, split:]
    half, width = pieces[0].shape
    whole = lambda array: pl.BlockSpec(array.shape, lambda k, f: (0,) * array.ndim)
    block = lambda size: pl.BlockSpec((2 * half, size), lambda k, f: (k ^ f[0], 0))
    gain = gain[None, :]
    rows = chips * 2 * half
    return pl.pallas_call(
        normed_kernel,
        grid_spec=pltpu.PrefetchScalarGridSpec(
            num_scalar_prefetch=1,
            grid=(chips,),
            in_specs=[whole(piece) for piece in pieces] + [whole(gain), whole(small)],
            out_specs=[block(width), block(split), block(small.shape[-1] - split)],
        ),
        out_shape=[
            jax.ShapeDtypeStruct((rows, width), bf16),
            jax.ShapeDtypeStruct((rows, split), f32),
            jax.ShapeDtypeStruct((rows, small.shape[-1] - split), f32),
        ],
        compiler_params=pltpu.CompilerParams(vmem_limit_bytes=62 << 20),
        cost_estimate=BESIDE,
    )(chip_flip()[None], *pieces, gain, small)


def gate_terms(gate, up):
    sigma = jax.nn.sigmoid(gate)
    silu = gate * sigma
    return (
        (silu * up).astype(bf16),
        silu.astype(bf16),
        (up * sigma * (1.0 + gate * (1.0 - sigma))).astype(bf16),
    )


def gate_kernel(flip_ref, rows_ref, weight_ref, active_ref, silu_ref, slope_ref):
    chips, groups, _, own, width = weight_ref.shape
    depth = groups * own
    both = 0.0
    for place in range(chips):
        block = weight_ref[place ^ flip_ref[0]]
        block = jnp.concatenate([block[:, j].reshape(depth, width) for j in range(2)], 1)
        both = both + matmul(rows_ref[:, place * depth : (place + 1) * depth], block)
    active_ref[...], silu_ref[...], slope_ref[...] = gate_terms(both[:, :width], both[:, width:])


def gated(rows, gate_up):
    chips, groups, _, own, width = gate_up.shape
    if width % 128:
        gate, up = [gate_up[:, :, j].reshape(rows.shape[1], width) for j in range(2)]
        return gate_terms(matmul(rows, gate), matmul(rows, up))
    out = pl.BlockSpec((rows.shape[0], 128), lambda i, f: (0, i))
    return pl.pallas_call(
        gate_kernel,
        grid_spec=pltpu.PrefetchScalarGridSpec(
            num_scalar_prefetch=1,
            grid=(width // 128,),
            in_specs=[
                pl.BlockSpec(rows.shape, lambda i, f: (0, 0)),
                pl.BlockSpec((chips, groups, 2, own, 128), lambda i, f: (0, 0, 0, 0, i)),
            ],
            out_specs=[out] * 3,
        ),
        out_shape=[jax.ShapeDtypeStruct((rows.shape[0], width), bf16)] * 3,
        compiler_params=pltpu.CompilerParams(vmem_limit_bytes=48 << 20),
        cost_estimate=BESIDE,
    )(chip_flip()[None], rows, gate_up)


def gate_back_kernel(seed_ref, down_ref, silu_ref, slope_ref, gate_ref, up_ref):
    grads = outer_cols(seed_ref[...], down_ref[...])
    gate_ref[...] = (grads * slope_ref[...].astype(f32)).astype(bf16)
    up_ref[...] = (grads * silu_ref[...].astype(f32)).astype(bf16)


def gated_back(seed, down_proj, silu, slope):
    width, depth = down_proj.shape
    if width % 128:
        grads = outer_cols(seed, down_proj)
        return (grads * slope.astype(f32)).astype(bf16), (grads * silu.astype(f32)).astype(bf16)
    rows = lambda size: pl.BlockSpec((TILE, size), lambda i: (i, 0))
    return pl.pallas_call(
        gate_back_kernel,
        grid=(seed.shape[0] // TILE,),
        in_specs=[
            rows(depth),
            pl.BlockSpec(down_proj.shape, lambda i: (0, 0)),
            rows(width),
            rows(width),
        ],
        out_specs=[rows(width)] * 2,
        out_shape=[jax.ShapeDtypeStruct(silu.shape, bf16)] * 2,
        compiler_params=pltpu.CompilerParams(vmem_limit_bytes=48 << 20),
        cost_estimate=BESIDE,
    )(seed, down_proj, silu, slope)


def per_device(
    tokens,
    lengths,
    attn_gain,
    w_qdown,
    q_gain,
    w_qup,
    w_key,
    w_value,
    w_out,
    ffn_gain,
    w_gate,
    w_up,
    w_down,
    cotangent,
):
    slot_count, seq_span, width = tokens.shape[1:]
    assert slot_count == CORES
    chips, dp = lax.axis_size("chip"), lax.axis_size("dp")
    chip, core = lax.axis_index("chip"), lax.axis_index("core")
    devices = chips * CORES * dp
    row_count = CORES * seq_span
    span = chips * row_count
    head_width = w_key.shape[1]
    q_width = w_qdown.shape[1]
    down_shape = w_down.shape
    score_scale = 1.0 / math.sqrt(head_width)
    grad_scale = 1.0 / math.sqrt(slot_count * seq_span * devices)

    half = head_width // 2
    own_rows, own_q = attn_gain.shape[0], q_gain.shape[0]
    q_cols, v_cols, k_cols = q_width // chips, head_width // chips, half // chips
    small_cols = q_cols + 2 * v_cols
    length = lengths[0, core]
    positions = chip * row_count + jnp.arange(row_count, dtype=jnp.int32)
    valid_mask = (positions < length).astype(f32)[:, None]
    tokens_own = pair_in(tokens[0])
    inputs = tokens_own.astype(f32)
    flip = chip_flip()[None]

    key_pairs = w_key.reshape(own_rows, 2, chips, k_cols).transpose(2, 0, 1, 3)
    small = jnp.concatenate(
        [
            by_columns(w_qdown),
            key_pairs.reshape(chips, own_rows, 2 * k_cols),
            by_columns(w_value),
        ],
        2,
    )
    gains = [jnp.pad(gain, (0, small_cols - gain.shape[0])) for gain in (attn_gain, ffn_gain, q_gain)]
    gains = jnp.pad(jnp.stack(gains), ((0, 13), (0, 0)))
    small = jnp.concatenate([small, jnp.broadcast_to(gains, (chips,) + gains.shape)], 1)
    small, up_q, gate_up = split_columns(small, w_qup, w_gate, w_up)
    tokens_own, small = tie(tokens_own, small)
    tokens_near = gather_near(tokens_own)
    cos_all, sin_all = rotary(jnp.arange(span, dtype=jnp.int32), head_width)
    cos_own = lax.dynamic_slice_in_dim(cos_all, chip * k_cols, k_cols, 1)
    sin_own = lax.dynamic_slice_in_dim(sin_all, chip * k_cols, k_cols, 1)
    out_proj, small, tokens_near, tables = tie(
        gather_rows(w_out), exchange(small), tokens_near, (cos_all, sin_all, cos_own, sin_own)
    )
    cos_all, sin_all, cos_own, sin_own = tables
    small = gather_blocks(small)
    tokens_pieces, up_q, gate_up = tie(far_pieces(tokens_near), up_q, gate_up)
    up_q = gather_columns(up_q)
    small, cotangent = tie(small, cotangent)
    seed_grad = (pair_in(cotangent[0]).astype(f32) * valid_mask).astype(bf16)
    gains = small[:, :, own_rows : own_rows + 3].astype(f32)
    gains = jnp.stack(reordered(list(gains), flip[0]))
    gain_one = gains[:, :, 0, :own_rows].reshape(-1)
    gain_two = gains[:, :, 1, :own_rows].reshape(-1)
    gain_q = gains[:, :, 2, :own_q].reshape(chips, -1)[chip]
    up_q = up_q.reshape(chips, q_cols, -1)

    normed_all, q_down, kv_raw = normed_rows(
        tokens_pieces, gain_one, small, own_rows, q_cols
    )
    q_down, kv_raw, gate_up = tie(q_down, kv_raw, exchange(gate_up))
    scale_q = lax.rsqrt(row_sums(q_down * q_down) / q_width + epsilon)
    gate_up = gather_blocks(gate_up)
    down_proj = gather_rows(w_down)
    gate_up = gate_up.reshape(chips, CORES * dp, 2, own_rows, -1)
    q_normed = (q_down * scale_q * gain_q).astype(bf16)
    k_one, k_two = kv_raw[:, :k_cols], kv_raw[:, k_cols:v_cols]
    key_cols = [k_one * cos_own - k_two * sin_own, k_two * cos_own + k_one * sin_own]
    shared = jnp.concatenate(key_cols + [kv_raw[:, v_cols:]], 1).astype(bf16)
    shared = gather_chips(jnp.concatenate([q_normed, shared], 1))
    shared, seed_tied = tie(shared, seed_grad)
    seed_near = gather_near(seed_tied)
    shared = shared.reshape(chips, span, small_cols)
    local, sender = jnp.arange(2 * v_cols), (jnp.arange(chips) ^ flip[0])[:, None]
    target = jnp.where(
        local < v_cols,
        local // k_cols * half + sender * k_cols + local % k_cols,
        head_width + sender * v_cols + local - v_cols,
    )
    place = (target[:, :, None] == jnp.arange(2 * head_width)).astype(bf16)
    key_values = jnp.einsum(
        "ksc,kcn->sn", shared[:, :, q_cols:], place, preferred_element_type=f32
    ).astype(bf16)
    keys, values = key_values[:, :head_width], key_values[:, head_width:]

    queries, mixed, log_total = attend(
        length[None], flip, shared, up_q, keys, values, cos_all, sin_all, score_scale
    )
    part, *seed_near = tie(product("nn", mixed, out_proj, pieces=True), *seed_near)
    middle = inputs + scatter_chips(part)
    scale_two = rms_scale(middle)
    normed2 = gather_chips((middle * scale_two * gain_two).astype(bf16))

    small_rows = small.reshape(CORES, -1, small_cols)
    small_rows = take(small_rows, core) if chips == 4 else small_rows[0]
    normed2, seed_near = tie(normed2, seed_near)
    activated, silu, slope = gated(normed2, gate_up)
    activated, seed_pieces = tie(activated, far_pieces(seed_near))
    seed_all = join_rows(seed_pieces)
    down_terms = weight_terms(activated, seed_all, grad_scale)
    down_terms, down_proj = tie(down_terms, down_proj)
    down_half = sum_cores(*down_terms)
    gate_grad, up_grad = gated_back(seed_all, down_proj, silu, slope)
    gate_grad, up_grad, down_half, small_rows = tie(gate_grad, up_grad, down_half, small_rows)
    small_near = gather_near(small_rows) if chips == 4 else (small_rows,)
    grad_w_down = scatter_dp(down_half)
    part, gate_grad, up_grad = tie(
        spread([gate_grad, up_grad], gate_up, own_rows), gate_grad, up_grad
    )
    gate_part = weight_terms(normed2, gate_grad, grad_scale, flip[0])
    up_part = weight_terms(normed2, up_grad, grad_scale, flip[0])
    part, small_near = tie(part, small_near)
    near, gate_part, up_part = tie(scatter_near(part), gate_part, up_part)
    near, gate_half = tie(near, sum_cores(*gate_part))
    grad_w_gate = scatter_dp(gate_half)
    grad_normed2, up_half = scatter_far(near), sum_cores(*up_part)
    grad_normed2, grad_w_down, up_half = tie(grad_normed2, grad_w_down, up_half)
    grad_w_up = scatter_dp(up_half)
    grad_middle = seed_grad.astype(f32) + norm_back(grad_normed2, middle, scale_two, gain_two)
    grad_branch, activated = tie(grad_middle.astype(bf16), activated)
    q_rows = shared[:, :, :q_cols].transpose(1, 0, 2).reshape(span, q_width)
    grad_branch, out_part, q_rows = tie(
        gather_chips(grad_branch), product("nn", activated, down_proj, pieces=True), q_rows
    )
    out_near = scatter_near(out_part)
    out_terms = weight_terms(mixed, grad_branch, grad_scale)
    out_terms, grad_branch, grad_w_gate = tie(out_terms, grad_branch, grad_w_gate)
    grad_mixed, out_half, small_near = tie(
        product("nt", grad_branch, out_proj), sum_cores(*out_terms), small_near
    )
    small_pieces = far_pieces(small_near) if chips == 4 else list(small_near)
    grad_w_out = scatter_dp(out_half)
    grad_q, grad_k, grad_v = attend_back(
        length[None], flip, queries, grad_mixed, log_total, keys, values, cos_all, sin_all, score_scale
    )
    grad_q, out_near, small_pieces = tie(grad_q, out_near, small_pieces)
    output = middle + scatter_far(out_near)
    back, grad_q = tie(back_terms(grad_q, up_q, grad_k, grad_v, place), grad_q)
    qup_part = weight_terms(q_rows, grad_q, grad_scale, jnp.int32(0))
    back, qup_part, grad_w_up, output, small_pieces = scatter_chips(
        back, (qup_part, grad_w_up, output, small_pieces)
    )
    back, qup_half, grad_w_out = tie(back, sum_cores(*qup_part), grad_w_out)
    grad_w_qup = scatter_dp(qup_half)
    weighted = back[:, :q_cols] * gain_q
    mean = row_sums(weighted * q_down) / q_width
    pair = jnp.concatenate([grad_w_gate, grad_w_up], 2)
    mean, pair = tie(mean, pair)
    pair = trade_blocks(pair)
    grad_q_down = scale_q * weighted - q_down * scale_q**3 * mean
    k_one, k_two = back[:, q_cols : q_cols + k_cols], back[:, q_cols + k_cols : q_cols + 2 * k_cols]
    back = jnp.concatenate(
        [
            grad_q_down,
            k_one * cos_own + k_two * sin_own,
            k_two * cos_own - k_one * sin_own,
            back[:, q_cols + v_cols :],
        ],
        1,
    ).astype(bf16)
    small_mine = join_rows(small_pieces)
    small_other = swap_cores(small_mine)
    back_parts = exchange(reordered(jnp.split(back, chips, 0), flip[0]))
    small_part = weight_terms(normed_all, back, grad_scale, flip[0])
    back_parts, small_part, small_pair = tie(back_parts, small_part, (small_mine, small_other))
    small_half = sum_cores(*small_part)
    grad_small = scatter_dp(small_half)
    if chips == 4:
        shape = (chips, -1, CORES * dp, small.shape[2], small_cols)
        small_pair = [array.reshape(shape) for array in small_pair]
    grad_normed = whole_products(back_parts, *small_pair, small, own_rows)
    grad_normed, grad_w_qup = tie(grad_normed, grad_w_qup)
    grad_w_qup, pair = tie(trade_blocks(grad_w_qup), pair)
    out_tokens = pair_out(output.astype(bf16))[None]
    grad_inputs = grad_middle + norm_back(grad_normed, inputs, rms_scale(inputs), gain_one)
    grad_tokens = pair_out(grad_inputs)[None]
    grad_w_qup = join_columns(grad_w_qup)
    parts = jnp.stack(reordered(trade_blocks(grad_small), flip[0]), 1).astype(f32)
    grad_w_key = parts[:, :, q_cols : q_cols + v_cols].reshape(own_rows, chips, 2, k_cols)
    grad_w_key = grad_w_key.transpose(0, 2, 1, 3).reshape(own_rows, head_width)
    pairs = [jnp.split(block, 2, 1) for block in pair]
    grad_w_gate, grad_w_up = [join_columns([pair[j] for pair in pairs]) for j in range(2)]
    grad_w_qdown = parts[:, :, :q_cols].reshape(own_rows, q_width)
    grad_w_value = parts[:, :, q_cols + v_cols :].reshape(own_rows, head_width)
    overlap = lambda weight, grad: jnp.sum(weight.astype(f32) * grad, axis=1)
    attn_terms = overlap(w_qdown, grad_w_qdown) + overlap(w_key, grad_w_key)
    attn_terms = attn_terms + overlap(w_value, grad_w_value)
    ffn_terms = overlap(w_gate, grad_w_gate) + overlap(w_up, grad_w_up)
    return (
        out_tokens,
        grad_tokens,
        attn_terms / attn_gain.astype(f32),
        grad_w_qdown,
        overlap(w_qup, grad_w_qup) / q_gain.astype(f32),
        grad_w_qup,
        grad_w_key,
        grad_w_value,
        grad_w_out.astype(f32).reshape(w_out.shape),
        ffn_terms / ffn_gain.astype(f32),
        grad_w_gate,
        grad_w_up,
        grad_w_down.astype(f32).reshape(down_shape),
    )


def solution(mesh):
    seq, dp = mesh.shape["seq"], mesh.shape["dp"]
    chips = Mesh(
        np.asarray(mesh.devices).reshape(seq // CORES, CORES, dp), ("chip", "core", "dp")
    )
    every = ("chip", "core", "dp")
    rows, vector = P(every, None), P(every)
    block = P("dp", None, ("chip", "core"), None)
    weights = (vector, rows, vector, rows, rows, rows, rows, vector, rows, rows, rows)
    return jax.shard_map(
        per_device,
        mesh=chips,
        in_specs=(block, P("dp", None)) + weights + (block,),
        out_specs=(block, block) + weights,
        check_vma=False,
    )
```

```python
import functools
import math

import jax
import jax.numpy as jnp
import numpy as np
from jax import lax
from jax.experimental import pallas as pl
from jax.experimental.pallas import tpu as pltpu
from jax.sharding import Mesh
from jax.sharding import PartitionSpec as P

epsilon = 1e-06
CORES = 2
TILE = 256
f32, bf16 = jnp.float32, jnp.bfloat16
BESIDE = pl.CostEstimate(flops=1, bytes_accessed=1, transcendentals=0)


def rms_scale(values):
    return lax.rsqrt(jnp.mean(values * values, axis=-1, keepdims=True) + epsilon)


def rotate_half(values):
    half_width = values.shape[-1] // 2
    return jnp.concatenate([-values[..., half_width:], values[..., :half_width]], axis=-1)


def rotary(positions, head_width):
    half_width = head_width // 2
    frequency = jnp.exp(
        jnp.arange(half_width, dtype=f32) * (-2.0 * math.log(10000.0) / head_width)
    )
    angles = positions.astype(f32)[:, None] * frequency[None, :]
    cos_table = jnp.cos(angles)
    sin_table = jnp.sin(angles)
    return (
        jnp.concatenate([cos_table, cos_table], -1),
        jnp.concatenate([sin_table, sin_table], -1),
    )


def matmul(left, right):
    return jnp.dot(left, right, preferred_element_type=f32)


def inner_rows(left, right):
    return lax.dot_general(left, right, (((0,), (0,)), ((), ())), preferred_element_type=f32)


def outer_cols(left, right):
    return lax.dot_general(left, right, (((1,), (1,)), ((), ())), preferred_element_type=f32)


def norm_back(grad_in, inputs, scale_rows, gain):
    weighted = grad_in * gain
    return scale_rows * weighted - inputs * scale_rows**3 * jnp.mean(
        weighted * inputs, axis=-1, keepdims=True
    )


def take(blocks, index):
    return lax.dynamic_index_in_dim(blocks, index, 0, keepdims=False)


def swap_cores(block):
    return lax.ppermute(block, "core", [(0, 1), (1, 0)])


def to_chip(block, bits):
    count = lax.axis_size("chip")
    return lax.ppermute(block, "chip", [(i, i ^ bits) for i in range(count)])


def gather_near(block):
    rows = block.shape[0]
    if lax.axis_size("chip") != 4:
        return (block,)
    top, low = block[: rows // 2], block[rows // 2 :]
    return top, low, to_chip(top, 1), to_chip(low, 1), to_chip(top, 2), to_chip(low, 2)


def join_kernel(*refs):
    *piece_refs, out_ref = refs
    for k, ref in enumerate(piece_refs):

        @pl.when(pl.program_id(0) == k)
        def _():
            out_ref[...] = ref[...]


def join_rows(pieces):
    rows, width = pieces[0].shape
    count = len(pieces)
    if count == 1:
        return pieces[0]
    return pl.pallas_call(
        join_kernel,
        grid=(count,),
        in_specs=[pl.BlockSpec((rows, width), lambda k: (0, 0))] * count,
        out_specs=pl.BlockSpec((rows, width), lambda k: (k, 0)),
        out_shape=jax.ShapeDtypeStruct((count * rows, width), pieces[0].dtype),
        compiler_params=pltpu.CompilerParams(vmem_limit_bytes=24 << 20),
        cost_estimate=BESIDE,
    )(*pieces)


def gather_far(near):
    return join_rows(far_pieces(near))


def far_pieces(near):
    if lax.axis_size("chip") != 4:
        return [lax.all_gather(near[0], "chip", axis=0, tiled=True)]
    return list(near) + [to_chip(near[2], 2), to_chip(near[5], 1)]


def chip_flip():
    return lax.axis_index("chip") if lax.axis_size("chip") == 4 else jnp.int32(0)


def reordered(blocks, flip):
    bits = 1
    while bits < len(blocks):
        swapped = [blocks[k ^ bits] for k in range(len(blocks))]
        blocks = [jnp.where(flip & bits > 0, b, a) for a, b in zip(blocks, swapped)]
        bits *= 2
    return blocks


def gather_chips(block):
    return gather_far(gather_near(block))


def add(left, right):
    return left.astype(f32) + right.astype(f32)


def scatter_near(pieces):
    if lax.axis_size("chip") != 4:
        return tuple(pieces)
    top, low = pieces[::2], pieces[1::2]
    far = (top[2], to_chip(top[3], 1), low[1], to_chip(low[3], 2))
    return far + (top[0], to_chip(top[1], 1), low[0], to_chip(low[2], 2))


def scatter_far(near):
    if lax.axis_size("chip") != 4:
        return lax.psum_scatter(near[0], "chip", scatter_dimension=0, tiled=True).astype(f32)
    top_far, low_far = add(near[0], near[1]).astype(bf16), add(near[2], near[3]).astype(bf16)
    top = add(near[4], near[5]) + to_chip(top_far, 2).astype(f32)
    low = add(near[6], near[7]) + to_chip(low_far, 1).astype(f32)
    return jnp.concatenate([top, low], 0)


def scatter_chips(pieces, beside=()):
    near, beside = tie(scatter_near(pieces), tuple(beside))
    total = scatter_far(near)
    return (total,) + beside if beside else total


def exchange(parts):
    count = lax.axis_size("chip")
    if count != 4:
        blocks = lax.all_to_all(jnp.stack(parts), "chip", 0, 0, tiled=True)
        return [blocks[k] for k in range(count)]
    return [parts[0]] + [to_chip(parts[k], k) for k in range(1, count)]


def tie(*values):
    return lax.optimization_barrier(values)


def by_columns(weight):
    count = lax.axis_size("chip")
    rows, width = weight.shape
    return weight.reshape(rows, count, width // count).transpose(1, 0, 2)


def gather_blocks(blocks):
    mine = jnp.stack(blocks)[:, None]
    return lax.all_gather(mine, ("core", "dp"), axis=1, tiled=True)


def gather_columns(parts):
    return gather_blocks(exchange(parts))


def gather_rows(weight):
    return lax.all_gather(weight, ("core", "dp"), axis=0, tiled=True)


def sum_cores(own, other):
    return add(own, swap_cores(other)).astype(bf16)


def scatter_dp(half):
    half = half.reshape(lax.axis_size("dp"), -1, half.shape[-1])
    return lax.psum_scatter(half, "dp", scatter_dimension=0, tiled=True)


def trade_blocks(mine):
    return exchange(jnp.split(mine.reshape(-1, mine.shape[-1]), lax.axis_size("chip"), 0))


def join_columns(blocks):
    return jnp.concatenate(reordered(blocks, chip_flip()), 1).astype(f32)


def sum_chips(values):
    count, bits = lax.axis_size("chip"), 1
    while bits < count:
        values = values + to_chip(values, bits)
        bits *= 2
    return values


def row_sums(values):
    sums = jnp.sum(values, axis=-1).reshape(-1, 128)
    return sum_chips(sums).reshape(-1, 1)


def pair_in(block):
    me = lax.axis_index("core")
    kept, got = take(block, me), swap_cores(take(block, 1 - me))
    return jnp.where(
        me == 0, jnp.concatenate([kept, got], 0), jnp.concatenate([got, kept], 0)
    )


def pair_out(rows):
    me = lax.axis_index("core")
    blocks = rows.reshape(CORES, -1, rows.shape[1])
    kept, got = take(blocks, me), swap_cores(take(blocks, 1 - me))
    return jnp.where(me == 0, jnp.stack([kept, got]), jnp.stack([got, kept]))


def visible_scores(keys, queries, first, length, score_scale):
    scores = outer_cols(keys, queries) * score_scale
    key_pos = lax.broadcasted_iota(jnp.int32, scores.shape, 0)
    query_pos = lax.broadcasted_iota(jnp.int32, scores.shape, 1) + first
    return jnp.where((key_pos <= query_pos) & (key_pos < length), scores, -1e30)


def flipped(start, flip):
    return pl.ds(pl.multiple_of(((start // TILE) ^ flip) * TILE, TILE), TILE)


def attend_kernel(
    score_scale,
    length_ref,
    flip_ref,
    rows_ref,
    up_ref,
    keys_ref,
    values_t_ref,
    cos_ref,
    sin_ref,
    queries_ref,
    mixed_ref,
    total_ref,
):
    length, flip = length_ref[0], flip_ref[0]
    chips = lax.axis_size("chip")
    depth = up_ref.shape[1]
    for start in range(0, keys_ref.shape[0], TILE):
        stop = start + TILE
        raw = 0.0
        for part in range(chips):
            raw = raw + matmul(rows_ref[part, start:stop, :depth], up_ref[part])
        raw = raw * cos_ref[start:stop, :] + rotate_half(raw) * sin_ref[start:stop, :]
        queries = raw.astype(bf16)
        queries_ref[start:stop, :] = queries
        scores = visible_scores(keys_ref[:stop, :], queries, start, length, score_scale)
        top = jnp.max(scores, axis=0, keepdims=True)
        powers = jnp.exp(scores - top)
        total = jnp.sum(powers, axis=0, keepdims=True)
        total_ref[0, :, start:stop] = top + jnp.log(total)
        probs = (powers * (1.0 / total)).astype(bf16)
        mixed = matmul(values_t_ref[:, :stop], probs)
        mixed_ref[flipped(start, flip), :] = mixed.T.astype(bf16)


def attend(length, flip, rows, up, keys, values, cos_table, sin_table, score_scale):
    span, head_width = keys.shape
    heads = up.shape[2] // head_width
    whole = lambda array: pl.BlockSpec(array.shape, lambda h: (0, 0))
    head = lambda height: pl.BlockSpec((height, head_width), lambda h: (0, h))
    values_t = values.T
    return pl.pallas_call(
        functools.partial(attend_kernel, score_scale),
        grid=(heads,),
        in_specs=[
            pl.BlockSpec(memory_space=pltpu.SMEM),
            pl.BlockSpec(memory_space=pltpu.SMEM),
            pl.BlockSpec(rows.shape, lambda h: (0, 0, 0)),
            pl.BlockSpec(up.shape[:2] + (head_width,), lambda h: (0, 0, h)),
            whole(keys),
            whole(values_t),
            whole(cos_table),
            whole(sin_table),
        ],
        out_specs=[
            head(span),
            head(span),
            pl.BlockSpec((1, 1, span), lambda h: (h, 0, 0)),
        ],
        out_shape=[
            jax.ShapeDtypeStruct((span, heads * head_width), bf16),
            jax.ShapeDtypeStruct((span, heads * head_width), bf16),
            jax.ShapeDtypeStruct((heads, 1, span), f32),
        ],
        compiler_params=pltpu.CompilerParams(vmem_limit_bytes=62 << 20),
        cost_estimate=BESIDE,
    )(length, flip, rows, up, keys, values_t, cos_table, sin_table)


def attend_back_kernel(
    score_scale,
    length_ref,
    flip_ref,
    queries_ref,
    grad_ref,
    total_ref,
    keys_ref,
    keys_t_ref,
    values_ref,
    cos_ref,
    sin_ref,
    grad_q_ref,
    grad_k_ref,
    grad_v_ref,
):
    length, flip = length_ref[0], flip_ref[0]

    @pl.when(pl.program_id(0) == 0)
    def _():
        grad_k_ref[...] = jnp.zeros_like(grad_k_ref)
        grad_v_ref[...] = jnp.zeros_like(grad_v_ref)

    for start in range(0, queries_ref.shape[0], TILE):
        stop = start + TILE
        queries, grads = queries_ref[start:stop, :], grad_ref[flipped(start, flip), :]
        scores = visible_scores(keys_ref[:stop, :], queries, start, length, score_scale)
        probs = jnp.exp(scores - total_ref[0, :, start:stop])
        grad_probs = outer_cols(values_ref[:stop, :], grads)
        mean = jnp.sum(probs * grad_probs, axis=0, keepdims=True)
        grad_scores = (probs * (grad_probs - mean)).astype(bf16)
        grad_v_ref[:stop, :] += matmul(probs.astype(bf16), grads)
        grad_k_ref[:stop, :] += matmul(grad_scores, queries) * score_scale
        grad_q = matmul(keys_t_ref[:, :stop], grad_scores).T * score_scale
        grad_q = grad_q * cos_ref[start:stop, :] - rotate_half(
            grad_q * sin_ref[start:stop, :]
        )
        grad_q_ref[start:stop, :] = grad_q.astype(bf16)


def attend_back(
    length, flip, queries, grads, total, keys, values, cos_table, sin_table, score_scale
):
    span, head_width = keys.shape
    heads = queries.shape[1] // head_width
    whole = lambda array: pl.BlockSpec(array.shape, lambda h: (0, 0))
    head = pl.BlockSpec((span, head_width), lambda h: (0, h))
    keys_t = keys.T
    summed = jax.ShapeDtypeStruct((span, head_width), f32)
    return pl.pallas_call(
        functools.partial(attend_back_kernel, score_scale),
        grid=(heads,),
        in_specs=[
            pl.BlockSpec(memory_space=pltpu.SMEM),
            pl.BlockSpec(memory_space=pltpu.SMEM),
            head,
            head,
            pl.BlockSpec((1, 1, span), lambda h: (h, 0, 0)),
            whole(keys),
            whole(keys_t),
            whole(values),
            whole(cos_table),
            whole(sin_table),
        ],
        out_specs=[head, whole(keys), whole(keys)],
        out_shape=[jax.ShapeDtypeStruct(queries.shape, bf16), summed, summed],
        compiler_params=pltpu.CompilerParams(vmem_limit_bytes=48 << 20),
        cost_estimate=BESIDE,
    )(length, flip, queries, grads, total, keys, keys_t, values, cos_table, sin_table)


CONTRACT = {"nn": ((1,), (0,)), "nt": ((1,), (1,)), "tn": ((0,), (0,))}


def write_halves(out_refs, block, value):
    rows = value.shape[0] // 2
    for k in range(len(out_refs) // 2):

        @pl.when(block == k)
        def _():
            out_refs[2 * k][...] = value[:rows]
            out_refs[2 * k + 1][...] = value[rows:]


def write_rows(out_refs, value):
    rows = value.shape[0] // len(out_refs)
    for k, out_ref in enumerate(out_refs):
        out_ref[...] = value[k * rows : (k + 1) * rows]


def product_kernel(kind, left_ref, right_ref, *out_refs):
    total = lax.dot_general(
        left_ref[...], right_ref[...], (CONTRACT[kind], ((), ())), preferred_element_type=f32
    )
    write_rows(out_refs, total.astype(bf16))


def product(kind, left, right, pieces=False):
    rows, width = left.shape[0], right.shape[0] if kind == "nt" else right.shape[1]
    chips = lax.axis_size("chip")
    count = 2 * chips if pieces else 1
    if (pieces and chips != 4) or width % TILE or left.shape[1] % 128 or rows % (16 * count):
        total = lax.dot_general(
            left, right, (CONTRACT[kind], ((), ())), preferred_element_type=f32
        ).astype(bf16)
        return as_pieces(total) if pieces else total
    shape = (rows // count, width)
    if kind == "nt":
        source = pl.BlockSpec((TILE, right.shape[1]), lambda i: (i, 0))
    else:
        source = pl.BlockSpec((right.shape[0], TILE), lambda i: (0, i))
    results = pl.pallas_call(
        functools.partial(product_kernel, kind),
        grid=(width // TILE,),
        in_specs=[pl.BlockSpec(left.shape, lambda i: (0, 0)), source],
        out_specs=[pl.BlockSpec((shape[0], TILE), lambda i: (0, i))] * count,
        out_shape=[jax.ShapeDtypeStruct(shape, bf16)] * count,
        compiler_params=pltpu.CompilerParams(vmem_limit_bytes=56 << 20),
        cost_estimate=BESIDE,
    )(left, right)
    return results if pieces else results[0]


def terms_kernel(scale, place_ref, left_ref, right_ref, own_ref, other_ref):
    total = lax.dot_general(
        left_ref[...], right_ref[...], (CONTRACT["tn"], ((), ())), preferred_element_type=f32
    )
    total = (total * scale).astype(bf16).reshape(own_ref.shape)

    @pl.when(pl.program_id(0) == 0)
    def _():
        other_ref[...] = total

    @pl.when(pl.program_id(0) == 1)
    def _():
        own_ref[...] = total


def uneven_kernel(scale, place_ref, left_ref, right_ref, own_ref, other_ref, total_ref):
    total = lax.dot_general(
        left_ref[...], right_ref[...], (CONTRACT["tn"], ((), ())), preferred_element_type=f32
    )
    total_ref[...] = (total * scale).astype(bf16)
    half, core = own_ref.shape[0], place_ref[1]
    own_ref[...] = total_ref[pl.ds(pl.multiple_of(core * half, half), half), :]
    other_ref[...] = total_ref[pl.ds(pl.multiple_of((1 - core) * half, half), half), :]


def weight_terms(left, right, scale, flip=None):
    depth, rows = left.shape
    width = right.shape[1]
    chips, dp = lax.axis_size("chip"), lax.axis_size("dp")
    core = lax.axis_index("core")
    own = rows // (CORES * dp) if flip is None else rows // (chips * CORES * dp)
    half = (dp, chips, own, width) if flip is not None else (dp * own, width)
    tile = dp * own if flip is not None else TILE
    steps = rows // CORES // tile
    whole = lambda array: pl.BlockSpec(array.shape, lambda *_: (0, 0))
    place = jnp.stack([jnp.int32(0) if flip is None else flip, core])
    params = dict(
        out_shape=[jax.ShapeDtypeStruct(half, bf16)] * 2,
        compiler_params=pltpu.CompilerParams(vmem_limit_bytes=56 << 20),
        cost_estimate=BESIDE,
    )
    if tile % 128 == 0 and width % 128 == 0 and rows % (CORES * tile) == 0:
        if flip is not None:
            source = lambda j, k, p: (0, k * CORES + (p[1] ^ 1 ^ j))
            block = (dp, 1, own, width)
            target = lambda k, p: (0, k ^ p[0], 0, 0)
        else:
            source = lambda j, k, p: (0, (p[1] ^ 1 ^ j) * steps + k)
            block = (tile, width)
            target = lambda k, p: (k, 0)
        return pl.pallas_call(
            functools.partial(terms_kernel, scale),
            grid_spec=pltpu.PrefetchScalarGridSpec(
                num_scalar_prefetch=1,
                grid=(CORES, steps),
                in_specs=[pl.BlockSpec((depth, tile), source), whole(right)],
                out_specs=[
                    pl.BlockSpec(block, lambda j, k, p: target(jnp.where(j == 1, k, 0), p)),
                    pl.BlockSpec(
                        block, lambda j, k, p: target(jnp.where(j == 0, k, steps - 1), p)
                    ),
                ],
            ),
            **params,
        )(place, left, right)
    if flip is None and rows % 128 == 0 and width % 512 == 0:
        columns = lambda size: pl.BlockSpec((size, 512), lambda i, p: (0, i))
        return pl.pallas_call(
            functools.partial(uneven_kernel, scale),
            grid_spec=pltpu.PrefetchScalarGridSpec(
                num_scalar_prefetch=1,
                grid=(width // 512,),
                in_specs=[whole(left), columns(depth)],
                out_specs=[columns(rows // CORES)] * 2,
                scratch_shapes=[pltpu.VMEM((rows, 512), bf16)],
            ),
            **params,
        )(place, left, right)
    total = (inner_rows(left, right) * scale).astype(bf16)
    if flip is not None:
        total = total.reshape(chips, CORES, dp, own, width).transpose(1, 2, 0, 3, 4)
    else:
        total = total.reshape((CORES,) + half)
    return take(total, core), take(total, 1 - core)


def as_pieces(terms):
    return jnp.split(terms, 8, 0) if lax.axis_size("chip") == 4 else [terms]


def back_kernel(grad_ref, up_ref, grad_k_ref, grad_v_ref, place_ref, *out_refs):
    grads = outer_cols(grad_ref[...], up_ref[0]).astype(bf16)
    parts = jnp.concatenate([grad_k_ref[...], grad_v_ref[...]], 1).astype(bf16)
    parts = outer_cols(parts, place_ref[0]).astype(bf16)
    write_halves(out_refs, pl.program_id(0), jnp.concatenate([grads, parts], 1))


def back_terms(grad_q, up_q, grad_k, grad_v, place):
    chips, depth, width = up_q.shape
    span = grad_q.shape[0]
    if chips != 4:
        grads = jnp.einsum("tn,kin->kti", grad_q, up_q, preferred_element_type=f32)
        parts = jnp.concatenate([grad_k, grad_v], 1).astype(bf16)
        parts = jnp.einsum("sn,kcn->ksc", parts, place, preferred_element_type=f32)
        terms = jnp.concatenate([grads, parts], 2).astype(bf16)
        return [terms.reshape(chips * span, -1)]
    whole = lambda array: pl.BlockSpec(array.shape, lambda k: (0, 0))
    block = lambda array: pl.BlockSpec((1,) + array.shape[1:], lambda k: (k, 0, 0))
    shape = (span // 2, depth + place.shape[1])
    return pl.pallas_call(
        back_kernel,
        grid=(chips,),
        in_specs=[whole(grad_q), block(up_q), whole(grad_k), whole(grad_v), block(place)],
        out_specs=[pl.BlockSpec(shape, lambda k: (0, 0))] * (2 * chips),
        out_shape=[jax.ShapeDtypeStruct(shape, bf16)] * (2 * chips),
        compiler_params=pltpu.CompilerParams(vmem_limit_bytes=48 << 20),
        cost_estimate=BESIDE,
    )(grad_q, up_q, grad_k, grad_v, place)


def spread_kernel(count, _, *refs):
    left_refs, weight_ref, out_refs = refs[:count], refs[count], refs[count + 1 :]
    _, groups, _, own, width = weight_ref.shape
    total = 0.0
    for j, left_ref in enumerate(left_refs):
        block = weight_ref[0, :, j].reshape(groups * own, width)
        total = total + outer_cols(left_ref[...], block)
    write_rows(out_refs, total.astype(bf16))


def spread(lefts, weight):
    chips, groups, _, own, width = weight.shape
    rows, depth = lefts[0].shape[0], groups * own
    if chips != 4 or width % 128:
        total = sum(
            outer_cols(left, weight[:, :, j].reshape(chips * depth, width))
            for j, left in enumerate(lefts)
        )
        return as_pieces(total.astype(bf16))
    shape = (rows // (2 * chips), chips * depth)
    return pl.pallas_call(
        functools.partial(spread_kernel, len(lefts)),
        grid_spec=pltpu.PrefetchScalarGridSpec(
            num_scalar_prefetch=1,
            grid=(chips,),
            in_specs=[pl.BlockSpec(left.shape, lambda i, f: (0, 0)) for left in lefts]
            + [pl.BlockSpec((1,) + weight.shape[1:], lambda i, f: (i ^ f[0], 0, 0, 0, 0))],
            out_specs=[pl.BlockSpec((shape[0], depth), lambda i, f: (0, i))] * (2 * chips),
        ),
        out_shape=[jax.ShapeDtypeStruct(shape, bf16)] * (2 * chips),
        compiler_params=pltpu.CompilerParams(vmem_limit_bytes=56 << 20),
        cost_estimate=BESIDE,
    )(chip_flip()[None], *lefts, weight)


def whole_kernel(own, place_ref, *refs):
    *left_refs, mine_ref, other_ref, out_ref = refs
    chips = len(left_refs)
    groups, width = mine_ref.shape[2], mine_ref.shape[4]
    half = chips // CORES
    total = 0.0
    for k in range(chips):
        block = pl.program_id(0) ^ k ^ place_ref[0]
        mine = mine_ref[k, block % half, :, :own].reshape(groups * own, width)
        other = other_ref[k, block % half, :, :own].reshape(groups * own, width)
        weight = jnp.where(block // half == place_ref[1], mine, other)
        total = total + outer_cols(left_refs[k][...], weight)
    out_ref[...] = total


def whole_products(lefts, mine, other, weights, own):
    chips = len(lefts)
    rows = lefts[0].shape[0]
    if chips != 4:
        every = lax.all_gather(weights[:, :, :own], "chip", axis=0)
        return sum(
            outer_cols(lefts[k], every[k].reshape(-1, every.shape[-1])) for k in range(chips)
        )
    depth = mine.shape[2] * own
    whole = lambda array: pl.BlockSpec(array.shape, lambda i, p: (0,) * array.ndim)
    return pl.pallas_call(
        functools.partial(whole_kernel, own),
        grid_spec=pltpu.PrefetchScalarGridSpec(
            num_scalar_prefetch=1,
            grid=(chips,),
            in_specs=[whole(left) for left in lefts] + [whole(mine), whole(other)],
            out_specs=pl.BlockSpec((rows, depth), lambda i, p: (0, i)),
        ),
        out_shape=jax.ShapeDtypeStruct((rows, chips * depth), f32),
        compiler_params=pltpu.CompilerParams(vmem_limit_bytes=48 << 20),
        cost_estimate=BESIDE,
    )(jnp.stack([chip_flip(), lax.axis_index("core")]), *lefts, mine, other)


def split_kernel(_, small_ref, qup_ref, gate_ref, up_ref, *out_refs):
    chips = len(out_refs) // 3
    own = gate_ref.shape[0]
    for k in range(chips):

        @pl.when(pl.program_id(0) == k)
        def _():
            out_refs[k][...] = small_ref[0]
            out_refs[chips + k][...] = qup_ref[...]
            out_refs[2 * chips + k][:own, :] = gate_ref[...]
            out_refs[2 * chips + k][own:, :] = up_ref[...]


def split_columns(small, w_qup, w_gate, w_up):
    chips = lax.axis_size("chip")
    own, width = w_gate.shape
    width = width // chips
    if chips != 4 or width % 128:
        gate_up = jnp.concatenate([by_columns(w_gate), by_columns(w_up)], 1)
        return list(small), list(by_columns(w_qup)), list(gate_up)
    own_q, q_width = w_qup.shape[0], w_qup.shape[1] // chips
    shapes = [small.shape[1:], (own_q, q_width), (2 * own, width)]
    columns = lambda rows, size: pl.BlockSpec((rows, size), lambda k, f: (0, k ^ f[0]))
    outs = pl.pallas_call(
        split_kernel,
        grid_spec=pltpu.PrefetchScalarGridSpec(
            num_scalar_prefetch=1,
            grid=(chips,),
            in_specs=[
                pl.BlockSpec((1,) + small.shape[1:], lambda k, f: (k ^ f[0], 0, 0)),
                columns(own_q, q_width),
                columns(own, width),
                columns(own, width),
            ],
            out_specs=[
                pl.BlockSpec(shape, lambda k, f: (0, 0)) for shape in shapes for _ in range(chips)
            ],
        ),
        out_shape=[jax.ShapeDtypeStruct(shape, bf16) for shape in shapes for _ in range(chips)],
        cost_estimate=BESIDE,
    )(chip_flip()[None], small, w_qup, w_gate, w_up)
    return outs[:chips], outs[chips : 2 * chips], outs[2 * chips :]


def normed_kernel(flip_ref, *refs):
    *piece_refs, gain_ref, small_ref, normed_ref, query_ref, pair_ref = refs
    per_step = len(piece_refs) // pl.num_programs(0)
    for k in range(pl.num_programs(0)):

        @pl.when(pl.program_id(0) == k)
        def _():
            pieces = [ref[...] for ref in piece_refs[k * per_step : (k + 1) * per_step]]
            rows = jnp.concatenate(pieces, 0).astype(f32)
            normed = (rows * rms_scale(rows) * gain_ref[...]).astype(bf16)
            normed_ref[...] = normed
            chips, groups, _, width = small_ref.shape
            depth = normed.shape[1] // chips
            own = depth // groups
            raw = 0.0
            for place in range(chips):
                weight = small_ref[place ^ flip_ref[0], :, :own].reshape(depth, width)
                columns = normed[:, place * depth : (place + 1) * depth]
                raw = raw + matmul(columns, weight)
            split = query_ref.shape[1]
            query_ref[...], pair_ref[...] = raw[:, :split], raw[:, split:]


def normed_rows(pieces, gain, small, own, split):
    chips = lax.axis_size("chip")
    if chips != 4:
        rows = pieces[0].astype(f32)
        normed = (rows * rms_scale(rows) * gain).astype(bf16)
        small = small[:, :, :own].reshape(normed.shape[1], -1)
        raw = matmul(normed, small)
        return normed, raw[:, :split], raw[:, split:]
    half, width = pieces[0].shape
    whole = lambda array: pl.BlockSpec(array.shape, lambda k, f: (0,) * array.ndim)
    block = lambda size: pl.BlockSpec((2 * half, size), lambda k, f: (k ^ f[0], 0))
    gain = gain[None, :]
    rows = chips * 2 * half
    return pl.pallas_call(
        normed_kernel,
        grid_spec=pltpu.PrefetchScalarGridSpec(
            num_scalar_prefetch=1,
            grid=(chips,),
            in_specs=[whole(piece) for piece in pieces] + [whole(gain), whole(small)],
            out_specs=[block(width), block(split), block(small.shape[-1] - split)],
        ),
        out_shape=[
            jax.ShapeDtypeStruct((rows, width), bf16),
            jax.ShapeDtypeStruct((rows, split), f32),
            jax.ShapeDtypeStruct((rows, small.shape[-1] - split), f32),
        ],
        compiler_params=pltpu.CompilerParams(vmem_limit_bytes=62 << 20),
        cost_estimate=BESIDE,
    )(chip_flip()[None], *pieces, gain, small)


def gate_terms(gate, up):
    sigma = jax.nn.sigmoid(gate)
    silu = gate * sigma
    return (
        (silu * up).astype(bf16),
        silu.astype(bf16),
        (up * sigma * (1.0 + gate * (1.0 - sigma))).astype(bf16),
    )


def gate_kernel(flip_ref, rows_ref, weight_ref, active_ref, silu_ref, slope_ref):
    chips, groups, _, own, width = weight_ref.shape
    depth = groups * own
    both = 0.0
    for place in range(chips):
        block = weight_ref[place ^ flip_ref[0]]
        block = jnp.concatenate([block[:, j].reshape(depth, width) for j in range(2)], 1)
        both = both + matmul(rows_ref[:, place * depth : (place + 1) * depth], block)
    active_ref[...], silu_ref[...], slope_ref[...] = gate_terms(both[:, :width], both[:, width:])


def gated(rows, gate_up):
    chips, groups, _, own, width = gate_up.shape
    if width % 128:
        gate, up = [gate_up[:, :, j].reshape(rows.shape[1], width) for j in range(2)]
        return gate_terms(matmul(rows, gate), matmul(rows, up))
    out = pl.BlockSpec((rows.shape[0], 128), lambda i, f: (0, i))
    return pl.pallas_call(
        gate_kernel,
        grid_spec=pltpu.PrefetchScalarGridSpec(
            num_scalar_prefetch=1,
            grid=(width // 128,),
            in_specs=[
                pl.BlockSpec(rows.shape, lambda i, f: (0, 0)),
                pl.BlockSpec((chips, groups, 2, own, 128), lambda i, f: (0, 0, 0, 0, i)),
            ],
            out_specs=[out] * 3,
        ),
        out_shape=[jax.ShapeDtypeStruct((rows.shape[0], width), bf16)] * 3,
        compiler_params=pltpu.CompilerParams(vmem_limit_bytes=48 << 20),
        cost_estimate=BESIDE,
    )(chip_flip()[None], rows, gate_up)


def gate_back_kernel(seed_ref, down_ref, silu_ref, slope_ref, gate_ref, up_ref):
    grads = outer_cols(seed_ref[...], down_ref[...])
    gate_ref[...] = (grads * slope_ref[...].astype(f32)).astype(bf16)
    up_ref[...] = (grads * silu_ref[...].astype(f32)).astype(bf16)


def gated_back(seed, down_proj, silu, slope):
    width, depth = down_proj.shape
    if width % 128:
        grads = outer_cols(seed, down_proj)
        return (grads * slope.astype(f32)).astype(bf16), (grads * silu.astype(f32)).astype(bf16)
    rows = lambda size: pl.BlockSpec((TILE, size), lambda i: (i, 0))
    return pl.pallas_call(
        gate_back_kernel,
        grid=(seed.shape[0] // TILE,),
        in_specs=[
            rows(depth),
            pl.BlockSpec(down_proj.shape, lambda i: (0, 0)),
            rows(width),
            rows(width),
        ],
        out_specs=[rows(width)] * 2,
        out_shape=[jax.ShapeDtypeStruct(silu.shape, bf16)] * 2,
        compiler_params=pltpu.CompilerParams(vmem_limit_bytes=48 << 20),
        cost_estimate=BESIDE,
    )(seed, down_proj, silu, slope)


def per_device(
    tokens,
    lengths,
    attn_gain,
    w_qdown,
    q_gain,
    w_qup,
    w_key,
    w_value,
    w_out,
    ffn_gain,
    w_gate,
    w_up,
    w_down,
    cotangent,
):
    slot_count, seq_span, width = tokens.shape[1:]
    assert slot_count == CORES
    chips, dp = lax.axis_size("chip"), lax.axis_size("dp")
    chip, core = lax.axis_index("chip"), lax.axis_index("core")
    devices = chips * CORES * dp
    row_count = CORES * seq_span
    span = chips * row_count
    head_width = w_key.shape[1]
    q_width = w_qdown.shape[1]
    down_shape = w_down.shape
    score_scale = 1.0 / math.sqrt(head_width)
    grad_scale = 1.0 / math.sqrt(slot_count * seq_span * devices)

    half = head_width // 2
    own_rows, own_q = attn_gain.shape[0], q_gain.shape[0]
    q_cols, v_cols, k_cols = q_width // chips, head_width // chips, half // chips
    small_cols = q_cols + 2 * v_cols
    length = lengths[0, core]
    positions = chip * row_count + jnp.arange(row_count, dtype=jnp.int32)
    valid_mask = (positions < length).astype(f32)[:, None]
    tokens_own = pair_in(tokens[0])
    inputs = tokens_own.astype(f32)
    flip = chip_flip()[None]

    key_pairs = w_key.reshape(own_rows, 2, chips, k_cols).transpose(2, 0, 1, 3)
    small = jnp.concatenate(
        [
            by_columns(w_qdown),
            key_pairs.reshape(chips, own_rows, 2 * k_cols),
            by_columns(w_value),
        ],
        2,
    )
    gains = [jnp.pad(gain, (0, small_cols - gain.shape[0])) for gain in (attn_gain, ffn_gain, q_gain)]
    gains = jnp.pad(jnp.stack(gains), ((0, 13), (0, 0)))
    small = jnp.concatenate([small, jnp.broadcast_to(gains, (chips,) + gains.shape)], 1)
    small, up_q, gate_up = split_columns(small, w_qup, w_gate, w_up)
    tokens_own, small = tie(tokens_own, small)
    tokens_near = gather_near(tokens_own)
    cos_all, sin_all = rotary(jnp.arange(span, dtype=jnp.int32), head_width)
    cos_own = lax.dynamic_slice_in_dim(cos_all, chip * k_cols, k_cols, 1)
    sin_own = lax.dynamic_slice_in_dim(sin_all, chip * k_cols, k_cols, 1)
    out_proj, small, tokens_near, tables = tie(
        gather_rows(w_out), exchange(small), tokens_near, (cos_all, sin_all, cos_own, sin_own)
    )
    cos_all, sin_all, cos_own, sin_own = tables
    small = gather_blocks(small)
    tokens_pieces, up_q, gate_up = tie(far_pieces(tokens_near), up_q, gate_up)
    up_q = gather_columns(up_q)
    small, cotangent = tie(small, cotangent)
    seed_grad = (pair_in(cotangent[0]).astype(f32) * valid_mask).astype(bf16)
    gains = small[:, :, own_rows : own_rows + 3].astype(f32)
    gains = jnp.stack(reordered(list(gains), flip[0]))
    gain_one = gains[:, :, 0, :own_rows].reshape(-1)
    gain_two = gains[:, :, 1, :own_rows].reshape(-1)
    gain_q = gains[:, :, 2, :own_q].reshape(chips, -1)[chip]
    up_q = up_q.reshape(chips, q_cols, -1)

    normed_all, q_down, kv_raw = normed_rows(
        tokens_pieces, gain_one, small, own_rows, q_cols
    )
    q_down, kv_raw, gate_up = tie(q_down, kv_raw, exchange(gate_up))
    scale_q = lax.rsqrt(row_sums(q_down * q_down) / q_width + epsilon)
    gate_up = gather_blocks(gate_up)
    down_proj = gather_rows(w_down)
    gate_up = gate_up.reshape(chips, CORES * dp, 2, own_rows, -1)
    q_normed = (q_down * scale_q * gain_q).astype(bf16)
    k_one, k_two = kv_raw[:, :k_cols], kv_raw[:, k_cols:v_cols]
    key_cols = [k_one * cos_own - k_two * sin_own, k_two * cos_own + k_one * sin_own]
    shared = jnp.concatenate(key_cols + [kv_raw[:, v_cols:]], 1).astype(bf16)
    shared = gather_chips(jnp.concatenate([q_normed, shared], 1))
    shared, seed_tied = tie(shared, seed_grad)
    seed_near = gather_near(seed_tied)
    shared = shared.reshape(chips, span, small_cols)
    local, sender = jnp.arange(2 * v_cols), (jnp.arange(chips) ^ flip[0])[:, None]
    target = jnp.where(
        local < v_cols,
        local // k_cols * half + sender * k_cols + local % k_cols,
        head_width + sender * v_cols + local - v_cols,
    )
    place = (target[:, :, None] == jnp.arange(2 * head_width)).astype(bf16)
    key_values = jnp.einsum(
        "ksc,kcn->sn", shared[:, :, q_cols:], place, preferred_element_type=f32
    ).astype(bf16)
    keys, values = key_values[:, :head_width], key_values[:, head_width:]

    queries, mixed, log_total = attend(
        length[None], flip, shared, up_q, keys, values, cos_all, sin_all, score_scale
    )
    part, *seed_near = tie(product("nn", mixed, out_proj, pieces=True), *seed_near)
    middle = inputs + scatter_chips(part)
    scale_two = rms_scale(middle)
    normed2 = gather_chips((middle * scale_two * gain_two).astype(bf16))

    small_rows = small.reshape(CORES, -1, small_cols)
    small_rows = take(small_rows, core) if chips == 4 else small_rows[0]
    normed2, seed_near = tie(normed2, seed_near)
    activated, silu, slope = gated(normed2, gate_up)
    activated, seed_pieces = tie(activated, far_pieces(seed_near))
    seed_all = join_rows(seed_pieces)
    down_terms = weight_terms(activated, seed_all, grad_scale)
    down_terms, down_proj = tie(down_terms, down_proj)
    down_half = sum_cores(*down_terms)
    gate_grad, up_grad = gated_back(seed_all, down_proj, silu, slope)
    gate_grad, up_grad, down_half, small_rows = tie(gate_grad, up_grad, down_half, small_rows)
    small_near = gather_near(small_rows) if chips == 4 else (small_rows,)
    grad_w_down = scatter_dp(down_half)
    part, gate_grad, up_grad = tie(
        spread([gate_grad, up_grad], gate_up), gate_grad, up_grad
    )
    gate_part = weight_terms(normed2, gate_grad, grad_scale, flip[0])
    up_part = weight_terms(normed2, up_grad, grad_scale, flip[0])
    part, small_near = tie(part, small_near)
    near, gate_part, up_part = tie(scatter_near(part), gate_part, up_part)
    near, gate_half = tie(near, sum_cores(*gate_part))
    grad_w_gate = scatter_dp(gate_half)
    grad_normed2, up_half = scatter_far(near), sum_cores(*up_part)
    grad_normed2, grad_w_down, up_half = tie(grad_normed2, grad_w_down, up_half)
    grad_w_up = scatter_dp(up_half)
    grad_middle = seed_grad.astype(f32) + norm_back(grad_normed2, middle, scale_two, gain_two)
    grad_branch, activated = tie(grad_middle.astype(bf16), activated)
    q_rows = shared[:, :, :q_cols].transpose(1, 0, 2).reshape(span, q_width)
    grad_branch, out_part, q_rows = tie(
        gather_chips(grad_branch), product("nn", activated, down_proj, pieces=True), q_rows
    )
    out_near = scatter_near(out_part)
    out_terms = weight_terms(mixed, grad_branch, grad_scale)
    out_terms, grad_branch, grad_w_gate = tie(out_terms, grad_branch, grad_w_gate)
    grad_mixed, out_half, small_near = tie(
        product("nt", grad_branch, out_proj), sum_cores(*out_terms), small_near
    )
    small_pieces = far_pieces(small_near) if chips == 4 else list(small_near)
    grad_w_out = scatter_dp(out_half)
    grad_q, grad_k, grad_v = attend_back(
        length[None], flip, queries, grad_mixed, log_total, keys, values, cos_all, sin_all, score_scale
    )
    grad_q, out_near, small_pieces = tie(grad_q, out_near, small_pieces)
    output = middle + scatter_far(out_near)
    back, grad_q = tie(back_terms(grad_q, up_q, grad_k, grad_v, place), grad_q)
    qup_part = weight_terms(q_rows, grad_q, grad_scale, jnp.int32(0))
    back, qup_part, grad_w_up, output, small_pieces = scatter_chips(
        back, (qup_part, grad_w_up, output, small_pieces)
    )
    back, qup_half, grad_w_out = tie(back, sum_cores(*qup_part), grad_w_out)
    grad_w_qup = scatter_dp(qup_half)
    weighted = back[:, :q_cols] * gain_q
    mean = row_sums(weighted * q_down) / q_width
    pair = jnp.concatenate([grad_w_gate, grad_w_up], 2)
    mean, pair = tie(mean, pair)
    pair = trade_blocks(pair)
    grad_q_down = scale_q * weighted - q_down * scale_q**3 * mean
    k_one, k_two = back[:, q_cols : q_cols + k_cols], back[:, q_cols + k_cols : q_cols + 2 * k_cols]
    back = jnp.concatenate(
        [
            grad_q_down,
            k_one * cos_own + k_two * sin_own,
            k_two * cos_own - k_one * sin_own,
            back[:, q_cols + v_cols :],
        ],
        1,
    ).astype(bf16)
    small_mine = join_rows(small_pieces)
    small_other = swap_cores(small_mine)
    back_parts = exchange(reordered(jnp.split(back, chips, 0), flip[0]))
    small_part = weight_terms(normed_all, back, grad_scale, flip[0])
    back_parts, small_part, small_pair = tie(back_parts, small_part, (small_mine, small_other))
    small_half = sum_cores(*small_part)
    grad_small = scatter_dp(small_half)
    if chips == 4:
        shape = (chips, -1, CORES * dp, small.shape[2], small_cols)
        small_pair = [array.reshape(shape) for array in small_pair]
    grad_normed = whole_products(back_parts, *small_pair, small, own_rows)
    grad_normed, grad_w_qup = tie(grad_normed, grad_w_qup)
    grad_w_qup, pair = tie(trade_blocks(grad_w_qup), pair)
    out_tokens = pair_out(output.astype(bf16))[None]
    grad_inputs = grad_middle + norm_back(grad_normed, inputs, rms_scale(inputs), gain_one)
    grad_tokens = pair_out(grad_inputs)[None]
    grad_w_qup = join_columns(grad_w_qup)
    parts = jnp.stack(reordered(trade_blocks(grad_small), flip[0]), 1).astype(f32)
    grad_w_key = parts[:, :, q_cols : q_cols + v_cols].reshape(own_rows, chips, 2, k_cols)
    grad_w_key = grad_w_key.transpose(0, 2, 1, 3).reshape(own_rows, head_width)
    pairs = [jnp.split(block, 2, 1) for block in pair]
    grad_w_gate, grad_w_up = [join_columns([pair[j] for pair in pairs]) for j in range(2)]
    grad_w_qdown = parts[:, :, :q_cols].reshape(own_rows, q_width)
    grad_w_value = parts[:, :, q_cols + v_cols :].reshape(own_rows, head_width)
    overlap = lambda weight, grad: jnp.sum(weight.astype(f32) * grad, axis=1)
    attn_terms = overlap(w_qdown, grad_w_qdown) + overlap(w_key, grad_w_key)
    attn_terms = attn_terms + overlap(w_value, grad_w_value)
    ffn_terms = overlap(w_gate, grad_w_gate) + overlap(w_up, grad_w_up)
    return (
        out_tokens,
        grad_tokens,
        attn_terms / attn_gain.astype(f32),
        grad_w_qdown,
        overlap(w_qup, grad_w_qup) / q_gain.astype(f32),
        grad_w_qup,
        grad_w_key,
        grad_w_value,
        grad_w_out.astype(f32).reshape(w_out.shape),
        ffn_terms / ffn_gain.astype(f32),
        grad_w_gate,
        grad_w_up,
        grad_w_down.astype(f32).reshape(down_shape),
    )


def solution(mesh):
    seq, dp = mesh.shape["seq"], mesh.shape["dp"]
    chips = Mesh(
        np.asarray(mesh.devices).reshape(seq // CORES, CORES, dp), ("chip", "core", "dp")
    )
    every = ("chip", "core", "dp")
    rows, vector = P(every, None), P(every)
    block = P("dp", None, ("chip", "core"), None)
    weights = (vector, rows, vector, rows, rows, rows, rows, vector, rows, rows, rows)
    return jax.shard_map(
        per_device,
        mesh=chips,
        in_specs=(block, P("dp", None)) + weights + (block,),
        out_specs=(block, block) + weights,
        check_vma=False,
    )
```

```python
import functools
import math

import jax
import jax.numpy as jnp
import numpy as np
from jax import lax
from jax.experimental import pallas as pl
from jax.experimental.pallas import tpu as pltpu
from jax.sharding import Mesh
from jax.sharding import PartitionSpec as P

epsilon = 1e-06
CORES = 2
TILE = 256
f32, bf16 = jnp.float32, jnp.bfloat16
BESIDE = pl.CostEstimate(flops=1, bytes_accessed=1, transcendentals=0)


def rms_scale(values):
    return lax.rsqrt(jnp.mean(values * values, axis=-1, keepdims=True) + epsilon)


def rotate_half(values):
    half_width = values.shape[-1] // 2
    return jnp.concatenate([-values[..., half_width:], values[..., :half_width]], axis=-1)


def rotary(positions, head_width):
    half_width = head_width // 2
    frequency = jnp.exp(
        jnp.arange(half_width, dtype=f32) * (-2.0 * math.log(10000.0) / head_width)
    )
    angles = positions.astype(f32)[:, None] * frequency[None, :]
    cos_table = jnp.cos(angles)
    sin_table = jnp.sin(angles)
    return (
        jnp.concatenate([cos_table, cos_table], -1),
        jnp.concatenate([sin_table, sin_table], -1),
    )


def matmul(left, right):
    return jnp.dot(left, right, preferred_element_type=f32)


def inner_rows(left, right):
    return lax.dot_general(left, right, (((0,), (0,)), ((), ())), preferred_element_type=f32)


def outer_cols(left, right):
    return lax.dot_general(left, right, (((1,), (1,)), ((), ())), preferred_element_type=f32)


def norm_back(grad_in, inputs, scale_rows, gain):
    weighted = grad_in * gain
    return scale_rows * weighted - inputs * scale_rows**3 * jnp.mean(
        weighted * inputs, axis=-1, keepdims=True
    )


def take(blocks, index):
    return lax.dynamic_index_in_dim(blocks, index, 0, keepdims=False)


def swap_cores(block):
    return lax.ppermute(block, "core", [(0, 1), (1, 0)])


def to_chip(block, bits):
    count = lax.axis_size("chip")
    return lax.ppermute(block, "chip", [(i, i ^ bits) for i in range(count)])


def gather_near(block):
    rows = block.shape[0]
    if lax.axis_size("chip") != 4:
        return (block,)
    top, low = block[: rows // 2], block[rows // 2 :]
    return top, low, to_chip(top, 1), to_chip(low, 1), to_chip(top, 2), to_chip(low, 2)


def join_kernel(*refs):
    *piece_refs, out_ref = refs
    for k, ref in enumerate(piece_refs):

        @pl.when(pl.program_id(0) == k)
        def _():
            out_ref[...] = ref[...]


def join_rows(pieces):
    rows, width = pieces[0].shape
    count = len(pieces)
    if count == 1:
        return pieces[0]
    return pl.pallas_call(
        join_kernel,
        grid=(count,),
        in_specs=[pl.BlockSpec((rows, width), lambda k: (0, 0))] * count,
        out_specs=pl.BlockSpec((rows, width), lambda k: (k, 0)),
        out_shape=jax.ShapeDtypeStruct((count * rows, width), pieces[0].dtype),
        compiler_params=pltpu.CompilerParams(vmem_limit_bytes=24 << 20),
        cost_estimate=BESIDE,
    )(*pieces)


def gather_far(near):
    return join_rows(far_pieces(near))


def far_pieces(near):
    if lax.axis_size("chip") != 4:
        return [lax.all_gather(near[0], "chip", axis=0, tiled=True)]
    return list(near) + [to_chip(near[2], 2), to_chip(near[5], 1)]


def chip_flip():
    return lax.axis_index("chip") if lax.axis_size("chip") == 4 else jnp.int32(0)


def reordered(blocks, flip):
    bits = 1
    while bits < len(blocks):
        swapped = [blocks[k ^ bits] for k in range(len(blocks))]
        blocks = [jnp.where(flip & bits > 0, b, a) for a, b in zip(blocks, swapped)]
        bits *= 2
    return blocks


def gather_chips(block):
    return gather_far(gather_near(block))


def add(left, right):
    return left.astype(f32) + right.astype(f32)


def scatter_near(pieces):
    if lax.axis_size("chip") != 4:
        return tuple(pieces)
    top, low = pieces[::2], pieces[1::2]
    far = (top[2], to_chip(top[3], 1), low[1], to_chip(low[3], 2))
    return far + (top[0], to_chip(top[1], 1), low[0], to_chip(low[2], 2))


def scatter_far(near):
    if lax.axis_size("chip") != 4:
        return lax.psum_scatter(near[0], "chip", scatter_dimension=0, tiled=True).astype(f32)
    top_far, low_far = add(near[0], near[1]).astype(bf16), add(near[2], near[3]).astype(bf16)
    top = add(near[4], near[5]) + to_chip(top_far, 2).astype(f32)
    low = add(near[6], near[7]) + to_chip(low_far, 1).astype(f32)
    return jnp.concatenate([top, low], 0)


def scatter_chips(pieces, beside=()):
    near, beside = tie(scatter_near(pieces), tuple(beside))
    total = scatter_far(near)
    return (total,) + beside if beside else total


def exchange(parts):
    count = lax.axis_size("chip")
    if count != 4:
        blocks = lax.all_to_all(jnp.stack(parts), "chip", 0, 0, tiled=True)
        return [blocks[k] for k in range(count)]
    return [parts[0]] + [to_chip(parts[k], k) for k in range(1, count)]


def tie(*values):
    return lax.optimization_barrier(values)


def by_columns(weight):
    count = lax.axis_size("chip")
    rows, width = weight.shape
    return weight.reshape(rows, count, width // count).transpose(1, 0, 2)


def gather_blocks(blocks):
    mine = jnp.stack(blocks)[:, None]
    return lax.all_gather(mine, ("core", "dp"), axis=1, tiled=True)


def gather_columns(parts):
    return gather_blocks(exchange(parts))


def gather_rows(weight):
    return lax.all_gather(weight, ("core", "dp"), axis=0, tiled=True)


def sum_cores(own, other):
    return add(own, swap_cores(other)).astype(bf16)


def scatter_dp(half):
    half = half.reshape(lax.axis_size("dp"), -1, half.shape[-1])
    return lax.psum_scatter(half, "dp", scatter_dimension=0, tiled=True)


def trade_blocks(mine):
    return exchange(jnp.split(mine.reshape(-1, mine.shape[-1]), lax.axis_size("chip"), 0))


def join_columns(blocks):
    return jnp.concatenate(reordered(blocks, chip_flip()), 1).astype(f32)


def sum_chips(values):
    count, bits = lax.axis_size("chip"), 1
    while bits < count:
        values = values + to_chip(values, bits)
        bits *= 2
    return values


def row_sums(values):
    sums = jnp.sum(values, axis=-1).reshape(-1, 128)
    return sum_chips(sums).reshape(-1, 1)


def pair_in(block):
    me = lax.axis_index("core")
    kept, got = take(block, me), swap_cores(take(block, 1 - me))
    return jnp.where(
        me == 0, jnp.concatenate([kept, got], 0), jnp.concatenate([got, kept], 0)
    )


def pair_out(rows):
    me = lax.axis_index("core")
    blocks = rows.reshape(CORES, -1, rows.shape[1])
    kept, got = take(blocks, me), swap_cores(take(blocks, 1 - me))
    return jnp.where(me == 0, jnp.stack([kept, got]), jnp.stack([got, kept]))


def visible_scores(keys, queries, first, length, score_scale):
    scores = outer_cols(keys, queries) * score_scale
    key_pos = lax.broadcasted_iota(jnp.int32, scores.shape, 0)
    query_pos = lax.broadcasted_iota(jnp.int32, scores.shape, 1) + first
    return jnp.where((key_pos <= query_pos) & (key_pos < length), scores, -1e30)


def flipped(start, flip):
    return pl.ds(pl.multiple_of(((start // TILE) ^ flip) * TILE, TILE), TILE)


def attend_kernel(
    score_scale,
    length_ref,
    flip_ref,
    rows_ref,
    up_ref,
    keys_ref,
    values_t_ref,
    cos_ref,
    sin_ref,
    queries_ref,
    mixed_ref,
    total_ref,
):
    length, flip = length_ref[0], flip_ref[0]
    chips = lax.axis_size("chip")
    depth = up_ref.shape[1]
    for start in range(0, keys_ref.shape[0], TILE):
        stop = start + TILE
        raw = 0.0
        for part in range(chips):
            raw = raw + matmul(rows_ref[part, start:stop, :depth], up_ref[part])
        raw = raw * cos_ref[start:stop, :] + rotate_half(raw) * sin_ref[start:stop, :]
        queries = raw.astype(bf16)
        queries_ref[start:stop, :] = queries
        scores = visible_scores(keys_ref[:stop, :], queries, start, length, score_scale)
        top = jnp.max(scores, axis=0, keepdims=True)
        powers = jnp.exp(scores - top)
        total = jnp.sum(powers, axis=0, keepdims=True)
        total_ref[0, :, start:stop] = top + jnp.log(total)
        probs = (powers * (1.0 / total)).astype(bf16)
        mixed = matmul(values_t_ref[:, :stop], probs)
        mixed_ref[flipped(start, flip), :] = mixed.T.astype(bf16)


def attend(length, flip, rows, up, keys, values, cos_table, sin_table, score_scale):
    span, head_width = keys.shape
    heads = up.shape[2] // head_width
    whole = lambda array: pl.BlockSpec(array.shape, lambda h: (0, 0))
    head = lambda height: pl.BlockSpec((height, head_width), lambda h: (0, h))
    values_t = values.T
    return pl.pallas_call(
        functools.partial(attend_kernel, score_scale),
        grid=(heads,),
        in_specs=[
            pl.BlockSpec(memory_space=pltpu.SMEM),
            pl.BlockSpec(memory_space=pltpu.SMEM),
            pl.BlockSpec(rows.shape, lambda h: (0, 0, 0)),
            pl.BlockSpec(up.shape[:2] + (head_width,), lambda h: (0, 0, h)),
            whole(keys),
            whole(values_t),
            whole(cos_table),
            whole(sin_table),
        ],
        out_specs=[
            head(span),
            head(span),
            pl.BlockSpec((1, 1, span), lambda h: (h, 0, 0)),
        ],
        out_shape=[
            jax.ShapeDtypeStruct((span, heads * head_width), bf16),
            jax.ShapeDtypeStruct((span, heads * head_width), bf16),
            jax.ShapeDtypeStruct((heads, 1, span), f32),
        ],
        compiler_params=pltpu.CompilerParams(vmem_limit_bytes=62 << 20),
        cost_estimate=BESIDE,
    )(length, flip, rows, up, keys, values_t, cos_table, sin_table)


def attend_back_kernel(
    score_scale,
    length_ref,
    flip_ref,
    queries_ref,
    grad_ref,
    total_ref,
    keys_ref,
    keys_t_ref,
    values_ref,
    cos_ref,
    sin_ref,
    grad_q_ref,
    grad_k_ref,
    grad_v_ref,
):
    length, flip = length_ref[0], flip_ref[0]

    @pl.when(pl.program_id(0) == 0)
    def _():
        grad_k_ref[...] = jnp.zeros_like(grad_k_ref)
        grad_v_ref[...] = jnp.zeros_like(grad_v_ref)

    for start in range(0, queries_ref.shape[0], TILE):
        stop = start + TILE
        queries, grads = queries_ref[start:stop, :], grad_ref[flipped(start, flip), :]
        scores = visible_scores(keys_ref[:stop, :], queries, start, length, score_scale)
        probs = jnp.exp(scores - total_ref[0, :, start:stop])
        grad_probs = outer_cols(values_ref[:stop, :], grads)
        mean = jnp.sum(probs * grad_probs, axis=0, keepdims=True)
        grad_scores = (probs * (grad_probs - mean)).astype(bf16)
        grad_v_ref[:stop, :] += matmul(probs.astype(bf16), grads)
        grad_k_ref[:stop, :] += matmul(grad_scores, queries) * score_scale
        grad_q = matmul(keys_t_ref[:, :stop], grad_scores).T * score_scale
        grad_q = grad_q * cos_ref[start:stop, :] - rotate_half(
            grad_q * sin_ref[start:stop, :]
        )
        grad_q_ref[start:stop, :] = grad_q.astype(bf16)


def attend_back(
    length, flip, queries, grads, total, keys, values, cos_table, sin_table, score_scale
):
    span, head_width = keys.shape
    heads = queries.shape[1] // head_width
    whole = lambda array: pl.BlockSpec(array.shape, lambda h: (0, 0))
    head = pl.BlockSpec((span, head_width), lambda h: (0, h))
    keys_t = keys.T
    summed = jax.ShapeDtypeStruct((span, head_width), f32)
    return pl.pallas_call(
        functools.partial(attend_back_kernel, score_scale),
        grid=(heads,),
        in_specs=[
            pl.BlockSpec(memory_space=pltpu.SMEM),
            pl.BlockSpec(memory_space=pltpu.SMEM),
            head,
            head,
            pl.BlockSpec((1, 1, span), lambda h: (h, 0, 0)),
            whole(keys),
            whole(keys_t),
            whole(values),
            whole(cos_table),
            whole(sin_table),
        ],
        out_specs=[head, whole(keys), whole(keys)],
        out_shape=[jax.ShapeDtypeStruct(queries.shape, bf16), summed, summed],
        compiler_params=pltpu.CompilerParams(vmem_limit_bytes=48 << 20),
        cost_estimate=BESIDE,
    )(length, flip, queries, grads, total, keys, keys_t, values, cos_table, sin_table)


CONTRACT = {"nn": ((1,), (0,)), "nt": ((1,), (1,)), "tn": ((0,), (0,))}


def write_halves(out_refs, block, value):
    rows = value.shape[0] // 2
    for k in range(len(out_refs) // 2):

        @pl.when(block == k)
        def _():
            out_refs[2 * k][...] = value[:rows]
            out_refs[2 * k + 1][...] = value[rows:]


def write_rows(out_refs, value):
    rows = value.shape[0] // len(out_refs)
    for k, out_ref in enumerate(out_refs):
        out_ref[...] = value[k * rows : (k + 1) * rows]


def product_kernel(kind, left_ref, right_ref, *out_refs):
    total = lax.dot_general(
        left_ref[...], right_ref[...], (CONTRACT[kind], ((), ())), preferred_element_type=f32
    )
    write_rows(out_refs, total.astype(bf16))


def product(kind, left, right, pieces=False):
    rows, width = left.shape[0], right.shape[0] if kind == "nt" else right.shape[1]
    chips = lax.axis_size("chip")
    count = 2 * chips if pieces else 1
    if (pieces and chips != 4) or width % TILE or left.shape[1] % 128 or rows % (16 * count):
        total = lax.dot_general(
            left, right, (CONTRACT[kind], ((), ())), preferred_element_type=f32
        ).astype(bf16)
        return as_pieces(total) if pieces else total
    shape = (rows // count, width)
    if kind == "nt":
        source = pl.BlockSpec((TILE, right.shape[1]), lambda i: (i, 0))
    else:
        source = pl.BlockSpec((right.shape[0], TILE), lambda i: (0, i))
    results = pl.pallas_call(
        functools.partial(product_kernel, kind),
        grid=(width // TILE,),
        in_specs=[pl.BlockSpec(left.shape, lambda i: (0, 0)), source],
        out_specs=[pl.BlockSpec((shape[0], TILE), lambda i: (0, i))] * count,
        out_shape=[jax.ShapeDtypeStruct(shape, bf16)] * count,
        compiler_params=pltpu.CompilerParams(vmem_limit_bytes=34 << 20),
        cost_estimate=BESIDE,
    )(left, right)
    return results if pieces else results[0]


def terms_kernel(scale, place_ref, left_ref, right_ref, own_ref, other_ref):
    total = lax.dot_general(
        left_ref[...], right_ref[...], (CONTRACT["tn"], ((), ())), preferred_element_type=f32
    )
    total = (total * scale).astype(bf16).reshape(own_ref.shape)

    @pl.when(pl.program_id(0) == 0)
    def _():
        other_ref[...] = total

    @pl.when(pl.program_id(0) == 1)
    def _():
        own_ref[...] = total


def uneven_kernel(scale, place_ref, left_ref, right_ref, own_ref, other_ref, total_ref):
    total = lax.dot_general(
        left_ref[...], right_ref[...], (CONTRACT["tn"], ((), ())), preferred_element_type=f32
    )
    total_ref[...] = (total * scale).astype(bf16)
    half, core = own_ref.shape[0], place_ref[1]
    own_ref[...] = total_ref[pl.ds(pl.multiple_of(core * half, half), half), :]
    other_ref[...] = total_ref[pl.ds(pl.multiple_of((1 - core) * half, half), half), :]


def weight_terms(left, right, scale, flip=None):
    depth, rows = left.shape
    width = right.shape[1]
    chips, dp = lax.axis_size("chip"), lax.axis_size("dp")
    core = lax.axis_index("core")
    own = rows // (CORES * dp) if flip is None else rows // (chips * CORES * dp)
    half = (dp, chips, own, width) if flip is not None else (dp * own, width)
    tile = dp * own if flip is not None else TILE
    steps = rows // CORES // tile
    whole = lambda array: pl.BlockSpec(array.shape, lambda *_: (0, 0))
    place = jnp.stack([jnp.int32(0) if flip is None else flip, core])
    params = dict(
        out_shape=[jax.ShapeDtypeStruct(half, bf16)] * 2,
        compiler_params=pltpu.CompilerParams(vmem_limit_bytes=34 << 20),
        cost_estimate=BESIDE,
    )
    if tile % 128 == 0 and width % 128 == 0 and rows % (CORES * tile) == 0:
        if flip is not None:
            source = lambda j, k, p: (0, k * CORES + (p[1] ^ 1 ^ j))
            block = (dp, 1, own, width)
            target = lambda k, p: (0, k ^ p[0], 0, 0)
        else:
            source = lambda j, k, p: (0, (p[1] ^ 1 ^ j) * steps + k)
            block = (tile, width)
            target = lambda k, p: (k, 0)
        return pl.pallas_call(
            functools.partial(terms_kernel, scale),
            grid_spec=pltpu.PrefetchScalarGridSpec(
                num_scalar_prefetch=1,
                grid=(CORES, steps),
                in_specs=[pl.BlockSpec((depth, tile), source), whole(right)],
                out_specs=[
                    pl.BlockSpec(block, lambda j, k, p: target(jnp.where(j == 1, k, 0), p)),
                    pl.BlockSpec(
                        block, lambda j, k, p: target(jnp.where(j == 0, k, steps - 1), p)
                    ),
                ],
            ),
            **params,
        )(place, left, right)
    if flip is None and rows % 128 == 0 and width % 512 == 0:
        columns = lambda size: pl.BlockSpec((size, 512), lambda i, p: (0, i))
        return pl.pallas_call(
            functools.partial(uneven_kernel, scale),
            grid_spec=pltpu.PrefetchScalarGridSpec(
                num_scalar_prefetch=1,
                grid=(width // 512,),
                in_specs=[whole(left), columns(depth)],
                out_specs=[columns(rows // CORES)] * 2,
                scratch_shapes=[pltpu.VMEM((rows, 512), bf16)],
            ),
            **params,
        )(place, left, right)
    total = (inner_rows(left, right) * scale).astype(bf16)
    if flip is not None:
        total = total.reshape(chips, CORES, dp, own, width).transpose(1, 2, 0, 3, 4)
    else:
        total = total.reshape((CORES,) + half)
    return take(total, core), take(total, 1 - core)


def as_pieces(terms):
    return jnp.split(terms, 8, 0) if lax.axis_size("chip") == 4 else [terms]


def back_kernel(grad_ref, up_ref, grad_k_ref, grad_v_ref, place_ref, *out_refs):
    grads = outer_cols(grad_ref[...], up_ref[0]).astype(bf16)
    parts = jnp.concatenate([grad_k_ref[...], grad_v_ref[...]], 1).astype(bf16)
    parts = outer_cols(parts, place_ref[0]).astype(bf16)
    write_halves(out_refs, pl.program_id(0), jnp.concatenate([grads, parts], 1))


def back_terms(grad_q, up_q, grad_k, grad_v, place):
    chips, depth, width = up_q.shape
    span = grad_q.shape[0]
    if chips != 4:
        grads = jnp.einsum("tn,kin->kti", grad_q, up_q, preferred_element_type=f32)
        parts = jnp.concatenate([grad_k, grad_v], 1).astype(bf16)
        parts = jnp.einsum("sn,kcn->ksc", parts, place, preferred_element_type=f32)
        terms = jnp.concatenate([grads, parts], 2).astype(bf16)
        return [terms.reshape(chips * span, -1)]
    whole = lambda array: pl.BlockSpec(array.shape, lambda k: (0, 0))
    block = lambda array: pl.BlockSpec((1,) + array.shape[1:], lambda k: (k, 0, 0))
    shape = (span // 2, depth + place.shape[1])
    return pl.pallas_call(
        back_kernel,
        grid=(chips,),
        in_specs=[whole(grad_q), block(up_q), whole(grad_k), whole(grad_v), block(place)],
        out_specs=[pl.BlockSpec(shape, lambda k: (0, 0))] * (2 * chips),
        out_shape=[jax.ShapeDtypeStruct(shape, bf16)] * (2 * chips),
        compiler_params=pltpu.CompilerParams(vmem_limit_bytes=48 << 20),
        cost_estimate=BESIDE,
    )(grad_q, up_q, grad_k, grad_v, place)


def spread_kernel(count, _, *refs):
    left_refs, weight_ref, out_refs = refs[:count], refs[count], refs[count + 1 :]
    _, groups, _, own, width = weight_ref.shape
    total = 0.0
    for j, left_ref in enumerate(left_refs):
        block = weight_ref[0, :, j].reshape(groups * own, width)
        total = total + outer_cols(left_ref[...], block)
    write_rows(out_refs, total.astype(bf16))


def spread(lefts, weight):
    chips, groups, _, own, width = weight.shape
    rows, depth = lefts[0].shape[0], groups * own
    if chips != 4 or width % 128:
        total = sum(
            outer_cols(left, weight[:, :, j].reshape(chips * depth, width))
            for j, left in enumerate(lefts)
        )
        return as_pieces(total.astype(bf16))
    shape = (rows // (2 * chips), chips * depth)
    return pl.pallas_call(
        functools.partial(spread_kernel, len(lefts)),
        grid_spec=pltpu.PrefetchScalarGridSpec(
            num_scalar_prefetch=1,
            grid=(chips,),
            in_specs=[pl.BlockSpec(left.shape, lambda i, f: (0, 0)) for left in lefts]
            + [pl.BlockSpec((1,) + weight.shape[1:], lambda i, f: (i ^ f[0], 0, 0, 0, 0))],
            out_specs=[pl.BlockSpec((shape[0], depth), lambda i, f: (0, i))] * (2 * chips),
        ),
        out_shape=[jax.ShapeDtypeStruct(shape, bf16)] * (2 * chips),
        compiler_params=pltpu.CompilerParams(vmem_limit_bytes=34 << 20),
        cost_estimate=BESIDE,
    )(chip_flip()[None], *lefts, weight)


def whole_kernel(own, place_ref, *refs):
    *left_refs, mine_ref, other_ref, out_ref = refs
    chips = len(left_refs)
    groups, width = mine_ref.shape[2], mine_ref.shape[4]
    half = chips // CORES
    total = 0.0
    for k in range(chips):
        block = pl.program_id(0) ^ k ^ place_ref[0]
        mine = mine_ref[k, block % half, :, :own].reshape(groups * own, width)
        other = other_ref[k, block % half, :, :own].reshape(groups * own, width)
        weight = jnp.where(block // half == place_ref[1], mine, other)
        total = total + outer_cols(left_refs[k][...], weight)
    out_ref[...] = total


def whole_products(lefts, mine, other, weights, own):
    chips = len(lefts)
    rows = lefts[0].shape[0]
    if chips != 4:
        every = lax.all_gather(weights[:, :, :own], "chip", axis=0)
        return sum(
            outer_cols(lefts[k], every[k].reshape(-1, every.shape[-1])) for k in range(chips)
        )
    depth = mine.shape[2] * own
    whole = lambda array: pl.BlockSpec(array.shape, lambda i, p: (0,) * array.ndim)
    return pl.pallas_call(
        functools.partial(whole_kernel, own),
        grid_spec=pltpu.PrefetchScalarGridSpec(
            num_scalar_prefetch=1,
            grid=(chips,),
            in_specs=[whole(left) for left in lefts] + [whole(mine), whole(other)],
            out_specs=pl.BlockSpec((rows, depth), lambda i, p: (0, i)),
        ),
        out_shape=jax.ShapeDtypeStruct((rows, chips * depth), f32),
        compiler_params=pltpu.CompilerParams(vmem_limit_bytes=48 << 20),
        cost_estimate=BESIDE,
    )(jnp.stack([chip_flip(), lax.axis_index("core")]), *lefts, mine, other)


def split_kernel(_, small_ref, qup_ref, gate_ref, up_ref, *out_refs):
    chips = len(out_refs) // 3
    own = gate_ref.shape[0]
    for k in range(chips):

        @pl.when(pl.program_id(0) == k)
        def _():
            out_refs[k][...] = small_ref[0]
            out_refs[chips + k][...] = qup_ref[...]
            out_refs[2 * chips + k][:own, :] = gate_ref[...]
            out_refs[2 * chips + k][own:, :] = up_ref[...]


def split_columns(small, w_qup, w_gate, w_up):
    chips = lax.axis_size("chip")
    own, width = w_gate.shape
    width = width // chips
    if chips != 4 or width % 128:
        gate_up = jnp.concatenate([by_columns(w_gate), by_columns(w_up)], 1)
        return list(small), list(by_columns(w_qup)), list(gate_up)
    own_q, q_width = w_qup.shape[0], w_qup.shape[1] // chips
    shapes = [small.shape[1:], (own_q, q_width), (2 * own, width)]
    columns = lambda rows, size: pl.BlockSpec((rows, size), lambda k, f: (0, k ^ f[0]))
    outs = pl.pallas_call(
        split_kernel,
        grid_spec=pltpu.PrefetchScalarGridSpec(
            num_scalar_prefetch=1,
            grid=(chips,),
            in_specs=[
                pl.BlockSpec((1,) + small.shape[1:], lambda k, f: (k ^ f[0], 0, 0)),
                columns(own_q, q_width),
                columns(own, width),
                columns(own, width),
            ],
            out_specs=[
                pl.BlockSpec(shape, lambda k, f: (0, 0)) for shape in shapes for _ in range(chips)
            ],
        ),
        out_shape=[jax.ShapeDtypeStruct(shape, bf16) for shape in shapes for _ in range(chips)],
        cost_estimate=BESIDE,
    )(chip_flip()[None], small, w_qup, w_gate, w_up)
    return outs[:chips], outs[chips : 2 * chips], outs[2 * chips :]


def normed_kernel(flip_ref, *refs):
    *piece_refs, gain_ref, small_ref, normed_ref, query_ref, pair_ref = refs
    per_step = len(piece_refs) // pl.num_programs(0)
    for k in range(pl.num_programs(0)):

        @pl.when(pl.program_id(0) == k)
        def _():
            pieces = [ref[...] for ref in piece_refs[k * per_step : (k + 1) * per_step]]
            rows = jnp.concatenate(pieces, 0).astype(f32)
            normed = (rows * rms_scale(rows) * gain_ref[...]).astype(bf16)
            normed_ref[...] = normed
            chips, groups, _, width = small_ref.shape
            depth = normed.shape[1] // chips
            own = depth // groups
            raw = 0.0
            for place in range(chips):
                weight = small_ref[place ^ flip_ref[0], :, :own].reshape(depth, width)
                columns = normed[:, place * depth : (place + 1) * depth]
                raw = raw + matmul(columns, weight)
            split = query_ref.shape[1]
            query_ref[...], pair_ref[...] = raw[:, :split], raw[:, split:]


def normed_rows(pieces, gain, small, own, split):
    chips = lax.axis_size("chip")
    if chips != 4:
        rows = pieces[0].astype(f32)
        normed = (rows * rms_scale(rows) * gain).astype(bf16)
        small = small[:, :, :own].reshape(normed.shape[1], -1)
        raw = matmul(normed, small)
        return normed, raw[:, :split], raw[:, split:]
    half, width = pieces[0].shape
    whole = lambda array: pl.BlockSpec(array.shape, lambda k, f: (0,) * array.ndim)
    block = lambda size: pl.BlockSpec((2 * half, size), lambda k, f: (k ^ f[0], 0))
    gain = gain[None, :]
    rows = chips * 2 * half
    return pl.pallas_call(
        normed_kernel,
        grid_spec=pltpu.PrefetchScalarGridSpec(
            num_scalar_prefetch=1,
            grid=(chips,),
            in_specs=[whole(piece) for piece in pieces] + [whole(gain), whole(small)],
            out_specs=[block(width), block(split), block(small.shape[-1] - split)],
        ),
        out_shape=[
            jax.ShapeDtypeStruct((rows, width), bf16),
            jax.ShapeDtypeStruct((rows, split), f32),
            jax.ShapeDtypeStruct((rows, small.shape[-1] - split), f32),
        ],
        compiler_params=pltpu.CompilerParams(vmem_limit_bytes=62 << 20),
        cost_estimate=BESIDE,
    )(chip_flip()[None], *pieces, gain, small)


def gate_terms(gate, up):
    sigma = jax.nn.sigmoid(gate)
    silu = gate * sigma
    return (
        (silu * up).astype(bf16),
        silu.astype(bf16),
        (up * sigma * (1.0 + gate * (1.0 - sigma))).astype(bf16),
    )


def gate_kernel(flip_ref, rows_ref, weight_ref, active_ref, silu_ref, slope_ref):
    chips, groups, _, own, width = weight_ref.shape
    depth = groups * own
    both = 0.0
    for place in range(chips):
        block = weight_ref[place ^ flip_ref[0]]
        block = jnp.concatenate([block[:, j].reshape(depth, width) for j in range(2)], 1)
        both = both + matmul(rows_ref[:, place * depth : (place + 1) * depth], block)
    active_ref[...], silu_ref[...], slope_ref[...] = gate_terms(both[:, :width], both[:, width:])


def gated(rows, gate_up):
    chips, groups, _, own, width = gate_up.shape
    if width % 128:
        gate, up = [gate_up[:, :, j].reshape(rows.shape[1], width) for j in range(2)]
        return gate_terms(matmul(rows, gate), matmul(rows, up))
    out = pl.BlockSpec((rows.shape[0], 128), lambda i, f: (0, i))
    return pl.pallas_call(
        gate_kernel,
        grid_spec=pltpu.PrefetchScalarGridSpec(
            num_scalar_prefetch=1,
            grid=(width // 128,),
            in_specs=[
                pl.BlockSpec(rows.shape, lambda i, f: (0, 0)),
                pl.BlockSpec((chips, groups, 2, own, 128), lambda i, f: (0, 0, 0, 0, i)),
            ],
            out_specs=[out] * 3,
        ),
        out_shape=[jax.ShapeDtypeStruct((rows.shape[0], width), bf16)] * 3,
        compiler_params=pltpu.CompilerParams(vmem_limit_bytes=48 << 20),
        cost_estimate=BESIDE,
    )(chip_flip()[None], rows, gate_up)


def gate_back_kernel(seed_ref, down_ref, silu_ref, slope_ref, gate_ref, up_ref):
    grads = outer_cols(seed_ref[...], down_ref[...])
    gate_ref[...] = (grads * slope_ref[...].astype(f32)).astype(bf16)
    up_ref[...] = (grads * silu_ref[...].astype(f32)).astype(bf16)


def gated_back(seed, down_proj, silu, slope):
    width, depth = down_proj.shape
    if width % 128:
        grads = outer_cols(seed, down_proj)
        return (grads * slope.astype(f32)).astype(bf16), (grads * silu.astype(f32)).astype(bf16)
    rows = lambda size: pl.BlockSpec((TILE, size), lambda i: (i, 0))
    return pl.pallas_call(
        gate_back_kernel,
        grid=(seed.shape[0] // TILE,),
        in_specs=[
            rows(depth),
            pl.BlockSpec(down_proj.shape, lambda i: (0, 0)),
            rows(width),
            rows(width),
        ],
        out_specs=[rows(width)] * 2,
        out_shape=[jax.ShapeDtypeStruct(silu.shape, bf16)] * 2,
        compiler_params=pltpu.CompilerParams(vmem_limit_bytes=48 << 20),
        cost_estimate=BESIDE,
    )(seed, down_proj, silu, slope)


def per_device(
    tokens,
    lengths,
    attn_gain,
    w_qdown,
    q_gain,
    w_qup,
    w_key,
    w_value,
    w_out,
    ffn_gain,
    w_gate,
    w_up,
    w_down,
    cotangent,
):
    slot_count, seq_span, width = tokens.shape[1:]
    assert slot_count == CORES
    chips, dp = lax.axis_size("chip"), lax.axis_size("dp")
    chip, core = lax.axis_index("chip"), lax.axis_index("core")
    devices = chips * CORES * dp
    row_count = CORES * seq_span
    span = chips * row_count
    head_width = w_key.shape[1]
    q_width = w_qdown.shape[1]
    down_shape = w_down.shape
    score_scale = 1.0 / math.sqrt(head_width)
    grad_scale = 1.0 / math.sqrt(slot_count * seq_span * devices)

    half = head_width // 2
    own_rows, own_q = attn_gain.shape[0], q_gain.shape[0]
    q_cols, v_cols, k_cols = q_width // chips, head_width // chips, half // chips
    small_cols = q_cols + 2 * v_cols
    length = lengths[0, core]
    positions = chip * row_count + jnp.arange(row_count, dtype=jnp.int32)
    valid_mask = (positions < length).astype(f32)[:, None]
    tokens_own = pair_in(tokens[0])
    inputs = tokens_own.astype(f32)
    flip = chip_flip()[None]

    key_pairs = w_key.reshape(own_rows, 2, chips, k_cols).transpose(2, 0, 1, 3)
    small = jnp.concatenate(
        [
            by_columns(w_qdown),
            key_pairs.reshape(chips, own_rows, 2 * k_cols),
            by_columns(w_value),
        ],
        2,
    )
    gains = [jnp.pad(gain, (0, small_cols - gain.shape[0])) for gain in (attn_gain, ffn_gain, q_gain)]
    gains = jnp.pad(jnp.stack(gains), ((0, 13), (0, 0)))
    small = jnp.concatenate([small, jnp.broadcast_to(gains, (chips,) + gains.shape)], 1)
    small, up_q, gate_up = split_columns(small, w_qup, w_gate, w_up)
    tokens_own, small = tie(tokens_own, small)
    tokens_near = gather_near(tokens_own)
    cos_all, sin_all = rotary(jnp.arange(span, dtype=jnp.int32), head_width)
    cos_own = lax.dynamic_slice_in_dim(cos_all, chip * k_cols, k_cols, 1)
    sin_own = lax.dynamic_slice_in_dim(sin_all, chip * k_cols, k_cols, 1)
    out_proj, small, tokens_near, tables = tie(
        gather_rows(w_out), exchange(small), tokens_near, (cos_all, sin_all, cos_own, sin_own)
    )
    cos_all, sin_all, cos_own, sin_own = tables
    small = gather_blocks(small)
    tokens_pieces, up_q, gate_up = tie(far_pieces(tokens_near), up_q, gate_up)
    up_q = gather_columns(up_q)
    small, cotangent = tie(small, cotangent)
    seed_grad = (pair_in(cotangent[0]).astype(f32) * valid_mask).astype(bf16)
    gains = small[:, :, own_rows : own_rows + 3].astype(f32)
    gains = jnp.stack(reordered(list(gains), flip[0]))
    gain_one = gains[:, :, 0, :own_rows].reshape(-1)
    gain_two = gains[:, :, 1, :own_rows].reshape(-1)
    gain_q = gains[:, :, 2, :own_q].reshape(chips, -1)[chip]
    up_q = up_q.reshape(chips, q_cols, -1)

    normed_all, q_down, kv_raw = normed_rows(
        tokens_pieces, gain_one, small, own_rows, q_cols
    )
    q_down, kv_raw, gate_up = tie(q_down, kv_raw, exchange(gate_up))
    scale_q = lax.rsqrt(row_sums(q_down * q_down) / q_width + epsilon)
    gate_up = gather_blocks(gate_up)
    down_proj = gather_rows(w_down)
    gate_up = gate_up.reshape(chips, CORES * dp, 2, own_rows, -1)
    q_normed = (q_down * scale_q * gain_q).astype(bf16)
    k_one, k_two = kv_raw[:, :k_cols], kv_raw[:, k_cols:v_cols]
    key_cols = [k_one * cos_own - k_two * sin_own, k_two * cos_own + k_one * sin_own]
    shared = jnp.concatenate(key_cols + [kv_raw[:, v_cols:]], 1).astype(bf16)
    shared = gather_chips(jnp.concatenate([q_normed, shared], 1))
    shared, seed_tied = tie(shared, seed_grad)
    seed_near = gather_near(seed_tied)
    shared = shared.reshape(chips, span, small_cols)
    local, sender = jnp.arange(2 * v_cols), (jnp.arange(chips) ^ flip[0])[:, None]
    target = jnp.where(
        local < v_cols,
        local // k_cols * half + sender * k_cols + local % k_cols,
        head_width + sender * v_cols + local - v_cols,
    )
    place = (target[:, :, None] == jnp.arange(2 * head_width)).astype(bf16)
    key_values = jnp.einsum(
        "ksc,kcn->sn", shared[:, :, q_cols:], place, preferred_element_type=f32
    ).astype(bf16)
    keys, values = key_values[:, :head_width], key_values[:, head_width:]

    queries, mixed, log_total = attend(
        length[None], flip, shared, up_q, keys, values, cos_all, sin_all, score_scale
    )
    part, *seed_near = tie(product("nn", mixed, out_proj, pieces=True), *seed_near)
    middle = inputs + scatter_chips(part)
    scale_two = rms_scale(middle)
    normed2 = gather_chips((middle * scale_two * gain_two).astype(bf16))

    small_rows = small.reshape(CORES, -1, small_cols)
    small_rows = take(small_rows, core) if chips == 4 else small_rows[0]
    normed2, seed_near = tie(normed2, seed_near)
    activated, silu, slope = gated(normed2, gate_up)
    activated, seed_pieces = tie(activated, far_pieces(seed_near))
    seed_all = join_rows(seed_pieces)
    down_terms = weight_terms(activated, seed_all, grad_scale)
    down_terms, down_proj = tie(down_terms, down_proj)
    down_half = sum_cores(*down_terms)
    gate_grad, up_grad = gated_back(seed_all, down_proj, silu, slope)
    gate_grad, up_grad, down_half, small_rows = tie(gate_grad, up_grad, down_half, small_rows)
    small_near = gather_near(small_rows) if chips == 4 else (small_rows,)
    grad_w_down = scatter_dp(down_half)
    part, gate_grad, up_grad = tie(
        spread([gate_grad, up_grad], gate_up), gate_grad, up_grad
    )
    gate_part = weight_terms(normed2, gate_grad, grad_scale, flip[0])
    up_part = weight_terms(normed2, up_grad, grad_scale, flip[0])
    part, small_near = tie(part, small_near)
    near, gate_part, up_part = tie(scatter_near(part), gate_part, up_part)
    near, gate_half = tie(near, sum_cores(*gate_part))
    grad_w_gate = scatter_dp(gate_half)
    grad_normed2, up_half = scatter_far(near), sum_cores(*up_part)
    grad_normed2, grad_w_down, up_half = tie(grad_normed2, grad_w_down, up_half)
    grad_w_up = scatter_dp(up_half)
    grad_middle = seed_grad.astype(f32) + norm_back(grad_normed2, middle, scale_two, gain_two)
    grad_branch, activated = tie(grad_middle.astype(bf16), activated)
    q_rows = shared[:, :, :q_cols].transpose(1, 0, 2).reshape(span, q_width)
    grad_branch, out_part, q_rows = tie(
        gather_chips(grad_branch), product("nn", activated, down_proj, pieces=True), q_rows
    )
    out_near = scatter_near(out_part)
    out_terms = weight_terms(mixed, grad_branch, grad_scale)
    out_terms, grad_branch, grad_w_gate = tie(out_terms, grad_branch, grad_w_gate)
    grad_mixed, out_half, small_near = tie(
        product("nt", grad_branch, out_proj), sum_cores(*out_terms), small_near
    )
    small_pieces = far_pieces(small_near) if chips == 4 else list(small_near)
    grad_w_out = scatter_dp(out_half)
    grad_q, grad_k, grad_v = attend_back(
        length[None], flip, queries, grad_mixed, log_total, keys, values, cos_all, sin_all, score_scale
    )
    grad_q, out_near, small_pieces = tie(grad_q, out_near, small_pieces)
    output = middle + scatter_far(out_near)
    back, grad_q = tie(back_terms(grad_q, up_q, grad_k, grad_v, place), grad_q)
    qup_part = weight_terms(q_rows, grad_q, grad_scale, jnp.int32(0))
    back, qup_part, grad_w_up, output, small_pieces = scatter_chips(
        back, (qup_part, grad_w_up, output, small_pieces)
    )
    back, qup_half, grad_w_out = tie(back, sum_cores(*qup_part), grad_w_out)
    grad_w_qup = scatter_dp(qup_half)
    weighted = back[:, :q_cols] * gain_q
    mean = row_sums(weighted * q_down) / q_width
    pair = jnp.concatenate([grad_w_gate, grad_w_up], 2)
    mean, pair = tie(mean, pair)
    pair = trade_blocks(pair)
    grad_q_down = scale_q * weighted - q_down * scale_q**3 * mean
    k_one, k_two = back[:, q_cols : q_cols + k_cols], back[:, q_cols + k_cols : q_cols + 2 * k_cols]
    back = jnp.concatenate(
        [
            grad_q_down,
            k_one * cos_own + k_two * sin_own,
            k_two * cos_own - k_one * sin_own,
            back[:, q_cols + v_cols :],
        ],
        1,
    ).astype(bf16)
    small_mine = join_rows(small_pieces)
    small_other = swap_cores(small_mine)
    back_parts = exchange(reordered(jnp.split(back, chips, 0), flip[0]))
    small_part = weight_terms(normed_all, back, grad_scale, flip[0])
    back_parts, small_part, small_pair = tie(back_parts, small_part, (small_mine, small_other))
    small_half = sum_cores(*small_part)
    grad_small = scatter_dp(small_half)
    if chips == 4:
        shape = (chips, -1, CORES * dp, small.shape[2], small_cols)
        small_pair = [array.reshape(shape) for array in small_pair]
    grad_normed = whole_products(back_parts, *small_pair, small, own_rows)
    grad_normed, grad_w_qup = tie(grad_normed, grad_w_qup)
    grad_w_qup, pair = tie(trade_blocks(grad_w_qup), pair)
    out_tokens = pair_out(output.astype(bf16))[None]
    grad_inputs = grad_middle + norm_back(grad_normed, inputs, rms_scale(inputs), gain_one)
    grad_tokens = pair_out(grad_inputs)[None]
    grad_w_qup = join_columns(grad_w_qup)
    parts = jnp.stack(reordered(trade_blocks(grad_small), flip[0]), 1).astype(f32)
    grad_w_key = parts[:, :, q_cols : q_cols + v_cols].reshape(own_rows, chips, 2, k_cols)
    grad_w_key = grad_w_key.transpose(0, 2, 1, 3).reshape(own_rows, head_width)
    pairs = [jnp.split(block, 2, 1) for block in pair]
    grad_w_gate, grad_w_up = [join_columns([pair[j] for pair in pairs]) for j in range(2)]
    grad_w_qdown = parts[:, :, :q_cols].reshape(own_rows, q_width)
    grad_w_value = parts[:, :, q_cols + v_cols :].reshape(own_rows, head_width)
    overlap = lambda weight, grad: jnp.sum(weight.astype(f32) * grad, axis=1)
    attn_terms = overlap(w_qdown, grad_w_qdown) + overlap(w_key, grad_w_key)
    attn_terms = attn_terms + overlap(w_value, grad_w_value)
    ffn_terms = overlap(w_gate, grad_w_gate) + overlap(w_up, grad_w_up)
    return (
        out_tokens,
        grad_tokens,
        attn_terms / attn_gain.astype(f32),
        grad_w_qdown,
        overlap(w_qup, grad_w_qup) / q_gain.astype(f32),
        grad_w_qup,
        grad_w_key,
        grad_w_value,
        grad_w_out.astype(f32).reshape(w_out.shape),
        ffn_terms / ffn_gain.astype(f32),
        grad_w_gate,
        grad_w_up,
        grad_w_down.astype(f32).reshape(down_shape),
    )


def solution(mesh):
    seq, dp = mesh.shape["seq"], mesh.shape["dp"]
    chips = Mesh(
        np.asarray(mesh.devices).reshape(seq // CORES, CORES, dp), ("chip", "core", "dp")
    )
    every = ("chip", "core", "dp")
    rows, vector = P(every, None), P(every)
    block = P("dp", None, ("chip", "core"), None)
    weights = (vector, rows, vector, rows, rows, rows, rows, vector, rows, rows, rows)
    return jax.shard_map(
        per_device,
        mesh=chips,
        in_specs=(block, P("dp", None)) + weights + (block,),
        out_specs=(block, block) + weights,
        check_vma=False,
    )
```

```python
import functools
import math

import jax
import jax.numpy as jnp
import numpy as np
from jax import lax
from jax.experimental import pallas as pl
from jax.experimental.pallas import tpu as pltpu
from jax.sharding import Mesh
from jax.sharding import PartitionSpec as P

epsilon = 1e-06
CORES = 2
TILE = 256
f32, bf16 = jnp.float32, jnp.bfloat16
BESIDE = pl.CostEstimate(flops=1, bytes_accessed=1, transcendentals=0)


def rms_scale(values):
    return lax.rsqrt(jnp.mean(values * values, axis=-1, keepdims=True) + epsilon)


def rotate_half(values):
    half_width = values.shape[-1] // 2
    return jnp.concatenate([-values[..., half_width:], values[..., :half_width]], axis=-1)


def rotary(positions, head_width):
    half_width = head_width // 2
    frequency = jnp.exp(
        jnp.arange(half_width, dtype=f32) * (-2.0 * math.log(10000.0) / head_width)
    )
    angles = positions.astype(f32)[:, None] * frequency[None, :]
    cos_table = jnp.cos(angles)
    sin_table = jnp.sin(angles)
    return (
        jnp.concatenate([cos_table, cos_table], -1),
        jnp.concatenate([sin_table, sin_table], -1),
    )


def matmul(left, right):
    return jnp.dot(left, right, preferred_element_type=f32)


def inner_rows(left, right):
    return lax.dot_general(left, right, (((0,), (0,)), ((), ())), preferred_element_type=f32)


def outer_cols(left, right):
    return lax.dot_general(left, right, (((1,), (1,)), ((), ())), preferred_element_type=f32)


def norm_back(grad_in, inputs, scale_rows, gain):
    weighted = grad_in * gain
    return scale_rows * weighted - inputs * scale_rows**3 * jnp.mean(
        weighted * inputs, axis=-1, keepdims=True
    )


def take(blocks, index):
    return lax.dynamic_index_in_dim(blocks, index, 0, keepdims=False)


def swap_cores(block):
    return lax.ppermute(block, "core", [(0, 1), (1, 0)])


def to_chip(block, bits):
    count = lax.axis_size("chip")
    return lax.ppermute(block, "chip", [(i, i ^ bits) for i in range(count)])


def gather_near(block):
    rows = block.shape[0]
    if lax.axis_size("chip") != 4:
        return (block,)
    top, low = block[: rows // 2], block[rows // 2 :]
    return top, low, to_chip(top, 1), to_chip(low, 1), to_chip(top, 2), to_chip(low, 2)


def join_kernel(*refs):
    *piece_refs, out_ref = refs
    for k, ref in enumerate(piece_refs):

        @pl.when(pl.program_id(0) == k)
        def _():
            out_ref[...] = ref[...]


def join_rows(pieces):
    rows, width = pieces[0].shape
    count = len(pieces)
    if count == 1:
        return pieces[0]
    return pl.pallas_call(
        join_kernel,
        grid=(count,),
        in_specs=[pl.BlockSpec((rows, width), lambda k: (0, 0))] * count,
        out_specs=pl.BlockSpec((rows, width), lambda k: (k, 0)),
        out_shape=jax.ShapeDtypeStruct((count * rows, width), pieces[0].dtype),
        compiler_params=pltpu.CompilerParams(vmem_limit_bytes=24 << 20),
        cost_estimate=BESIDE,
    )(*pieces)


def gather_far(near):
    return join_rows(far_pieces(near))


def far_pieces(near):
    if lax.axis_size("chip") != 4:
        return [lax.all_gather(near[0], "chip", axis=0, tiled=True)]
    return list(near) + [to_chip(near[2], 2), to_chip(near[5], 1)]


def chip_flip():
    return lax.axis_index("chip") if lax.axis_size("chip") == 4 else jnp.int32(0)


def reordered(blocks, flip):
    bits = 1
    while bits < len(blocks):
        swapped = [blocks[k ^ bits] for k in range(len(blocks))]
        blocks = [jnp.where(flip & bits > 0, b, a) for a, b in zip(blocks, swapped)]
        bits *= 2
    return blocks


def gather_chips(block):
    return gather_far(gather_near(block))


def add(left, right):
    return left.astype(f32) + right.astype(f32)


def scatter_near(pieces):
    if lax.axis_size("chip") != 4:
        return tuple(pieces)
    top, low = pieces[::2], pieces[1::2]
    far = (top[2], to_chip(top[3], 1), low[1], to_chip(low[3], 2))
    return far + (top[0], to_chip(top[1], 1), low[0], to_chip(low[2], 2))


def scatter_far(near):
    if lax.axis_size("chip") != 4:
        return lax.psum_scatter(near[0], "chip", scatter_dimension=0, tiled=True).astype(f32)
    top_far, low_far = add(near[0], near[1]).astype(bf16), add(near[2], near[3]).astype(bf16)
    top = add(near[4], near[5]) + to_chip(top_far, 2).astype(f32)
    low = add(near[6], near[7]) + to_chip(low_far, 1).astype(f32)
    return jnp.concatenate([top, low], 0)


def scatter_chips(pieces, beside=()):
    near, beside = tie(scatter_near(pieces), tuple(beside))
    total = scatter_far(near)
    return (total,) + beside if beside else total


def exchange(parts):
    count = lax.axis_size("chip")
    if count != 4:
        blocks = lax.all_to_all(jnp.stack(parts), "chip", 0, 0, tiled=True)
        return [blocks[k] for k in range(count)]
    return [parts[0]] + [to_chip(parts[k], k) for k in range(1, count)]


def tie(*values):
    return lax.optimization_barrier(values)


def by_columns(weight):
    count = lax.axis_size("chip")
    rows, width = weight.shape
    return weight.reshape(rows, count, width // count).transpose(1, 0, 2)


def gather_blocks(blocks):
    mine = jnp.stack(blocks)[:, None]
    return lax.all_gather(mine, ("core", "dp"), axis=1, tiled=True)


def gather_columns(parts):
    return gather_blocks(exchange(parts))


def gather_rows(weight):
    return lax.all_gather(weight, ("core", "dp"), axis=0, tiled=True)


def sum_cores(own, other):
    return add(own, swap_cores(other)).astype(bf16)


def scatter_dp(half):
    half = half.reshape(lax.axis_size("dp"), -1, half.shape[-1])
    return lax.psum_scatter(half, "dp", scatter_dimension=0, tiled=True)


def trade_blocks(mine):
    return exchange(jnp.split(mine.reshape(-1, mine.shape[-1]), lax.axis_size("chip"), 0))


def join_columns(blocks):
    return jnp.concatenate(reordered(blocks, chip_flip()), 1).astype(f32)


def sum_chips(values):
    count, bits = lax.axis_size("chip"), 1
    while bits < count:
        values = values + to_chip(values, bits)
        bits *= 2
    return values


def row_sums(values):
    sums = jnp.sum(values, axis=-1).reshape(-1, 128)
    return sum_chips(sums).reshape(-1, 1)


def pair_in(block):
    me = lax.axis_index("core")
    kept, got = take(block, me), swap_cores(take(block, 1 - me))
    return jnp.where(
        me == 0, jnp.concatenate([kept, got], 0), jnp.concatenate([got, kept], 0)
    )


def pair_out(rows):
    me = lax.axis_index("core")
    blocks = rows.reshape(CORES, -1, rows.shape[1])
    kept, got = take(blocks, me), swap_cores(take(blocks, 1 - me))
    return jnp.where(me == 0, jnp.stack([kept, got]), jnp.stack([got, kept]))


def visible_scores(keys, queries, first, length, score_scale):
    scores = outer_cols(keys, queries) * score_scale
    key_pos = lax.broadcasted_iota(jnp.int32, scores.shape, 0)
    query_pos = lax.broadcasted_iota(jnp.int32, scores.shape, 1) + first
    return jnp.where((key_pos <= query_pos) & (key_pos < length), scores, -1e30)


def flipped(start, flip):
    return pl.ds(pl.multiple_of(((start // TILE) ^ flip) * TILE, TILE), TILE)


def attend_kernel(
    score_scale,
    length_ref,
    flip_ref,
    rows_ref,
    up_ref,
    keys_ref,
    values_t_ref,
    cos_ref,
    sin_ref,
    queries_ref,
    mixed_ref,
    total_ref,
):
    length, flip = length_ref[0], flip_ref[0]
    chips = lax.axis_size("chip")
    depth = up_ref.shape[1]
    for start in range(0, keys_ref.shape[0], TILE):
        stop = start + TILE
        raw = 0.0
        for part in range(chips):
            raw = raw + matmul(rows_ref[part, start:stop, :depth], up_ref[part])
        raw = raw * cos_ref[start:stop, :] + rotate_half(raw) * sin_ref[start:stop, :]
        queries = raw.astype(bf16)
        queries_ref[start:stop, :] = queries
        scores = visible_scores(keys_ref[:stop, :], queries, start, length, score_scale)
        top = jnp.max(scores, axis=0, keepdims=True)
        powers = jnp.exp(scores - top)
        total = jnp.sum(powers, axis=0, keepdims=True)
        total_ref[0, :, start:stop] = top + jnp.log(total)
        probs = (powers * (1.0 / total)).astype(bf16)
        mixed = matmul(values_t_ref[:, :stop], probs)
        mixed_ref[flipped(start, flip), :] = mixed.T.astype(bf16)


def attend(length, flip, rows, up, keys, values, cos_table, sin_table, score_scale):
    span, head_width = keys.shape
    heads = up.shape[2] // head_width
    whole = lambda array: pl.BlockSpec(array.shape, lambda h: (0, 0))
    head = lambda height: pl.BlockSpec((height, head_width), lambda h: (0, h))
    values_t = values.T
    return pl.pallas_call(
        functools.partial(attend_kernel, score_scale),
        grid=(heads,),
        in_specs=[
            pl.BlockSpec(memory_space=pltpu.SMEM),
            pl.BlockSpec(memory_space=pltpu.SMEM),
            pl.BlockSpec(rows.shape, lambda h: (0, 0, 0)),
            pl.BlockSpec(up.shape[:2] + (head_width,), lambda h: (0, 0, h)),
            whole(keys),
            whole(values_t),
            whole(cos_table),
            whole(sin_table),
        ],
        out_specs=[
            head(span),
            head(span),
            pl.BlockSpec((1, 1, span), lambda h: (h, 0, 0)),
        ],
        out_shape=[
            jax.ShapeDtypeStruct((span, heads * head_width), bf16),
            jax.ShapeDtypeStruct((span, heads * head_width), bf16),
            jax.ShapeDtypeStruct((heads, 1, span), f32),
        ],
        compiler_params=pltpu.CompilerParams(vmem_limit_bytes=62 << 20),
        cost_estimate=BESIDE,
    )(length, flip, rows, up, keys, values_t, cos_table, sin_table)


def attend_back_kernel(
    score_scale,
    length_ref,
    flip_ref,
    queries_ref,
    grad_ref,
    total_ref,
    keys_ref,
    keys_t_ref,
    values_ref,
    cos_ref,
    sin_ref,
    grad_q_ref,
    grad_k_ref,
    grad_v_ref,
):
    length, flip = length_ref[0], flip_ref[0]

    @pl.when(pl.program_id(0) == 0)
    def _():
        grad_k_ref[...] = jnp.zeros_like(grad_k_ref)
        grad_v_ref[...] = jnp.zeros_like(grad_v_ref)

    for start in range(0, queries_ref.shape[0], TILE):
        stop = start + TILE
        queries, grads = queries_ref[start:stop, :], grad_ref[flipped(start, flip), :]
        scores = visible_scores(keys_ref[:stop, :], queries, start, length, score_scale)
        probs = jnp.exp(scores - total_ref[0, :, start:stop])
        grad_probs = outer_cols(values_ref[:stop, :], grads)
        mean = jnp.sum(probs * grad_probs, axis=0, keepdims=True)
        grad_scores = (probs * (grad_probs - mean)).astype(bf16)
        grad_v_ref[:stop, :] += matmul(probs.astype(bf16), grads)
        grad_k_ref[:stop, :] += matmul(grad_scores, queries) * score_scale
        grad_q = matmul(keys_t_ref[:, :stop], grad_scores).T * score_scale
        grad_q = grad_q * cos_ref[start:stop, :] - rotate_half(
            grad_q * sin_ref[start:stop, :]
        )
        grad_q_ref[start:stop, :] = grad_q.astype(bf16)


def attend_back(
    length, flip, queries, grads, total, keys, values, cos_table, sin_table, score_scale
):
    span, head_width = keys.shape
    heads = queries.shape[1] // head_width
    whole = lambda array: pl.BlockSpec(array.shape, lambda h: (0, 0))
    head = pl.BlockSpec((span, head_width), lambda h: (0, h))
    keys_t = keys.T
    summed = jax.ShapeDtypeStruct((span, head_width), f32)
    return pl.pallas_call(
        functools.partial(attend_back_kernel, score_scale),
        grid=(heads,),
        in_specs=[
            pl.BlockSpec(memory_space=pltpu.SMEM),
            pl.BlockSpec(memory_space=pltpu.SMEM),
            head,
            head,
            pl.BlockSpec((1, 1, span), lambda h: (h, 0, 0)),
            whole(keys),
            whole(keys_t),
            whole(values),
            whole(cos_table),
            whole(sin_table),
        ],
        out_specs=[head, whole(keys), whole(keys)],
        out_shape=[jax.ShapeDtypeStruct(queries.shape, bf16), summed, summed],
        compiler_params=pltpu.CompilerParams(vmem_limit_bytes=36 << 20),
        cost_estimate=BESIDE,
    )(length, flip, queries, grads, total, keys, keys_t, values, cos_table, sin_table)


CONTRACT = {"nn": ((1,), (0,)), "nt": ((1,), (1,)), "tn": ((0,), (0,))}


def write_halves(out_refs, block, value):
    rows = value.shape[0] // 2
    for k in range(len(out_refs) // 2):

        @pl.when(block == k)
        def _():
            out_refs[2 * k][...] = value[:rows]
            out_refs[2 * k + 1][...] = value[rows:]


def write_rows(out_refs, value):
    rows = value.shape[0] // len(out_refs)
    for k, out_ref in enumerate(out_refs):
        out_ref[...] = value[k * rows : (k + 1) * rows]


def product_kernel(kind, left_ref, right_ref, *out_refs):
    total = lax.dot_general(
        left_ref[...], right_ref[...], (CONTRACT[kind], ((), ())), preferred_element_type=f32
    )
    write_rows(out_refs, total.astype(bf16))


def product(kind, left, right, pieces=False):
    rows, width = left.shape[0], right.shape[0] if kind == "nt" else right.shape[1]
    chips = lax.axis_size("chip")
    count = 2 * chips if pieces else 1
    if (pieces and chips != 4) or width % TILE or left.shape[1] % 128 or rows % (16 * count):
        total = lax.dot_general(
            left, right, (CONTRACT[kind], ((), ())), preferred_element_type=f32
        ).astype(bf16)
        return as_pieces(total) if pieces else total
    shape = (rows // count, width)
    if kind == "nt":
        source = pl.BlockSpec((TILE, right.shape[1]), lambda i: (i, 0))
    else:
        source = pl.BlockSpec((right.shape[0], TILE), lambda i: (0, i))
    results = pl.pallas_call(
        functools.partial(product_kernel, kind),
        grid=(width // TILE,),
        in_specs=[pl.BlockSpec(left.shape, lambda i: (0, 0)), source],
        out_specs=[pl.BlockSpec((shape[0], TILE), lambda i: (0, i))] * count,
        out_shape=[jax.ShapeDtypeStruct(shape, bf16)] * count,
        compiler_params=pltpu.CompilerParams(vmem_limit_bytes=34 << 20),
        cost_estimate=BESIDE,
    )(left, right)
    return results if pieces else results[0]


def terms_kernel(scale, place_ref, left_ref, right_ref, own_ref, other_ref):
    total = lax.dot_general(
        left_ref[...], right_ref[...], (CONTRACT["tn"], ((), ())), preferred_element_type=f32
    )
    total = (total * scale).astype(bf16).reshape(own_ref.shape)

    @pl.when(pl.program_id(0) == 0)
    def _():
        other_ref[...] = total

    @pl.when(pl.program_id(0) == 1)
    def _():
        own_ref[...] = total


def uneven_kernel(scale, place_ref, left_ref, right_ref, own_ref, other_ref, total_ref):
    total = lax.dot_general(
        left_ref[...], right_ref[...], (CONTRACT["tn"], ((), ())), preferred_element_type=f32
    )
    total_ref[...] = (total * scale).astype(bf16)
    half, core = own_ref.shape[0], place_ref[1]
    own_ref[...] = total_ref[pl.ds(pl.multiple_of(core * half, half), half), :]
    other_ref[...] = total_ref[pl.ds(pl.multiple_of((1 - core) * half, half), half), :]


def weight_terms(left, right, scale, flip=None):
    depth, rows = left.shape
    width = right.shape[1]
    chips, dp = lax.axis_size("chip"), lax.axis_size("dp")
    core = lax.axis_index("core")
    own = rows // (CORES * dp) if flip is None else rows // (chips * CORES * dp)
    half = (dp, chips, own, width) if flip is not None else (dp * own, width)
    tile = dp * own if flip is not None else TILE
    steps = rows // CORES // tile
    whole = lambda array: pl.BlockSpec(array.shape, lambda *_: (0, 0))
    place = jnp.stack([jnp.int32(0) if flip is None else flip, core])
    params = dict(
        out_shape=[jax.ShapeDtypeStruct(half, bf16)] * 2,
        compiler_params=pltpu.CompilerParams(vmem_limit_bytes=34 << 20),
        cost_estimate=BESIDE,
    )
    if tile % 128 == 0 and width % 128 == 0 and rows % (CORES * tile) == 0:
        if flip is not None:
            source = lambda j, k, p: (0, k * CORES + (p[1] ^ 1 ^ j))
            block = (dp, 1, own, width)
            target = lambda k, p: (0, k ^ p[0], 0, 0)
        else:
            source = lambda j, k, p: (0, (p[1] ^ 1 ^ j) * steps + k)
            block = (tile, width)
            target = lambda k, p: (k, 0)
        return pl.pallas_call(
            functools.partial(terms_kernel, scale),
            grid_spec=pltpu.PrefetchScalarGridSpec(
                num_scalar_prefetch=1,
                grid=(CORES, steps),
                in_specs=[pl.BlockSpec((depth, tile), source), whole(right)],
                out_specs=[
                    pl.BlockSpec(block, lambda j, k, p: target(jnp.where(j == 1, k, 0), p)),
                    pl.BlockSpec(
                        block, lambda j, k, p: target(jnp.where(j == 0, k, steps - 1), p)
                    ),
                ],
            ),
            **params,
        )(place, left, right)
    if flip is None and rows % 128 == 0 and width % 512 == 0:
        columns = lambda size: pl.BlockSpec((size, 512), lambda i, p: (0, i))
        return pl.pallas_call(
            functools.partial(uneven_kernel, scale),
            grid_spec=pltpu.PrefetchScalarGridSpec(
                num_scalar_prefetch=1,
                grid=(width // 512,),
                in_specs=[whole(left), columns(depth)],
                out_specs=[columns(rows // CORES)] * 2,
                scratch_shapes=[pltpu.VMEM((rows, 512), bf16)],
            ),
            **params,
        )(place, left, right)
    total = (inner_rows(left, right) * scale).astype(bf16)
    if flip is not None:
        total = total.reshape(chips, CORES, dp, own, width).transpose(1, 2, 0, 3, 4)
    else:
        total = total.reshape((CORES,) + half)
    return take(total, core), take(total, 1 - core)


def as_pieces(terms):
    return jnp.split(terms, 8, 0) if lax.axis_size("chip") == 4 else [terms]


def back_kernel(grad_ref, up_ref, grad_k_ref, grad_v_ref, place_ref, *out_refs):
    grads = outer_cols(grad_ref[...], up_ref[0]).astype(bf16)
    parts = jnp.concatenate([grad_k_ref[...], grad_v_ref[...]], 1).astype(bf16)
    parts = outer_cols(parts, place_ref[0]).astype(bf16)
    write_halves(out_refs, pl.program_id(0), jnp.concatenate([grads, parts], 1))


def back_terms(grad_q, up_q, grad_k, grad_v, place):
    chips, depth, width = up_q.shape
    span = grad_q.shape[0]
    if chips != 4:
        grads = jnp.einsum("tn,kin->kti", grad_q, up_q, preferred_element_type=f32)
        parts = jnp.concatenate([grad_k, grad_v], 1).astype(bf16)
        parts = jnp.einsum("sn,kcn->ksc", parts, place, preferred_element_type=f32)
        terms = jnp.concatenate([grads, parts], 2).astype(bf16)
        return [terms.reshape(chips * span, -1)]
    whole = lambda array: pl.BlockSpec(array.shape, lambda k: (0, 0))
    block = lambda array: pl.BlockSpec((1,) + array.shape[1:], lambda k: (k, 0, 0))
    shape = (span // 2, depth + place.shape[1])
    return pl.pallas_call(
        back_kernel,
        grid=(chips,),
        in_specs=[whole(grad_q), block(up_q), whole(grad_k), whole(grad_v), block(place)],
        out_specs=[pl.BlockSpec(shape, lambda k: (0, 0))] * (2 * chips),
        out_shape=[jax.ShapeDtypeStruct(shape, bf16)] * (2 * chips),
        compiler_params=pltpu.CompilerParams(vmem_limit_bytes=36 << 20),
        cost_estimate=BESIDE,
    )(grad_q, up_q, grad_k, grad_v, place)


def spread_kernel(count, _, *refs):
    left_refs, weight_ref, out_refs = refs[:count], refs[count], refs[count + 1 :]
    _, groups, _, own, width = weight_ref.shape
    total = 0.0
    for j, left_ref in enumerate(left_refs):
        block = weight_ref[0, :, j].reshape(groups * own, width)
        total = total + outer_cols(left_ref[...], block)
    write_rows(out_refs, total.astype(bf16))


def spread(lefts, weight):
    chips, groups, _, own, width = weight.shape
    rows, depth = lefts[0].shape[0], groups * own
    if chips != 4 or width % 128:
        total = sum(
            outer_cols(left, weight[:, :, j].reshape(chips * depth, width))
            for j, left in enumerate(lefts)
        )
        return as_pieces(total.astype(bf16))
    shape = (rows // (2 * chips), chips * depth)
    return pl.pallas_call(
        functools.partial(spread_kernel, len(lefts)),
        grid_spec=pltpu.PrefetchScalarGridSpec(
            num_scalar_prefetch=1,
            grid=(chips,),
            in_specs=[pl.BlockSpec(left.shape, lambda i, f: (0, 0)) for left in lefts]
            + [pl.BlockSpec((1,) + weight.shape[1:], lambda i, f: (i ^ f[0], 0, 0, 0, 0))],
            out_specs=[pl.BlockSpec((shape[0], depth), lambda i, f: (0, i))] * (2 * chips),
        ),
        out_shape=[jax.ShapeDtypeStruct(shape, bf16)] * (2 * chips),
        compiler_params=pltpu.CompilerParams(vmem_limit_bytes=34 << 20),
        cost_estimate=BESIDE,
    )(chip_flip()[None], *lefts, weight)


def whole_kernel(own, place_ref, *refs):
    *left_refs, mine_ref, other_ref, out_ref = refs
    chips = len(left_refs)
    groups, width = mine_ref.shape[2], mine_ref.shape[4]
    half = chips // CORES
    total = 0.0
    for k in range(chips):
        block = pl.program_id(0) ^ k ^ place_ref[0]
        mine = mine_ref[k, block % half, :, :own].reshape(groups * own, width)
        other = other_ref[k, block % half, :, :own].reshape(groups * own, width)
        weight = jnp.where(block // half == place_ref[1], mine, other)
        total = total + outer_cols(left_refs[k][...], weight)
    out_ref[...] = total


def whole_products(lefts, mine, other, weights, own):
    chips = len(lefts)
    rows = lefts[0].shape[0]
    if chips != 4:
        every = lax.all_gather(weights[:, :, :own], "chip", axis=0)
        return sum(
            outer_cols(lefts[k], every[k].reshape(-1, every.shape[-1])) for k in range(chips)
        )
    depth = mine.shape[2] * own
    whole = lambda array: pl.BlockSpec(array.shape, lambda i, p: (0,) * array.ndim)
    return pl.pallas_call(
        functools.partial(whole_kernel, own),
        grid_spec=pltpu.PrefetchScalarGridSpec(
            num_scalar_prefetch=1,
            grid=(chips,),
            in_specs=[whole(left) for left in lefts] + [whole(mine), whole(other)],
            out_specs=pl.BlockSpec((rows, depth), lambda i, p: (0, i)),
        ),
        out_shape=jax.ShapeDtypeStruct((rows, chips * depth), f32),
        compiler_params=pltpu.CompilerParams(vmem_limit_bytes=36 << 20),
        cost_estimate=BESIDE,
    )(jnp.stack([chip_flip(), lax.axis_index("core")]), *lefts, mine, other)


def split_kernel(_, small_ref, qup_ref, gate_ref, up_ref, *out_refs):
    chips = len(out_refs) // 3
    own = gate_ref.shape[0]
    for k in range(chips):

        @pl.when(pl.program_id(0) == k)
        def _():
            out_refs[k][...] = small_ref[0]
            out_refs[chips + k][...] = qup_ref[...]
            out_refs[2 * chips + k][:own, :] = gate_ref[...]
            out_refs[2 * chips + k][own:, :] = up_ref[...]


def split_columns(small, w_qup, w_gate, w_up):
    chips = lax.axis_size("chip")
    own, width = w_gate.shape
    width = width // chips
    if chips != 4 or width % 128:
        gate_up = jnp.concatenate([by_columns(w_gate), by_columns(w_up)], 1)
        return list(small), list(by_columns(w_qup)), list(gate_up)
    own_q, q_width = w_qup.shape[0], w_qup.shape[1] // chips
    shapes = [small.shape[1:], (own_q, q_width), (2 * own, width)]
    columns = lambda rows, size: pl.BlockSpec((rows, size), lambda k, f: (0, k ^ f[0]))
    outs = pl.pallas_call(
        split_kernel,
        grid_spec=pltpu.PrefetchScalarGridSpec(
            num_scalar_prefetch=1,
            grid=(chips,),
            in_specs=[
                pl.BlockSpec((1,) + small.shape[1:], lambda k, f: (k ^ f[0], 0, 0)),
                columns(own_q, q_width),
                columns(own, width),
                columns(own, width),
            ],
            out_specs=[
                pl.BlockSpec(shape, lambda k, f: (0, 0)) for shape in shapes for _ in range(chips)
            ],
        ),
        out_shape=[jax.ShapeDtypeStruct(shape, bf16) for shape in shapes for _ in range(chips)],
        cost_estimate=BESIDE,
    )(chip_flip()[None], small, w_qup, w_gate, w_up)
    return outs[:chips], outs[chips : 2 * chips], outs[2 * chips :]


def normed_kernel(flip_ref, *refs):
    *piece_refs, gain_ref, small_ref, normed_ref, query_ref, pair_ref = refs
    per_step = len(piece_refs) // pl.num_programs(0)
    for k in range(pl.num_programs(0)):

        @pl.when(pl.program_id(0) == k)
        def _():
            pieces = [ref[...] for ref in piece_refs[k * per_step : (k + 1) * per_step]]
            rows = jnp.concatenate(pieces, 0).astype(f32)
            normed = (rows * rms_scale(rows) * gain_ref[...]).astype(bf16)
            normed_ref[...] = normed
            chips, groups, _, width = small_ref.shape
            depth = normed.shape[1] // chips
            own = depth // groups
            raw = 0.0
            for place in range(chips):
                weight = small_ref[place ^ flip_ref[0], :, :own].reshape(depth, width)
                columns = normed[:, place * depth : (place + 1) * depth]
                raw = raw + matmul(columns, weight)
            split = query_ref.shape[1]
            query_ref[...], pair_ref[...] = raw[:, :split], raw[:, split:]


def normed_rows(pieces, gain, small, own, split):
    chips = lax.axis_size("chip")
    if chips != 4:
        rows = pieces[0].astype(f32)
        normed = (rows * rms_scale(rows) * gain).astype(bf16)
        small = small[:, :, :own].reshape(normed.shape[1], -1)
        raw = matmul(normed, small)
        return normed, raw[:, :split], raw[:, split:]
    half, width = pieces[0].shape
    whole = lambda array: pl.BlockSpec(array.shape, lambda k, f: (0,) * array.ndim)
    block = lambda size: pl.BlockSpec((2 * half, size), lambda k, f: (k ^ f[0], 0))
    gain = gain[None, :]
    rows = chips * 2 * half
    return pl.pallas_call(
        normed_kernel,
        grid_spec=pltpu.PrefetchScalarGridSpec(
            num_scalar_prefetch=1,
            grid=(chips,),
            in_specs=[whole(piece) for piece in pieces] + [whole(gain), whole(small)],
            out_specs=[block(width), block(split), block(small.shape[-1] - split)],
        ),
        out_shape=[
            jax.ShapeDtypeStruct((rows, width), bf16),
            jax.ShapeDtypeStruct((rows, split), f32),
            jax.ShapeDtypeStruct((rows, small.shape[-1] - split), f32),
        ],
        compiler_params=pltpu.CompilerParams(vmem_limit_bytes=62 << 20),
        cost_estimate=BESIDE,
    )(chip_flip()[None], *pieces, gain, small)


def gate_terms(gate, up):
    sigma = jax.nn.sigmoid(gate)
    silu = gate * sigma
    return (
        (silu * up).astype(bf16),
        silu.astype(bf16),
        (up * sigma * (1.0 + gate * (1.0 - sigma))).astype(bf16),
    )


def gate_kernel(flip_ref, rows_ref, weight_ref, active_ref, silu_ref, slope_ref):
    chips, groups, _, own, width = weight_ref.shape
    depth = groups * own
    both = 0.0
    for place in range(chips):
        block = weight_ref[place ^ flip_ref[0]]
        block = jnp.concatenate([block[:, j].reshape(depth, width) for j in range(2)], 1)
        both = both + matmul(rows_ref[:, place * depth : (place + 1) * depth], block)
    active_ref[...], silu_ref[...], slope_ref[...] = gate_terms(both[:, :width], both[:, width:])


def gated(rows, gate_up):
    chips, groups, _, own, width = gate_up.shape
    if width % 128:
        gate, up = [gate_up[:, :, j].reshape(rows.shape[1], width) for j in range(2)]
        return gate_terms(matmul(rows, gate), matmul(rows, up))
    out = pl.BlockSpec((rows.shape[0], 128), lambda i, f: (0, i))
    return pl.pallas_call(
        gate_kernel,
        grid_spec=pltpu.PrefetchScalarGridSpec(
            num_scalar_prefetch=1,
            grid=(width // 128,),
            in_specs=[
                pl.BlockSpec(rows.shape, lambda i, f: (0, 0)),
                pl.BlockSpec((chips, groups, 2, own, 128), lambda i, f: (0, 0, 0, 0, i)),
            ],
            out_specs=[out] * 3,
        ),
        out_shape=[jax.ShapeDtypeStruct((rows.shape[0], width), bf16)] * 3,
        compiler_params=pltpu.CompilerParams(vmem_limit_bytes=36 << 20),
        cost_estimate=BESIDE,
    )(chip_flip()[None], rows, gate_up)


def gate_back_kernel(seed_ref, down_ref, silu_ref, slope_ref, gate_ref, up_ref):
    grads = outer_cols(seed_ref[...], down_ref[...])
    gate_ref[...] = (grads * slope_ref[...].astype(f32)).astype(bf16)
    up_ref[...] = (grads * silu_ref[...].astype(f32)).astype(bf16)


def gated_back(seed, down_proj, silu, slope):
    width, depth = down_proj.shape
    if width % 128:
        grads = outer_cols(seed, down_proj)
        return (grads * slope.astype(f32)).astype(bf16), (grads * silu.astype(f32)).astype(bf16)
    rows = lambda size: pl.BlockSpec((TILE, size), lambda i: (i, 0))
    return pl.pallas_call(
        gate_back_kernel,
        grid=(seed.shape[0] // TILE,),
        in_specs=[
            rows(depth),
            pl.BlockSpec(down_proj.shape, lambda i: (0, 0)),
            rows(width),
            rows(width),
        ],
        out_specs=[rows(width)] * 2,
        out_shape=[jax.ShapeDtypeStruct(silu.shape, bf16)] * 2,
        compiler_params=pltpu.CompilerParams(vmem_limit_bytes=36 << 20),
        cost_estimate=BESIDE,
    )(seed, down_proj, silu, slope)


def per_device(
    tokens,
    lengths,
    attn_gain,
    w_qdown,
    q_gain,
    w_qup,
    w_key,
    w_value,
    w_out,
    ffn_gain,
    w_gate,
    w_up,
    w_down,
    cotangent,
):
    slot_count, seq_span, width = tokens.shape[1:]
    assert slot_count == CORES
    chips, dp = lax.axis_size("chip"), lax.axis_size("dp")
    chip, core = lax.axis_index("chip"), lax.axis_index("core")
    devices = chips * CORES * dp
    row_count = CORES * seq_span
    span = chips * row_count
    head_width = w_key.shape[1]
    q_width = w_qdown.shape[1]
    down_shape = w_down.shape
    score_scale = 1.0 / math.sqrt(head_width)
    grad_scale = 1.0 / math.sqrt(slot_count * seq_span * devices)

    half = head_width // 2
    own_rows, own_q = attn_gain.shape[0], q_gain.shape[0]
    q_cols, v_cols, k_cols = q_width // chips, head_width // chips, half // chips
    small_cols = q_cols + 2 * v_cols
    length = lengths[0, core]
    positions = chip * row_count + jnp.arange(row_count, dtype=jnp.int32)
    valid_mask = (positions < length).astype(f32)[:, None]
    tokens_own = pair_in(tokens[0])
    inputs = tokens_own.astype(f32)
    flip = chip_flip()[None]

    key_pairs = w_key.reshape(own_rows, 2, chips, k_cols).transpose(2, 0, 1, 3)
    small = jnp.concatenate(
        [
            by_columns(w_qdown),
            key_pairs.reshape(chips, own_rows, 2 * k_cols),
            by_columns(w_value),
        ],
        2,
    )
    gains = [jnp.pad(gain, (0, small_cols - gain.shape[0])) for gain in (attn_gain, ffn_gain, q_gain)]
    gains = jnp.pad(jnp.stack(gains), ((0, 13), (0, 0)))
    small = jnp.concatenate([small, jnp.broadcast_to(gains, (chips,) + gains.shape)], 1)
    small, up_q, gate_up = split_columns(small, w_qup, w_gate, w_up)
    tokens_own, small = tie(tokens_own, small)
    tokens_near = gather_near(tokens_own)
    cos_all, sin_all = rotary(jnp.arange(span, dtype=jnp.int32), head_width)
    cos_own = lax.dynamic_slice_in_dim(cos_all, chip * k_cols, k_cols, 1)
    sin_own = lax.dynamic_slice_in_dim(sin_all, chip * k_cols, k_cols, 1)
    out_proj, small, tokens_near, tables = tie(
        gather_rows(w_out), exchange(small), tokens_near, (cos_all, sin_all, cos_own, sin_own)
    )
    cos_all, sin_all, cos_own, sin_own = tables
    small = gather_blocks(small)
    tokens_pieces, up_q, gate_up = tie(far_pieces(tokens_near), up_q, gate_up)
    up_q = gather_columns(up_q)
    small, cotangent = tie(small, cotangent)
    seed_grad = (pair_in(cotangent[0]).astype(f32) * valid_mask).astype(bf16)
    gains = small[:, :, own_rows : own_rows + 3].astype(f32)
    gains = jnp.stack(reordered(list(gains), flip[0]))
    gain_one = gains[:, :, 0, :own_rows].reshape(-1)
    gain_two = gains[:, :, 1, :own_rows].reshape(-1)
    gain_q = gains[:, :, 2, :own_q].reshape(chips, -1)[chip]
    up_q = up_q.reshape(chips, q_cols, -1)

    normed_all, q_down, kv_raw = normed_rows(
        tokens_pieces, gain_one, small, own_rows, q_cols
    )
    q_down, kv_raw, gate_up = tie(q_down, kv_raw, exchange(gate_up))
    scale_q = lax.rsqrt(row_sums(q_down * q_down) / q_width + epsilon)
    gate_up = gather_blocks(gate_up)
    down_proj = gather_rows(w_down)
    gate_up = gate_up.reshape(chips, CORES * dp, 2, own_rows, -1)
    q_normed = (q_down * scale_q * gain_q).astype(bf16)
    k_one, k_two = kv_raw[:, :k_cols], kv_raw[:, k_cols:v_cols]
    key_cols = [k_one * cos_own - k_two * sin_own, k_two * cos_own + k_one * sin_own]
    shared = jnp.concatenate(key_cols + [kv_raw[:, v_cols:]], 1).astype(bf16)
    shared = gather_chips(jnp.concatenate([q_normed, shared], 1))
    shared, seed_tied = tie(shared, seed_grad)
    seed_near = gather_near(seed_tied)
    shared = shared.reshape(chips, span, small_cols)
    local, sender = jnp.arange(2 * v_cols), (jnp.arange(chips) ^ flip[0])[:, None]
    target = jnp.where(
        local < v_cols,
        local // k_cols * half + sender * k_cols + local % k_cols,
        head_width + sender * v_cols + local - v_cols,
    )
    place = (target[:, :, None] == jnp.arange(2 * head_width)).astype(bf16)
    key_values = jnp.einsum(
        "ksc,kcn->sn", shared[:, :, q_cols:], place, preferred_element_type=f32
    ).astype(bf16)
    keys, values = key_values[:, :head_width], key_values[:, head_width:]

    queries, mixed, log_total = attend(
        length[None], flip, shared, up_q, keys, values, cos_all, sin_all, score_scale
    )
    part, *seed_near = tie(product("nn", mixed, out_proj, pieces=True), *seed_near)
    middle = inputs + scatter_chips(part)
    scale_two = rms_scale(middle)
    normed2 = gather_chips((middle * scale_two * gain_two).astype(bf16))

    small_rows = small.reshape(CORES, -1, small_cols)
    small_rows = take(small_rows, core) if chips == 4 else small_rows[0]
    normed2, seed_near = tie(normed2, seed_near)
    activated, silu, slope = gated(normed2, gate_up)
    activated, seed_pieces = tie(activated, far_pieces(seed_near))
    seed_all = join_rows(seed_pieces)
    down_terms = weight_terms(activated, seed_all, grad_scale)
    down_terms, down_proj = tie(down_terms, down_proj)
    down_half = sum_cores(*down_terms)
    gate_grad, up_grad = gated_back(seed_all, down_proj, silu, slope)
    gate_grad, up_grad, down_half, small_rows = tie(gate_grad, up_grad, down_half, small_rows)
    small_near = gather_near(small_rows) if chips == 4 else (small_rows,)
    grad_w_down = scatter_dp(down_half)
    part, gate_grad, up_grad = tie(
        spread([gate_grad, up_grad], gate_up), gate_grad, up_grad
    )
    gate_part = weight_terms(normed2, gate_grad, grad_scale, flip[0])
    up_part = weight_terms(normed2, up_grad, grad_scale, flip[0])
    part, small_near = tie(part, small_near)
    near, gate_part, up_part = tie(scatter_near(part), gate_part, up_part)
    near, gate_half = tie(near, sum_cores(*gate_part))
    grad_w_gate = scatter_dp(gate_half)
    grad_normed2, up_half = scatter_far(near), sum_cores(*up_part)
    grad_normed2, grad_w_down, up_half = tie(grad_normed2, grad_w_down, up_half)
    grad_w_up = scatter_dp(up_half)
    grad_middle = seed_grad.astype(f32) + norm_back(grad_normed2, middle, scale_two, gain_two)
    grad_branch, activated = tie(grad_middle.astype(bf16), activated)
    q_rows = shared[:, :, :q_cols].transpose(1, 0, 2).reshape(span, q_width)
    grad_branch, out_part, q_rows = tie(
        gather_chips(grad_branch), product("nn", activated, down_proj, pieces=True), q_rows
    )
    out_near = scatter_near(out_part)
    out_terms = weight_terms(mixed, grad_branch, grad_scale)
    out_terms, grad_branch, grad_w_gate = tie(out_terms, grad_branch, grad_w_gate)
    grad_mixed, out_half, small_near = tie(
        product("nt", grad_branch, out_proj), sum_cores(*out_terms), small_near
    )
    small_pieces = far_pieces(small_near) if chips == 4 else list(small_near)
    grad_w_out = scatter_dp(out_half)
    grad_q, grad_k, grad_v = attend_back(
        length[None], flip, queries, grad_mixed, log_total, keys, values, cos_all, sin_all, score_scale
    )
    grad_q, out_near, small_pieces = tie(grad_q, out_near, small_pieces)
    output = middle + scatter_far(out_near)
    back, grad_q = tie(back_terms(grad_q, up_q, grad_k, grad_v, place), grad_q)
    qup_part = weight_terms(q_rows, grad_q, grad_scale, jnp.int32(0))
    back, qup_part, grad_w_up, output, small_pieces = scatter_chips(
        back, (qup_part, grad_w_up, output, small_pieces)
    )
    back, qup_half, grad_w_out = tie(back, sum_cores(*qup_part), grad_w_out)
    grad_w_qup = scatter_dp(qup_half)
    weighted = back[:, :q_cols] * gain_q
    mean = row_sums(weighted * q_down) / q_width
    pair = jnp.concatenate([grad_w_gate, grad_w_up], 2)
    mean, pair = tie(mean, pair)
    pair = trade_blocks(pair)
    grad_q_down = scale_q * weighted - q_down * scale_q**3 * mean
    k_one, k_two = back[:, q_cols : q_cols + k_cols], back[:, q_cols + k_cols : q_cols + 2 * k_cols]
    back = jnp.concatenate(
        [
            grad_q_down,
            k_one * cos_own + k_two * sin_own,
            k_two * cos_own - k_one * sin_own,
            back[:, q_cols + v_cols :],
        ],
        1,
    ).astype(bf16)
    small_mine = join_rows(small_pieces)
    small_other = swap_cores(small_mine)
    back_parts = exchange(reordered(jnp.split(back, chips, 0), flip[0]))
    small_part = weight_terms(normed_all, back, grad_scale, flip[0])
    back_parts, small_part, small_pair = tie(back_parts, small_part, (small_mine, small_other))
    small_half = sum_cores(*small_part)
    grad_small = scatter_dp(small_half)
    if chips == 4:
        shape = (chips, -1, CORES * dp, small.shape[2], small_cols)
        small_pair = [array.reshape(shape) for array in small_pair]
    grad_normed = whole_products(back_parts, *small_pair, small, own_rows)
    grad_normed, grad_w_qup = tie(grad_normed, grad_w_qup)
    grad_w_qup, pair = tie(trade_blocks(grad_w_qup), pair)
    out_tokens = pair_out(output.astype(bf16))[None]
    grad_inputs = grad_middle + norm_back(grad_normed, inputs, rms_scale(inputs), gain_one)
    grad_tokens = pair_out(grad_inputs)[None]
    grad_w_qup = join_columns(grad_w_qup)
    parts = jnp.stack(reordered(trade_blocks(grad_small), flip[0]), 1).astype(f32)
    grad_w_key = parts[:, :, q_cols : q_cols + v_cols].reshape(own_rows, chips, 2, k_cols)
    grad_w_key = grad_w_key.transpose(0, 2, 1, 3).reshape(own_rows, head_width)
    pairs = [jnp.split(block, 2, 1) for block in pair]
    grad_w_gate, grad_w_up = [join_columns([pair[j] for pair in pairs]) for j in range(2)]
    grad_w_qdown = parts[:, :, :q_cols].reshape(own_rows, q_width)
    grad_w_value = parts[:, :, q_cols + v_cols :].reshape(own_rows, head_width)
    overlap = lambda weight, grad: jnp.sum(weight.astype(f32) * grad, axis=1)
    attn_terms = overlap(w_qdown, grad_w_qdown) + overlap(w_key, grad_w_key)
    attn_terms = attn_terms + overlap(w_value, grad_w_value)
    ffn_terms = overlap(w_gate, grad_w_gate) + overlap(w_up, grad_w_up)
    return (
        out_tokens,
        grad_tokens,
        attn_terms / attn_gain.astype(f32),
        grad_w_qdown,
        overlap(w_qup, grad_w_qup) / q_gain.astype(f32),
        grad_w_qup,
        grad_w_key,
        grad_w_value,
        grad_w_out.astype(f32).reshape(w_out.shape),
        ffn_terms / ffn_gain.astype(f32),
        grad_w_gate,
        grad_w_up,
        grad_w_down.astype(f32).reshape(down_shape),
    )


def solution(mesh):
    seq, dp = mesh.shape["seq"], mesh.shape["dp"]
    chips = Mesh(
        np.asarray(mesh.devices).reshape(seq // CORES, CORES, dp), ("chip", "core", "dp")
    )
    every = ("chip", "core", "dp")
    rows, vector = P(every, None), P(every)
    block = P("dp", None, ("chip", "core"), None)
    weights = (vector, rows, vector, rows, rows, rows, rows, vector, rows, rows, rows)
    return jax.shard_map(
        per_device,
        mesh=chips,
        in_specs=(block, P("dp", None)) + weights + (block,),
        out_specs=(block, block) + weights,
        check_vma=False,
    )
```
